256 devices in a mesh: depth: 16 (over z_hi, x, core), rows: 16 (over y, z_lo).
Axes of the slice: x: 4, y: 4, z: 8 (z_hi: 2, z_lo: 4; z = z_hi * 4 + z_lo), core: 2. Of those that a mesh axis runs over, the one named last changes fastest.
Arguments:
- volume: bfloat16 [32, 64, 128, 128], P('depth', 'rows'), may hold values from -6 to 6
- fine_filters: bfloat16 [3, 3, 3, 128, 128], replicated, may hold values from -0.109375 to 0.109375
- fine_bias: float32 [128], replicated, may hold values from -0.5 to 0.5
- coarse_filters: bfloat16 [3, 3, 3, 128, 256], P(None, None, None, None, 'rows'), may hold values from -0.109375 to 0.109375
- coarse_bias: float32 [256], P('rows'), may hold values from -0.5 to 0.5
Outputs:
- encoded: bfloat16 [256, 16, 2048], P('rows', 'depth')
The draws below stay inside these ranges and needn't reach their ends.
All inputs are finite; a program needn't handle non-finite values.
Results may differ from the reference program's by a relative error of at most 0.0049.
Values may be sent and summed in bfloat16 or wider, within the bound.
No kernel may reach another device: no remote copies, remote signals or barrier semaphores. Data moves between devices by JAX's collectives and lax.ppermute only.
A program may use at most 64 MiB of HBM per device.

```python
import jax
import jax.numpy as jnp
from jax import lax

C3 = 128
C4 = 256
W = 128
ND = 32
NH = 64
PD = 16
PH = 32
PW = 64


def steps_of(own_key, extent, cuts, least, largest):
    factor_of = 1.0
    for dim, blocks in cuts:
        steps = jax.random.uniform(jax.random.fold_in(jax.random.fold_in(own_key, 6), dim), (blocks,), jnp.float32, least / len(cuts), largest / len(cuts))
        factor_of = factor_of * jnp.repeat(jnp.exp(steps), extent[dim] // blocks).reshape((-1,) + (1,) * (len(extent) - 1 - dim))
    return factor_of


def normal_values(key, shape, scale, reach, pieces=(), kind=jnp.bfloat16):
    array = jax.random.normal(key, shape, jnp.float32) * scale
    if len(pieces) > 0:
        array = steps_of(key, shape, pieces, -0.22, 0.18) * array
    return jnp.clip(array, min=-reach, max=reach).astype(kind)


def setup_inputs(seed: int = 0) -> dict:
    splits = jax.random.split(jax.random.key(seed), 6)
    return {
        "volume": normal_values(splits[0], (ND, NH, W, C3), 1.0, 6.0, ((0, 16), (1, 16))),
        "fine_filters": normal_values(splits[1], (3, 3, 3, C3, C3), (27 * C3) ** -0.5, 0.109375),
        "fine_bias": jnp.clip(jax.random.uniform(splits[2], (C3,), jnp.float32, -0.5, 0.5), -0.5, 0.5),
        "coarse_filters": normal_values(splits[3], (3, 3, 3, C3, C4), (27 * C3) ** -0.5, 0.109375, ((4, 16),)),
        "coarse_bias": jnp.clip(jax.random.uniform(splits[4], (C4,), jnp.float32, -0.5, 0.5) * steps_of(splits[4], (C4,), ((0, 16),), -0.4, 0.0), -0.5, 0.5),
    }


def reference(volume, fine_filters, fine_bias, coarse_filters, coarse_bias):
    padded = jnp.pad(volume, ((1, 1), (1, 1), (1, 1), (0, 0)))
    kernel_fine = fine_filters.astype(jnp.float32)

    def level_fine(block):
        start = (block * 2).astype(jnp.int32)
        piece = lax.dynamic_slice_in_dim(padded, start, 4, 0).astype(jnp.float32)
        summed = lax.conv_general_dilated(piece[None], kernel_fine, (1, 1, 1), "VALID", dimension_numbers=("NDHWC", "DHWIO", "NDHWC"), precision=lax.Precision.HIGHEST)[0]
        active = jnp.maximum(summed + fine_bias, 0.0).astype(jnp.bfloat16)
        return active.reshape(1, 2, NH // 2, 2, W // 2, 2, C3).max(axis=(1, 3, 5))[0]

    pooled = lax.map(level_fine, jnp.arange(ND // 2, dtype=jnp.int32))
    coarse_in = jnp.pad(pooled, ((1, 1), (1, 1), (1, 1), (0, 0))).astype(jnp.float32)
    summed = lax.conv_general_dilated(coarse_in[None], coarse_filters.astype(jnp.float32), (1, 1, 1), "VALID", dimension_numbers=("NDHWC", "DHWIO", "NDHWC"), precision=lax.Precision.HIGHEST)[0]
    active = jnp.maximum(summed + coarse_bias, 0.0).astype(jnp.bfloat16)
    return jnp.transpose(active, (3, 0, 1, 2)).reshape(C4, PD, PH * PW)
```

```python
import jax
import jax.numpy as jnp
from jax import lax
from jax.experimental import pallas as pl
from jax.experimental.pallas import tpu as pltpu
from jax.sharding import PartitionSpec as P

BF16 = jnp.bfloat16
F32 = jnp.float32


def near_pairs(count):
    return [(i, i ^ 1) for i in range(count)]


def far_pairs(count):
    return [(i, ((i - 1) ^ 1) + 1) for i in range(1, count - 1)]


def fine_kernel(odd, vol, x1, x2, r1, r2, c1, c2, w, bias, out, cells, peak):
    pd = odd[0]
    pr = odd[1]
    for j in range(4):
        for i in range(6):
            row = (i - 1) + pr * (5 - 2 * i)
            if j in (1, 2):
                plane = (j - 1) + pd * (3 - 2 * j)
                piece = r2[plane] if i == 0 else r1[plane] if i == 5 else vol[plane, row]
            else:
                side, slot = (x2, 1) if j == 0 else (x1, 0)
                piece = c2[slot] if i == 0 else c1[slot] if i == 5 else side[row]
            cells[j, i] = piece
    taps = [(a, b) for a in range(3) for b in range(3)]
    groups = [taps[i : i + 2] for i in range(0, 9, 2)]
    parts = []
    for s in range(2):
        total = None
        for group in groups:
            lhs = jnp.concatenate(
                [cells[s + a, b : b + 4].reshape(512, 128) for a, b in group], axis=1
            )
            rhs = jnp.concatenate(
                [
                    jnp.concatenate(
                        [w[a + pd * (2 - 2 * a), b + pr * (2 - 2 * b), c] for c in range(3)], axis=1
                    )
                    for a, b in group
                ],
                axis=0,
            )
            term = jnp.dot(lhs, rhs, preferred_element_type=F32)
            total = term if total is None else total + term
        parts.append(total)
    col = lax.broadcasted_iota(jnp.int32, (128, 128), 0)
    for q in range(2):
        best = None
        for s in range(2):
            for t in range(2):
                line = parts[s][(2 * q + t) * 128 : (2 * q + t + 1) * 128]
                left = jnp.where(col == 0, 0.0, pltpu.roll(line[:, :128], 1, 0))
                right = jnp.where(col == 127, 0.0, pltpu.roll(line[:, 256:], 127, 0))
                value = line[:, 128:256] + left + right
                best = value if best is None else jnp.maximum(best, value)
        peak[...] = best
        pooled = jnp.maximum(peak[pl.ds(0, 64, stride=2), :], peak[pl.ds(1, 64, stride=2), :])
        out[q + pr * (1 - 2 * q)] = jnp.maximum(pooled + bias[...], 0.0).astype(BF16)


def fine_level(odd, vol, x1, x2, r1, r2, c1, c2, w, bias):
    vmem = pl.BlockSpec(memory_space=pltpu.VMEM)
    return pl.pallas_call(
        fine_kernel,
        out_shape=jax.ShapeDtypeStruct((2, 64, 128), BF16),
        in_specs=[pl.BlockSpec(memory_space=pltpu.SMEM)] + [vmem] * 9,
        out_specs=vmem,
        scratch_shapes=[pltpu.VMEM((4, 6, 128, 128), BF16), pltpu.VMEM((128, 128), F32)],
        compiler_params=pltpu.CompilerParams(vmem_limit_bytes=32 * 1024 * 1024),
    )(odd, vol, x1, x2, r1, r2, c1, c2, w, bias)


def coarse_kernel(place, g0, g1, g2, g3, w, out, cells):
    y = place[0]
    z = place[1]
    cells[0] = jnp.zeros((64, 128), BF16)
    cells[33] = jnp.zeros((64, 128), BF16)
    for m, block in enumerate((g0, g1, g2, g3)):
        for k in range(4):
            row = lax.rem(y - m + 4, 4) * 8 + lax.rem(z - k + 4, 4) * 2
            cells[pl.ds(row + 1, 2)] = block[k]
    lines = 8
    size = lines * 64
    lane = lax.rem(lax.broadcasted_iota(jnp.int32, (48, size), 1), 64)
    for t in range(32 // lines):
        rhs = jnp.concatenate(
            [cells[t * lines + b : t * lines + b + lines].reshape(size, 128) for b in range(3)], axis=1
        )
        term = lax.dot_general(w[...], rhs, (((1,), (1,)), ((), ())), preferred_element_type=F32)
        left = jnp.where(lane == 0, 0.0, pltpu.roll(term[:48], 1, 1))
        right = jnp.where(lane == 63, 0.0, pltpu.roll(term[96:], size - 1, 1))
        value = term[48:96] + left + right
        for n in range(3):
            out[n, :, t * size : (t + 1) * size] = value[16 * n : 16 * n + 16]


def coarse_level(place, g0, g1, g2, g3, w):
    vmem = pl.BlockSpec(memory_space=pltpu.VMEM)
    return pl.pallas_call(
        coarse_kernel,
        out_shape=jax.ShapeDtypeStruct((3, 16, 2048), F32),
        in_specs=[pl.BlockSpec(memory_space=pltpu.SMEM)] + [vmem] * 5,
        out_specs=vmem,
        scratch_shapes=[pltpu.VMEM((34, 64, 128), BF16)],
        compiler_params=pltpu.CompilerParams(vmem_limit_bytes=32 * 1024 * 1024),
    )(place, g0, g1, g2, g3, w)


def body(volume, fine_filters, fine_bias, coarse_filters, coarse_bias):
    d = lax.axis_index("depth")
    r = lax.axis_index("rows")
    pd = lax.rem(d, 2)
    pr = lax.rem(r, 2)
    depth_near, depth_far = near_pairs(16), far_pairs(16)
    rows_near, rows_far = near_pairs(16), far_pairs(16)

    x2 = lax.ppermute(lax.dynamic_index_in_dim(volume, pd, 0, False), "depth", depth_far)
    x1 = lax.ppermute(lax.dynamic_index_in_dim(volume, 1 - pd, 0, False), "depth", depth_near)
    r2 = lax.ppermute(lax.dynamic_index_in_dim(volume, 3 * pr, 1, False), "rows", rows_far)
    r1 = lax.ppermute(lax.dynamic_index_in_dim(volume, 3 - 3 * pr, 1, False), "rows", rows_near)
    sides = jnp.stack([x1, x2])
    c2 = lax.ppermute(lax.dynamic_index_in_dim(sides, 3 * pr, 1, False), "rows", rows_far)
    c1 = lax.ppermute(lax.dynamic_index_in_dim(sides, 3 - 3 * pr, 1, False), "rows", rows_near)
    odd = jnp.stack([pd, pr]).astype(jnp.int32)
    pooled = fine_level(odd, volume, x1, x2, r1, r2, c1, c2, fine_filters, fine_bias.reshape(1, 128))

    def along_z(k):
        return [(y * 4 + z, y * 4 + (z + k) % 4) for y in range(4) for z in range(4)]

    def along_y(k):
        return [(y * 4 + z, (y + k) % 4 * 4 + z) for y in range(4) for z in range(4)]

    zs = {k: lax.ppermute(pooled, "rows", along_z(k)) for k in (2, 1, 3)}
    g0 = jnp.stack([pooled, zs[1], zs[2], zs[3]])
    gs = {k: lax.ppermute(g0, "rows", along_y(k)) for k in (2, 1, 3)}

    up, own, down = coarse_filters[0], coarse_filters[1], coarse_filters[2]
    near = jnp.where(pd == 0, up, down)
    far = jnp.where(pd == 0, down, up)
    w = jnp.stack([near, far, own])
    w = jnp.transpose(w, (2, 0, 4, 1, 3)).reshape(144, 384)
    place = jnp.stack([r // 4, lax.rem(r, 4)]).astype(jnp.int32)
    sums = coarse_level(place, g0, gs[1], gs[2], gs[3], w)
    far_sum = lax.ppermute(sums[1], "depth", depth_far)
    near_sum = lax.ppermute(sums[0], "depth", depth_near)
    total = sums[2] + near_sum + far_sum
    result = jnp.maximum(total + coarse_bias[:, None], 0.0).astype(BF16)
    return result.reshape(16, 1, 2048)


def solution(mesh):
    placed = (
        P("depth", "rows", None, None),
        P(),
        P(),
        P(None, None, None, None, "rows"),
        P("rows"),
    )
    return jax.shard_map(
        body, mesh=mesh, in_specs=placed, out_specs=P("rows", "depth", None), check_vma=False
    )
```

```python
import jax
import jax.numpy as jnp
from jax import lax
from jax.experimental import pallas as pl
from jax.experimental.pallas import tpu as pltpu
from jax.sharding import PartitionSpec as P

BF16 = jnp.bfloat16
F32 = jnp.float32


def near_pairs(count):
    return [(i, i ^ 1) for i in range(count)]


def far_pairs(count):
    return [(i, ((i - 1) ^ 1) + 1) for i in range(1, count - 1)]


def fine_kernel(vol, x1, x2, r1, r2, c1, c2, w, bias, out, cells, peak):
    pd = lax.rem(lax.axis_index("depth"), 2)
    pr = lax.rem(lax.axis_index("rows"), 2)
    for j in range(4):
        for i in range(6):
            row = (i - 1) + pr * (5 - 2 * i)
            if j in (1, 2):
                plane = (j - 1) + pd * (3 - 2 * j)
                piece = r2[plane] if i == 0 else r1[plane] if i == 5 else vol[plane, row]
            else:
                side, slot = (x2, 1) if j == 0 else (x1, 0)
                piece = c2[slot] if i == 0 else c1[slot] if i == 5 else side[row]
            cells[j, i] = piece
    taps = [(a, b) for a in range(3) for b in range(3)]
    groups = [taps[i : i + 2] for i in range(0, 9, 2)]
    parts = []
    for s in range(2):
        total = None
        for group in groups:
            lhs = jnp.concatenate(
                [cells[s + a, b : b + 4].reshape(512, 128) for a, b in group], axis=1
            )
            rhs = jnp.concatenate(
                [
                    jnp.concatenate(
                        [w[a + pd * (2 - 2 * a), b + pr * (2 - 2 * b), c] for c in range(3)], axis=1
                    )
                    for a, b in group
                ],
                axis=0,
            )
            term = jnp.dot(lhs, rhs, preferred_element_type=F32)
            total = term if total is None else total + term
        parts.append(total)
    col = lax.broadcasted_iota(jnp.int32, (128, 128), 0)
    for q in range(2):
        best = None
        for s in range(2):
            for t in range(2):
                line = parts[s][(2 * q + t) * 128 : (2 * q + t + 1) * 128]
                left = jnp.where(col == 0, 0.0, pltpu.roll(line[:, :128], 1, 0))
                right = jnp.where(col == 127, 0.0, pltpu.roll(line[:, 256:], 127, 0))
                value = line[:, 128:256] + left + right
                best = value if best is None else jnp.maximum(best, value)
        peak[...] = best
        pooled = jnp.maximum(peak[pl.ds(0, 64, stride=2), :], peak[pl.ds(1, 64, stride=2), :])
        out[q + pr * (1 - 2 * q)] = jnp.maximum(pooled + bias[...], 0.0).astype(BF16)


def fine_level(vol, x1, x2, r1, r2, c1, c2, w, bias):
    vmem = pl.BlockSpec(memory_space=pltpu.VMEM)
    return pl.pallas_call(
        fine_kernel,
        out_shape=jax.ShapeDtypeStruct((2, 64, 128), BF16),
        in_specs=[vmem] * 9,
        out_specs=vmem,
        scratch_shapes=[pltpu.VMEM((4, 6, 128, 128), BF16), pltpu.VMEM((128, 128), F32)],
        compiler_params=pltpu.CompilerParams(vmem_limit_bytes=32 * 1024 * 1024),
    )(vol, x1, x2, r1, r2, c1, c2, w, bias)


def coarse_kernel(p0, p1, p2, p3, w0, w1, w2, w3, o0, o1, o2, o3, cells):
    pd = lax.rem(lax.axis_index("depth"), 2)
    z = lax.rem(lax.axis_index("rows"), 4)
    for a in range(3):
        for i in (0, 1, 10, 11):
            cells[a, i] = jnp.zeros((64, 128), BF16)
    for k, piece in enumerate((p0, p1, p2, p3)):
        cells[:, pl.ds(2 + 2 * (z ^ k), 2)] = piece[...]
    lhs = jnp.concatenate(
        [
            jnp.concatenate(
                [w[9 * (a + pd * (2 - 2 * a)) + 3 * b + c] for a in range(3) for b in range(3)], axis=1
            )
            for c in range(3)
            for w in (w0, w1, w2, w3)
        ],
        axis=0,
    )
    for start, size in ((0, 256), (256, 256), (512, 128)):
        if start < 512:
            first = start // 64 + 1
            blocks = [
                cells[a, first + b : first + b + 4].reshape(256, 128) for a in range(3) for b in range(3)
            ]
        else:
            blocks = [
                jnp.concatenate([cells[a, 9 + b], cells[a, b]], axis=0) for a in range(3) for b in range(3)
            ]
        rhs = jnp.concatenate(blocks, axis=1)
        term = lax.dot_general(lhs, rhs, (((1,), (1,)), ((), ())), preferred_element_type=F32)
        lane = lax.rem(lax.broadcasted_iota(jnp.int32, (64, size), 1), 64)
        left = jnp.where(lane == 0, 0.0, pltpu.roll(term[:64], 1, 1))
        right = jnp.where(lane == 63, 0.0, pltpu.roll(term[128:], size - 1, 1))
        value = term[64:128] + left + right
        for k, out in enumerate((o0, o1, o2, o3)):
            out[:, start : start + size] = value[16 * k : 16 * k + 16]


def coarse_level(pieces, weights):
    vmem = pl.BlockSpec(memory_space=pltpu.VMEM)
    return pl.pallas_call(
        coarse_kernel,
        out_shape=[jax.ShapeDtypeStruct((16, 640), F32)] * 4,
        in_specs=[vmem] * 8,
        out_specs=[vmem] * 4,
        scratch_shapes=[pltpu.VMEM((3, 12, 64, 128), BF16)],
        compiler_params=pltpu.CompilerParams(vmem_limit_bytes=32 * 1024 * 1024),
    )(*pieces, *weights)


def join_kernel(s0, s1, s2, s3, bias, out, held):
    y = lax.div(lax.axis_index("rows"), 4)
    for k, part in enumerate((s0, s1, s2, s3)):
        held[y ^ k] = part[...]
    low = lax.broadcasted_iota(jnp.int32, (16, 128), 1) < 64
    for m in range(4):
        tiles = [held[m, :, 128 * i : 128 * i + 128] for i in range(4)]
        if m > 0:
            tiles[0] = tiles[0] + jnp.where(low, held[m - 1, :, 512:], 0.0)
        if m < 3:
            tiles[3] = tiles[3] + jnp.where(low, 0.0, held[m + 1, :, 512:])
        for i in range(4):
            value = jnp.maximum(tiles[i] + bias[...], 0.0).astype(BF16)
            out[:, 512 * m + 128 * i : 512 * m + 128 * i + 128] = value


def join(parts, bias):
    vmem = pl.BlockSpec(memory_space=pltpu.VMEM)
    return pl.pallas_call(
        join_kernel,
        out_shape=jax.ShapeDtypeStruct((16, 2048), BF16),
        in_specs=[vmem] * 5,
        out_specs=vmem,
        scratch_shapes=[pltpu.VMEM((4, 16, 640), F32)],
        compiler_params=pltpu.CompilerParams(vmem_limit_bytes=32 * 1024 * 1024),
    )(*parts, bias)


def body(volume, fine_filters, fine_bias, coarse_filters, coarse_bias):
    d = lax.axis_index("depth")
    r = lax.axis_index("rows")
    pd = lax.rem(d, 2)
    pr = lax.rem(r, 2)
    depth_near, depth_far = near_pairs(16), far_pairs(16)
    rows_near, rows_far = near_pairs(16), far_pairs(16)

    x2 = lax.ppermute(lax.dynamic_index_in_dim(volume, pd, 0, False), "depth", depth_far)
    x1 = lax.ppermute(lax.dynamic_index_in_dim(volume, 1 - pd, 0, False), "depth", depth_near)
    r2 = lax.ppermute(lax.dynamic_index_in_dim(volume, 3 * pr, 1, False), "rows", rows_far)
    r1 = lax.ppermute(lax.dynamic_index_in_dim(volume, 3 - 3 * pr, 1, False), "rows", rows_near)
    sides = jnp.stack([x1, x2])
    c2 = lax.ppermute(lax.dynamic_index_in_dim(sides, 3 * pr, 1, False), "rows", rows_far)
    c1 = lax.ppermute(lax.dynamic_index_in_dim(sides, 3 - 3 * pr, 1, False), "rows", rows_near)
    pooled = fine_level(volume, x1, x2, r1, r2, c1, c2, fine_filters, fine_bias.reshape(1, 128))

    def along_z(k):
        return [(i, i ^ k) for i in range(16)]

    def along_y(k):
        return [(i, i ^ (4 * k)) for i in range(16)]

    w = jnp.transpose(coarse_filters, (0, 1, 2, 4, 3)).reshape(27, 16, 128)
    weights = [w] + [None] * 3
    for k in (2, 1, 3):
        weights[k] = lax.ppermute(w, "rows", along_y(k))

    far = lax.ppermute(pooled, "depth", depth_far)
    near = lax.ppermute(pooled, "depth", depth_near)
    planes = jnp.stack([far, pooled, near])
    pieces = [planes] + [None] * 3
    for k in (3, 2, 1):
        pieces[k] = lax.ppermute(planes, "rows", along_z(k))
    sums = coarse_level(pieces, weights)
    parts = [sums[0]] + [None] * 3
    for k in (2, 1, 3):
        parts[k] = lax.ppermute(sums[k], "rows", along_y(k))
    result = join(parts, jnp.broadcast_to(coarse_bias[:, None], (16, 128)))
    return result.reshape(16, 1, 2048)


def solution(mesh):
    placed = (
        P("depth", "rows", None, None),
        P(),
        P(),
        P(None, None, None, None, "rows"),
        P("rows"),
    )
    return jax.shard_map(
        body, mesh=mesh, in_specs=placed, out_specs=P("rows", "depth", None), check_vma=False
    )
```

```python
import jax
import jax.numpy as jnp
from jax import lax
from jax.experimental import pallas as pl
from jax.experimental.pallas import tpu as pltpu
from jax.sharding import PartitionSpec as P

BF16 = jnp.bfloat16
F32 = jnp.float32


def near_pairs(count):
    return [(i, i ^ 1) for i in range(count)]


def far_pairs(count):
    return [(i, ((i - 1) ^ 1) + 1) for i in range(1, count - 1)]


def bridge_pairs():
    pairs = []
    for d, e in far_pairs(16):
        for r in range(16):
            y, z = r // 4, r % 4
            if min(d, e) != 7:
                pairs.append((d * 16 + r, e * 16 + r))
            elif z in (0, 3):
                pairs.append((d * 16 + r, e * 16 + y * 4 + 3 - z))
    return pairs


def relay_pairs():
    pairs = []
    for d in (7, 8):
        for y in range(4):
            for z, t in ((0, 1), (3, 2)):
                pairs.append((d * 16 + y * 4 + z, d * 16 + y * 4 + t))
    return pairs


def edges_kernel(x1, x2, far_edge, near_edge):
    pr = lax.rem(lax.axis_index("rows"), 2)
    for k, side in enumerate((x1, x2)):
        far_edge[k] = side[3 * pr]
        near_edge[k] = side[3 - 3 * pr]

def edges(x1, x2):
    vmem = pl.BlockSpec(memory_space=pltpu.VMEM)
    edge = jax.ShapeDtypeStruct((2, 128, 128), BF16)
    return pl.pallas_call(
        edges_kernel,
        out_shape=[edge, edge],
        in_specs=[vmem] * 2,
        out_specs=[vmem] * 2,
        compiler_params=pltpu.CompilerParams(vmem_limit_bytes=8 * 1024 * 1024),
    )(x1, x2)


def fine_kernel(vol, x1, x2, r1, r2, c1, c2, w, bias, out, cells, peak):
    pd = lax.rem(lax.axis_index("depth"), 2)
    pr = lax.rem(lax.axis_index("rows"), 2)
    for j in range(4):
        for i in range(6):
            row = (i - 1) + pr * (5 - 2 * i)
            if j in (1, 2):
                plane = (j - 1) + pd * (3 - 2 * j)
                piece = r2[plane] if i == 0 else r1[plane] if i == 5 else vol[plane, row]
            else:
                side, slot = (x2, 1) if j == 0 else (x1, 0)
                piece = c2[slot] if i == 0 else c1[slot] if i == 5 else side[row]
            cells[j, i] = piece
    taps = [(a, b) for a in range(3) for b in range(3)]
    groups = [taps[i : i + 2] for i in range(0, 9, 2)]
    parts = []
    for s in range(2):
        total = None
        for group in groups:
            lhs = jnp.concatenate(
                [cells[s + a, b : b + 4].reshape(512, 128) for a, b in group], axis=1
            )
            rhs = jnp.concatenate(
                [
                    jnp.concatenate(
                        [w[a + pd * (2 - 2 * a), b + pr * (2 - 2 * b), c] for c in range(3)], axis=1
                    )
                    for a, b in group
                ],
                axis=0,
            )
            term = jnp.dot(lhs, rhs, preferred_element_type=F32)
            total = term if total is None else total + term
        parts.append(total)
    col = lax.broadcasted_iota(jnp.int32, (128, 128), 0)
    for q in range(2):
        best = None
        for s in range(2):
            for t in range(2):
                line = parts[s][(2 * q + t) * 128 : (2 * q + t + 1) * 128]
                left = jnp.where(col == 0, 0.0, pltpu.roll(line[:, :128], 1, 0))
                right = jnp.where(col == 127, 0.0, pltpu.roll(line[:, 256:], 127, 0))
                value = line[:, 128:256] + left + right
                best = value if best is None else jnp.maximum(best, value)
        peak[...] = best
        pooled = jnp.maximum(peak[pl.ds(0, 64, stride=2), :], peak[pl.ds(1, 64, stride=2), :])
        out[q + pr * (1 - 2 * q)] = jnp.maximum(pooled + bias[...], 0.0).astype(BF16)


def fine_level(vol, x1, x2, r1, r2, c1, c2, w, bias):
    vmem = pl.BlockSpec(memory_space=pltpu.VMEM)
    return pl.pallas_call(
        fine_kernel,
        out_shape=jax.ShapeDtypeStruct((2, 64, 128), BF16),
        in_specs=[vmem] * 9,
        out_specs=vmem,
        scratch_shapes=[pltpu.VMEM((4, 6, 128, 128), BF16), pltpu.VMEM((128, 128), F32)],
        compiler_params=pltpu.CompilerParams(vmem_limit_bytes=32 * 1024 * 1024),
    )(vol, x1, x2, r1, r2, c1, c2, w, bias)


def assemble_kernel(p0, p1, p2, p3, w, plane, kept):
    for k, piece in enumerate((p0, p1, p2, p3)):
        plane[k] = piece[...]
    kept[...] = w[...]


def assemble(pieces, w):
    vmem = pl.BlockSpec(memory_space=pltpu.VMEM)
    return pl.pallas_call(
        assemble_kernel,
        out_shape=[jax.ShapeDtypeStruct((4, 2, 64, 128), BF16), jax.ShapeDtypeStruct(w.shape, BF16)],
        in_specs=[vmem] * 5,
        out_specs=[vmem] * 2,
        compiler_params=pltpu.CompilerParams(vmem_limit_bytes=8 * 1024 * 1024),
    )(*pieces, w)


def coarse_kernel(own, near, far, via, w0, w1, w2, w3, o0, o1, o2, o3, cells):
    pd = lax.rem(lax.axis_index("depth"), 2)
    d = lax.axis_index("depth")
    z = lax.rem(lax.axis_index("rows"), 4)
    split = (d == 7) | (d == 8)
    relayed = split & ((z == 1) | (z == 2))
    far_z = jnp.where(split, jnp.where(z < 2, 3, 0), z)
    for a in range(3):
        for i in (0, 1, 10, 11):
            cells[a, i] = jnp.zeros((64, 128), BF16)
    for k in range(4):
        cells[0, pl.ds(2 + 2 * (far_z ^ k), 2)] = jnp.where(relayed, via[k], far[k])
        cells[1, pl.ds(2 + 2 * (z ^ k), 2)] = own[k]
        cells[2, pl.ds(2 + 2 * (z ^ k), 2)] = near[k]
    lhs = jnp.concatenate(
        [
            jnp.concatenate(
                [w[9 * (a + pd * (2 - 2 * a)) + 3 * b + c] for a in range(3) for b in range(3)], axis=1
            )
            for c in range(3)
            for w in (w0, w1, w2, w3)
        ],
        axis=0,
    )
    for start, size in ((0, 256), (256, 256), (512, 128)):
        if start < 512:
            first = start // 64 + 1
            blocks = [
                cells[a, first + b : first + b + 4].reshape(256, 128) for a in range(3) for b in range(3)
            ]
        else:
            blocks = [
                jnp.concatenate([cells[a, 9 + b], cells[a, b]], axis=0) for a in range(3) for b in range(3)
            ]
        rhs = jnp.concatenate(blocks, axis=1)
        term = lax.dot_general(lhs, rhs, (((1,), (1,)), ((), ())), preferred_element_type=F32)
        lane = lax.rem(lax.broadcasted_iota(jnp.int32, (64, size), 1), 64)
        left = jnp.where(lane == 0, 0.0, pltpu.roll(term[:64], 1, 1))
        right = jnp.where(lane == 63, 0.0, pltpu.roll(term[128:], size - 1, 1))
        value = term[64:128] + left + right
        for k, out in enumerate((o0, o1, o2, o3)):
            out[:, start : start + size] = value[16 * k : 16 * k + 16]


def coarse_level(pieces, weights):
    vmem = pl.BlockSpec(memory_space=pltpu.VMEM)
    return pl.pallas_call(
        coarse_kernel,
        out_shape=[jax.ShapeDtypeStruct((16, 640), F32)] * 4,
        in_specs=[vmem] * 8,
        out_specs=[vmem] * 4,
        scratch_shapes=[pltpu.VMEM((3, 12, 64, 128), BF16)],
        compiler_params=pltpu.CompilerParams(vmem_limit_bytes=32 * 1024 * 1024),
    )(*pieces, *weights)


def join_kernel(s0, s1, s2, s3, bias, out, held):
    y = lax.div(lax.axis_index("rows"), 4)
    for k, part in enumerate((s0, s1, s2, s3)):
        held[y ^ k] = part[...]
    low = lax.broadcasted_iota(jnp.int32, (16, 128), 1) < 64
    for m in range(4):
        tiles = [held[m, :, 128 * i : 128 * i + 128] for i in range(4)]
        if m > 0:
            tiles[0] = tiles[0] + jnp.where(low, held[m - 1, :, 512:], 0.0)
        if m < 3:
            tiles[3] = tiles[3] + jnp.where(low, 0.0, held[m + 1, :, 512:])
        for i in range(4):
            value = jnp.maximum(tiles[i] + bias[...], 0.0).astype(BF16)
            out[:, 512 * m + 128 * i : 512 * m + 128 * i + 128] = value


def join(parts, bias):
    vmem = pl.BlockSpec(memory_space=pltpu.VMEM)
    return pl.pallas_call(
        join_kernel,
        out_shape=jax.ShapeDtypeStruct((16, 2048), BF16),
        in_specs=[vmem] * 5,
        out_specs=vmem,
        scratch_shapes=[pltpu.VMEM((4, 16, 640), F32)],
        compiler_params=pltpu.CompilerParams(vmem_limit_bytes=32 * 1024 * 1024),
    )(*parts, bias)


def body(volume, fine_filters, fine_bias, coarse_filters, coarse_bias):
    d = lax.axis_index("depth")
    r = lax.axis_index("rows")
    pd = lax.rem(d, 2)
    pr = lax.rem(r, 2)
    depth_near, depth_far = near_pairs(16), far_pairs(16)
    rows_near, rows_far = near_pairs(16), far_pairs(16)

    x2 = lax.ppermute(lax.dynamic_index_in_dim(volume, pd, 0, False), "depth", depth_far)
    x1 = lax.ppermute(lax.dynamic_index_in_dim(volume, 1 - pd, 0, False), "depth", depth_near)
    r2 = lax.ppermute(lax.dynamic_index_in_dim(volume, 3 * pr, 1, False), "rows", rows_far)
    r1 = lax.ppermute(lax.dynamic_index_in_dim(volume, 3 - 3 * pr, 1, False), "rows", rows_near)
    far_edge, near_edge = edges(x1, x2)
    c2 = lax.ppermute(far_edge, "rows", rows_far)
    c1 = lax.ppermute(near_edge, "rows", rows_near)

    def along_z(k):
        return [(i, i ^ k) for i in range(16)]

    def along_y(k):
        return [(i, i ^ (4 * k)) for i in range(16)]

    pooled = fine_level(
        volume, x1, x2, r1, r2, c1, c2, fine_filters, fine_bias.reshape(1, 128)
    )

    pieces = [pooled] + [None] * 3
    for k in (3, 2, 1):
        pieces[k] = lax.ppermute(pooled, "rows", along_z(k))
    w = jnp.transpose(coarse_filters, (0, 1, 2, 4, 3)).reshape(27, 16, 128)
    plane, w = assemble(pieces, w)
    weights = [w] + [None] * 3
    for k in (2, 1, 3):
        weights[k] = lax.ppermute(w, "rows", along_y(k))
    both = ("depth", "rows")
    far = lax.ppermute(plane, both, bridge_pairs())
    near = lax.ppermute(plane, "depth", depth_near)
    via = lax.ppermute(far, both, relay_pairs())
    sums = coarse_level((plane, near, far, via), weights)
    parts = [sums[0]] + [None] * 3
    for k in (2, 1, 3):
        parts[k] = lax.ppermute(sums[k], "rows", along_y(k))
    result = join(parts, jnp.broadcast_to(coarse_bias[:, None], (16, 128)))
    return result.reshape(16, 1, 2048)


def solution(mesh):
    placed = (
        P("depth", "rows", None, None),
        P(),
        P(),
        P(None, None, None, None, "rows"),
        P("rows"),
    )
    return jax.shard_map(
        body, mesh=mesh, in_specs=placed, out_specs=P("rows", "depth", None), check_vma=False
    )
```

```python
import jax
import jax.numpy as jnp
from jax import lax
from jax.experimental import pallas as pl
from jax.experimental.pallas import tpu as pltpu
from jax.sharding import PartitionSpec as P

BF16 = jnp.bfloat16
F32 = jnp.float32


def near_pairs(count):
    return [(i, i ^ 1) for i in range(count)]


def far_pairs(count):
    return [(i, min(max(((i - 1) ^ 1) + 1, 0), count - 1)) for i in range(count)]


def inner(axis):
    i = lax.axis_index(axis)
    return (i > 0) & (i < 15)


def fine_kernel(vol, x1, x2, r1, r2, c1, c2, w, bias, out, cells, peak):
    pd = lax.rem(lax.axis_index("depth"), 2)
    pr = lax.rem(lax.axis_index("rows"), 2)
    inner_d = inner("depth")
    inner_r = inner("rows")
    zero = jnp.zeros((128, 128), BF16)
    for j in range(4):
        for i in range(6):
            row = (i - 1) + pr * (5 - 2 * i)
            if j in (1, 2):
                plane = (j - 1) + pd * (3 - 2 * j)
                piece = r2[plane] if i == 0 else r1[plane] if i == 5 else vol[plane, row]
            else:
                side, slot = (x2, 1) if j == 0 else (x1, 0)
                piece = c2[slot] if i == 0 else c1[slot] if i == 5 else side[row]
            if i == 0:
                piece = jnp.where(inner_r, piece, zero)
            if j == 0:
                piece = jnp.where(inner_d, piece, zero)
            cells[j, i] = piece
    taps = [(a, b) for a in range(3) for b in range(3)]
    groups = [taps[i : i + 2] for i in range(0, 9, 2)]
    parts = []
    for s in range(2):
        total = None
        for group in groups:
            lhs = jnp.concatenate(
                [cells[s + a, b : b + 4].reshape(512, 128) for a, b in group], axis=1
            )
            rhs = jnp.concatenate(
                [
                    jnp.concatenate(
                        [w[a + pd * (2 - 2 * a), b + pr * (2 - 2 * b), c] for c in range(3)], axis=1
                    )
                    for a, b in group
                ],
                axis=0,
            )
            term = jnp.dot(lhs, rhs, preferred_element_type=F32)
            total = term if total is None else total + term
        parts.append(total)
    col = lax.broadcasted_iota(jnp.int32, (128, 128), 0)
    for q in range(2):
        best = None
        for s in range(2):
            for t in range(2):
                line = parts[s][(2 * q + t) * 128 : (2 * q + t + 1) * 128]
                left = jnp.where(col == 0, 0.0, pltpu.roll(line[:, :128], 1, 0))
                right = jnp.where(col == 127, 0.0, pltpu.roll(line[:, 256:], 127, 0))
                value = line[:, 128:256] + left + right
                best = value if best is None else jnp.maximum(best, value)
        peak[...] = best
        pooled = jnp.maximum(peak[pl.ds(0, 64, stride=2), :], peak[pl.ds(1, 64, stride=2), :])
        out[q + pr * (1 - 2 * q)] = jnp.maximum(pooled + bias[...], 0.0).astype(BF16)


def fine_level(vol, x1, x2, r1, r2, c1, c2, w, bias):
    vmem = pl.BlockSpec(memory_space=pltpu.VMEM)
    return pl.pallas_call(
        fine_kernel,
        out_shape=jax.ShapeDtypeStruct((2, 64, 128), BF16),
        in_specs=[vmem] * 9,
        out_specs=vmem,
        scratch_shapes=[pltpu.VMEM((4, 6, 128, 128), BF16), pltpu.VMEM((128, 128), F32)],
        compiler_params=pltpu.CompilerParams(vmem_limit_bytes=32 * 1024 * 1024),
    )(vol, x1, x2, r1, r2, c1, c2, w, bias)


def assemble_kernel(p0, p1, p2, p3, w, plane, kept):
    for k, piece in enumerate((p0, p1, p2, p3)):
        plane[k] = piece[...]
    kept[...] = w[...]


def assemble(pieces, w):
    vmem = pl.BlockSpec(memory_space=pltpu.VMEM)
    return pl.pallas_call(
        assemble_kernel,
        out_shape=[jax.ShapeDtypeStruct((4, 2, 64, 128), BF16), jax.ShapeDtypeStruct(w.shape, BF16)],
        in_specs=[vmem] * 5,
        out_specs=[vmem] * 2,
        compiler_params=pltpu.CompilerParams(vmem_limit_bytes=8 * 1024 * 1024),
    )(*pieces, w)


def coarse_kernel(own, near, far, w0, w1, w2, w3, o0, o1, o2, o3, cells):
    pd = lax.rem(lax.axis_index("depth"), 2)
    z = lax.rem(lax.axis_index("rows"), 4)
    inner_d = inner("depth")
    for a in range(3):
        for i in (0, 1, 10, 11):
            cells[a, i] = jnp.zeros((64, 128), BF16)
    for k in range(4):
        cells[0, pl.ds(2 + 2 * (z ^ k), 2)] = jnp.where(inner_d, far[k], jnp.zeros_like(far[k]))
        cells[1, pl.ds(2 + 2 * (z ^ k), 2)] = own[k]
        cells[2, pl.ds(2 + 2 * (z ^ k), 2)] = near[k]
    lhs = jnp.concatenate(
        [
            jnp.concatenate(
                [w[9 * (a + pd * (2 - 2 * a)) + 3 * b + c] for a in range(3) for b in range(3)], axis=1
            )
            for c in range(3)
            for w in (w0, w1, w2, w3)
        ],
        axis=0,
    )
    for start, size in ((0, 256), (256, 256), (512, 128)):
        if start < 512:
            first = start // 64 + 1
            blocks = [
                cells[a, first + b : first + b + 4].reshape(256, 128) for a in range(3) for b in range(3)
            ]
        else:
            blocks = [
                jnp.concatenate([cells[a, 9 + b], cells[a, b]], axis=0) for a in range(3) for b in range(3)
            ]
        rhs = jnp.concatenate(blocks, axis=1)
        term = lax.dot_general(lhs, rhs, (((1,), (1,)), ((), ())), preferred_element_type=F32)
        lane = lax.rem(lax.broadcasted_iota(jnp.int32, (64, size), 1), 64)
        left = jnp.where(lane == 0, 0.0, pltpu.roll(term[:64], 1, 1))
        right = jnp.where(lane == 63, 0.0, pltpu.roll(term[128:], size - 1, 1))
        value = term[64:128] + left + right
        for k, out in enumerate((o0, o1, o2, o3)):
            out[:, start : start + size] = value[16 * k : 16 * k + 16]


def coarse_level(pieces, weights):
    vmem = pl.BlockSpec(memory_space=pltpu.VMEM)
    return pl.pallas_call(
        coarse_kernel,
        out_shape=[jax.ShapeDtypeStruct((16, 640), F32)] * 4,
        in_specs=[vmem] * 7,
        out_specs=[vmem] * 4,
        scratch_shapes=[pltpu.VMEM((3, 12, 64, 128), BF16)],
        compiler_params=pltpu.CompilerParams(vmem_limit_bytes=32 * 1024 * 1024),
    )(*pieces, *weights)


def join_kernel(s0, s1, s2, s3, bias, out, held):
    y = lax.div(lax.axis_index("rows"), 4)
    for k, part in enumerate((s0, s1, s2, s3)):
        held[y ^ k] = part[...]
    low = lax.broadcasted_iota(jnp.int32, (16, 128), 1) < 64
    for m in range(4):
        tiles = [held[m, :, 128 * i : 128 * i + 128] for i in range(4)]
        if m > 0:
            tiles[0] = tiles[0] + jnp.where(low, held[m - 1, :, 512:], 0.0)
        if m < 3:
            tiles[3] = tiles[3] + jnp.where(low, 0.0, held[m + 1, :, 512:])
        for i in range(4):
            value = jnp.maximum(tiles[i] + bias[...], 0.0).astype(BF16)
            out[:, 512 * m + 128 * i : 512 * m + 128 * i + 128] = value


def join(parts, bias):
    vmem = pl.BlockSpec(memory_space=pltpu.VMEM)
    return pl.pallas_call(
        join_kernel,
        out_shape=jax.ShapeDtypeStruct((16, 2048), BF16),
        in_specs=[vmem] * 5,
        out_specs=vmem,
        scratch_shapes=[pltpu.VMEM((4, 16, 640), F32)],
        compiler_params=pltpu.CompilerParams(vmem_limit_bytes=32 * 1024 * 1024),
    )(*parts, bias)


def body(volume, fine_filters, fine_bias, coarse_filters, coarse_bias):
    d = lax.axis_index("depth")
    r = lax.axis_index("rows")
    pd = lax.rem(d, 2)
    pr = lax.rem(r, 2)
    depth_near, depth_far = near_pairs(16), far_pairs(16)
    rows_near, rows_far = near_pairs(16), far_pairs(16)

    x2 = lax.ppermute(lax.dynamic_index_in_dim(volume, pd, 0, False), "depth", depth_far)
    x1 = lax.ppermute(lax.dynamic_index_in_dim(volume, 1 - pd, 0, False), "depth", depth_near)
    r2 = lax.ppermute(lax.dynamic_index_in_dim(volume, 3 * pr, 1, False), "rows", rows_far)
    r1 = lax.ppermute(lax.dynamic_index_in_dim(volume, 3 - 3 * pr, 1, False), "rows", rows_near)
    sides = jnp.stack([x1, x2])
    c2 = lax.ppermute(lax.dynamic_index_in_dim(sides, 3 * pr, 1, False), "rows", rows_far)
    c1 = lax.ppermute(lax.dynamic_index_in_dim(sides, 3 - 3 * pr, 1, False), "rows", rows_near)

    def along_z(k):
        return [(i, i ^ k) for i in range(16)]

    def along_y(k):
        return [(i, i ^ (4 * k)) for i in range(16)]

    pooled = fine_level(
        volume, x1, x2, r1, r2, c1, c2, fine_filters, fine_bias.reshape(1, 128)
    )

    pieces = [pooled] + [None] * 3
    for k in (3, 2, 1):
        pieces[k] = lax.ppermute(pooled, "rows", along_z(k))
    w = jnp.transpose(coarse_filters, (0, 1, 2, 4, 3)).reshape(27, 16, 128)
    plane, w = assemble(pieces, w)
    weights = [w] + [None] * 3
    for k in (2, 1, 3):
        weights[k] = lax.ppermute(w, "rows", along_y(k))
    far = lax.ppermute(plane, "depth", depth_far)
    near = lax.ppermute(plane, "depth", depth_near)
    sums = coarse_level((plane, near, far), weights)
    parts = [sums[0]] + [None] * 3
    for k in (2, 1, 3):
        parts[k] = lax.ppermute(sums[k], "rows", along_y(k))
    result = join(parts, jnp.broadcast_to(coarse_bias[:, None], (16, 128)))
    return result.reshape(16, 1, 2048)


def solution(mesh):
    placed = (
        P("depth", "rows", None, None),
        P(),
        P(),
        P(None, None, None, None, "rows"),
        P("rows"),
    )
    return jax.shard_map(
        body, mesh=mesh, in_specs=placed, out_specs=P("rows", "depth", None), check_vma=False
    )
```

```python
import jax
import jax.numpy as jnp
from jax import lax
from jax.experimental import pallas as pl
from jax.experimental.pallas import tpu as pltpu
from jax.sharding import PartitionSpec as P

BF16 = jnp.bfloat16
F32 = jnp.float32


def near_pairs(count):
    return [(i, i ^ 1) for i in range(count)]


def far_pairs(count):
    return [(i, min(max(((i - 1) ^ 1) + 1, 0), count - 1)) for i in range(count)]


def inner(axis):
    i = lax.axis_index(axis)
    return (i > 0) & (i < 15)


def fine_kernel(vol, x2, x1, r2, r1, w2, c2, c1, w, bias, out, cells, peak):
    pd = lax.rem(lax.axis_index("depth"), 2)
    pr = lax.rem(lax.axis_index("rows"), 2)
    inner_d = inner("depth")
    inner_r = inner("rows")
    zero = jnp.zeros((128, 128), BF16)
    for j in range(4):
        for i in range(6):
            row = (i - 1) + pr * (5 - 2 * i)
            if j in (1, 2):
                plane = (j - 1) + pd * (3 - 2 * j)
                piece = r2[plane] if i == 0 else r1[plane] if i == 5 else vol[plane, row]
            else:
                side, slot = (x2, 0) if j == 0 else (x1, 1)
                piece = c2[slot] if i == 0 else c1[slot] if i == 5 else side[row]
            if i == 0:
                piece = jnp.where(inner_r, piece, zero)
            if j == 0:
                piece = jnp.where(inner_d, piece, zero)
            cells[j, i] = piece
    taps = [(a, b) for a in range(3) for b in range(3)]
    groups = [taps[i : i + 2] for i in range(0, 9, 2)]
    parts = []
    for s in range(2):
        total = None
        for group in groups:
            lhs = jnp.concatenate(
                [cells[s + a, b : b + 4].reshape(512, 128) for a, b in group], axis=1
            )
            rhs = jnp.concatenate(
                [
                    jnp.concatenate(
                        [w[a + pd * (2 - 2 * a), b + pr * (2 - 2 * b), c] for c in range(3)], axis=1
                    )
                    for a, b in group
                ],
                axis=0,
            )
            term = jnp.dot(lhs, rhs, preferred_element_type=F32)
            total = term if total is None else total + term
        parts.append(total)
    col = lax.broadcasted_iota(jnp.int32, (128, 128), 0)
    for q in range(2):
        best = None
        for s in range(2):
            for t in range(2):
                line = parts[s][(2 * q + t) * 128 : (2 * q + t + 1) * 128]
                left = jnp.where(col == 0, 0.0, pltpu.roll(line[:, :128], 1, 0))
                right = jnp.where(col == 127, 0.0, pltpu.roll(line[:, 256:], 127, 0))
                value = line[:, 128:256] + left + right
                best = value if best is None else jnp.maximum(best, value)
        peak[...] = best
        pooled = jnp.maximum(peak[pl.ds(0, 64, stride=2), :], peak[pl.ds(1, 64, stride=2), :])
        out[q + pr * (1 - 2 * q)] = jnp.maximum(pooled + bias[...], 0.0).astype(BF16)


def fine_level(vol, x2, x1, r2, r1, w2, c2, c1, w, bias):
    vmem = pl.BlockSpec(memory_space=pltpu.VMEM)
    return pl.pallas_call(
        fine_kernel,
        out_shape=jax.ShapeDtypeStruct((2, 64, 128), BF16),
        in_specs=[vmem] * 5 + [pl.BlockSpec(memory_space=pl.ANY)] + [vmem] * 4,
        out_specs=vmem,
        scratch_shapes=[pltpu.VMEM((4, 6, 128, 128), BF16), pltpu.VMEM((128, 128), F32)],
        compiler_params=pltpu.CompilerParams(vmem_limit_bytes=32 * 1024 * 1024),
    )(vol, x2, x1, r2, r1, w2, c2, c1, w, bias)


def assemble_kernel(p0, p1, p2, p3, w, plane, kept):
    for k, piece in enumerate((p0, p1, p2, p3)):
        plane[k] = piece[...]
    kept[...] = w[...]


def assemble(pieces, w):
    vmem = pl.BlockSpec(memory_space=pltpu.VMEM)
    return pl.pallas_call(
        assemble_kernel,
        out_shape=[jax.ShapeDtypeStruct((4, 2, 64, 128), BF16), jax.ShapeDtypeStruct(w.shape, BF16)],
        in_specs=[vmem] * 5,
        out_specs=[vmem] * 2,
        compiler_params=pltpu.CompilerParams(vmem_limit_bytes=8 * 1024 * 1024),
    )(*pieces, w)


def coarse_kernel(own, far, near, w0, w1, w2, w3, o0, o1, o2, o3, cells):
    pd = lax.rem(lax.axis_index("depth"), 2)
    z = lax.rem(lax.axis_index("rows"), 4)
    inner_d = inner("depth")
    for a in range(3):
        for i in (0, 1, 10, 11):
            cells[a, i] = jnp.zeros((64, 128), BF16)
    for m, k in enumerate((0, 3, 2, 1)):
        cells[0, pl.ds(2 + 2 * (z ^ k), 2)] = jnp.where(inner_d, far[m], jnp.zeros_like(far[m]))
        cells[1, pl.ds(2 + 2 * (z ^ k), 2)] = own[m]
        cells[2, pl.ds(2 + 2 * (z ^ k), 2)] = near[m]
    lhs = jnp.concatenate(
        [
            jnp.concatenate(
                [w[9 * (a + pd * (2 - 2 * a)) + 3 * b + c] for a in range(3) for b in range(3)], axis=1
            )
            for c in range(3)
            for w in (w0, w1, w2, w3)
        ],
        axis=0,
    )
    for start, size in ((0, 256), (256, 256), (512, 128)):
        if start < 512:
            first = start // 64 + 1
            blocks = [
                cells[a, first + b : first + b + 4].reshape(256, 128) for a in range(3) for b in range(3)
            ]
        else:
            blocks = [
                jnp.concatenate([cells[a, 9 + b], cells[a, b]], axis=0) for a in range(3) for b in range(3)
            ]
        rhs = jnp.concatenate(blocks, axis=1)
        term = lax.dot_general(lhs, rhs, (((1,), (1,)), ((), ())), preferred_element_type=F32)
        lane = lax.rem(lax.broadcasted_iota(jnp.int32, (64, size), 1), 64)
        left = jnp.where(lane == 0, 0.0, pltpu.roll(term[:64], 1, 1))
        right = jnp.where(lane == 63, 0.0, pltpu.roll(term[128:], size - 1, 1))
        value = term[64:128] + left + right
        for k, out in enumerate((o0, o1, o2, o3)):
            out[:, start : start + size] = value[16 * k : 16 * k + 16]


def coarse_level(pieces, weights):
    vmem = pl.BlockSpec(memory_space=pltpu.VMEM)
    return pl.pallas_call(
        coarse_kernel,
        out_shape=[jax.ShapeDtypeStruct((16, 640), F32)] * 4,
        in_specs=[vmem] * 7,
        out_specs=[vmem] * 4,
        scratch_shapes=[pltpu.VMEM((3, 12, 64, 128), BF16)],
        compiler_params=pltpu.CompilerParams(vmem_limit_bytes=32 * 1024 * 1024),
    )(*pieces, *weights)


def join_kernel(s0, s2, s1, s3, bias, out, held):
    y = lax.div(lax.axis_index("rows"), 4)
    for k, part in enumerate((s0, s1, s2, s3)):
        held[y ^ k] = part[...]
    low = lax.broadcasted_iota(jnp.int32, (16, 128), 1) < 64
    for m in range(4):
        tiles = [held[m, :, 128 * i : 128 * i + 128] for i in range(4)]
        if m > 0:
            tiles[0] = tiles[0] + jnp.where(low, held[m - 1, :, 512:], 0.0)
        if m < 3:
            tiles[3] = tiles[3] + jnp.where(low, 0.0, held[m + 1, :, 512:])
        for i in range(4):
            value = jnp.maximum(tiles[i] + bias[...], 0.0).astype(BF16)
            out[:, 512 * m + 128 * i : 512 * m + 128 * i + 128] = value


def join(parts, bias):
    vmem = pl.BlockSpec(memory_space=pltpu.VMEM)
    return pl.pallas_call(
        join_kernel,
        out_shape=jax.ShapeDtypeStruct((16, 2048), BF16),
        in_specs=[vmem] * 5,
        out_specs=vmem,
        scratch_shapes=[pltpu.VMEM((4, 16, 640), F32)],
        compiler_params=pltpu.CompilerParams(vmem_limit_bytes=32 * 1024 * 1024),
    )(*parts, bias)


def body(volume, fine_filters, fine_bias, coarse_filters, coarse_bias):
    d = lax.axis_index("depth")
    r = lax.axis_index("rows")
    pd = lax.rem(d, 2)
    pr = lax.rem(r, 2)
    depth_near, depth_far = near_pairs(16), far_pairs(16)
    rows_near, rows_far = near_pairs(16), far_pairs(16)

    x2 = lax.ppermute(lax.dynamic_index_in_dim(volume, pd, 0, False), "depth", depth_far)
    x1 = lax.ppermute(lax.dynamic_index_in_dim(volume, 1 - pd, 0, False), "depth", depth_near)
    r2 = lax.ppermute(lax.dynamic_index_in_dim(volume, 3 * pr, 1, False), "rows", rows_far)
    r1 = lax.ppermute(lax.dynamic_index_in_dim(volume, 3 - 3 * pr, 1, False), "rows", rows_near)
    sides = jnp.stack([x2, x1])
    c2 = lax.ppermute(lax.dynamic_index_in_dim(sides, 3 * pr, 1, False), "rows", rows_far)
    c1 = lax.ppermute(lax.dynamic_index_in_dim(sides, 3 - 3 * pr, 1, False), "rows", rows_near)

    def along_z(k):
        return [(i, i ^ k) for i in range(16)]

    def along_y(k):
        return [(i, i ^ (4 * k)) for i in range(16)]

    w = jnp.transpose(coarse_filters, (0, 1, 2, 4, 3)).reshape(27, 16, 128)
    w2 = lax.ppermute(w, "rows", along_y(2))
    pooled = fine_level(
        volume, x2, x1, r2, r1, w2, c2, c1, fine_filters, fine_bias.reshape(1, 128)
    )

    plane, kept = assemble([pooled] + [lax.ppermute(pooled, "rows", along_z(k)) for k in (3, 2, 1)], w)
    w1, w3 = [lax.ppermute(kept, "rows", along_y(k)) for k in (1, 3)]
    far = lax.ppermute(plane, "depth", depth_far)
    near = lax.ppermute(plane, "depth", depth_near)
    sums = coarse_level((plane, far, near), (w, w1, w2, w3))
    parts = [sums[0]] + [lax.ppermute(sums[k], "rows", along_y(k)) for k in (2, 1, 3)]
    result = join(parts, jnp.broadcast_to(coarse_bias[:, None], (16, 128)))
    return result.reshape(16, 1, 2048)


def solution(mesh):
    placed = (
        P("depth", "rows", None, None),
        P(),
        P(),
        P(None, None, None, None, "rows"),
        P("rows"),
    )
    return jax.shard_map(
        body, mesh=mesh, in_specs=placed, out_specs=P("rows", "depth", None), check_vma=False
    )
```

```python
import jax
import jax.numpy as jnp
from jax import lax
from jax.experimental import pallas as pl
from jax.experimental.pallas import tpu as pltpu
from jax.sharding import PartitionSpec as P

BF16 = jnp.bfloat16
F32 = jnp.float32


def near_pairs(count):
    return [(i, i ^ 1) for i in range(count)]


def far_pairs(count):
    return [(i, min(max(((i - 1) ^ 1) + 1, 0), count - 1)) for i in range(count)]


def far_and_z():
    pairs = [(d, d + 1) for d in range(1, 15, 2)] + [(15, 0)]
    return [[d * 16 + 4 * y + z for d in pair for z in range(4)] for pair in pairs for y in range(4)]


def inner(axis):
    i = lax.axis_index(axis)
    return (i > 0) & (i < 15)


def fine_kernel(vol, x2, x1, r2, r1, c2, c1, other, w, bias, out, cells, peak):
    pd = lax.rem(lax.axis_index("depth"), 2)
    pr = lax.rem(lax.axis_index("rows"), 2)
    inner_d = inner("depth")
    inner_r = inner("rows")
    zero = jnp.zeros((128, 128), BF16)
    for j in range(4):
        for i in range(6):
            row = (i - 1) + pr * (5 - 2 * i)
            if j in (1, 2):
                plane = (j - 1) + pd * (3 - 2 * j)
                piece = r2[plane] if i == 0 else r1[plane] if i == 5 else vol[plane, row]
            else:
                side, slot = (x2, 0) if j == 0 else (x1, 1)
                piece = c2[slot] if i == 0 else c1[slot] if i == 5 else side[row]
            if i == 0:
                piece = jnp.where(inner_r, piece, zero)
            if j == 0:
                piece = jnp.where(inner_d, piece, zero)
            cells[j, i] = piece
    taps = [(a, b) for a in range(3) for b in range(3)]
    groups = [taps[i : i + 2] for i in range(0, 9, 2)]
    parts = []
    for s in range(2):
        total = None
        for group in groups:
            lhs = jnp.concatenate(
                [cells[s + a, b : b + 4].reshape(512, 128) for a, b in group], axis=1
            )
            rhs = jnp.concatenate(
                [
                    jnp.concatenate(
                        [w[a + pd * (2 - 2 * a), b + pr * (2 - 2 * b), c] for c in range(3)], axis=1
                    )
                    for a, b in group
                ],
                axis=0,
            )
            term = jnp.dot(lhs, rhs, preferred_element_type=F32)
            total = term if total is None else total + term
        parts.append(total)
    col = lax.broadcasted_iota(jnp.int32, (128, 128), 0)
    for q in range(2):
        best = None
        for s in range(2):
            for t in range(2):
                line = parts[s][(2 * q + t) * 128 : (2 * q + t + 1) * 128]
                left = jnp.where(col == 0, 0.0, pltpu.roll(line[:, :128], 1, 0))
                right = jnp.where(col == 127, 0.0, pltpu.roll(line[:, 256:], 127, 0))
                value = line[:, 128:256] + left + right
                best = value if best is None else jnp.maximum(best, value)
        peak[...] = best
        pooled = jnp.maximum(peak[pl.ds(0, 64, stride=2), :], peak[pl.ds(1, 64, stride=2), :])
        value = jnp.maximum(pooled + bias[...], 0.0).astype(BF16)
        for k in range(8):
            out[k, q + pr * (1 - 2 * q)] = value


def fine_level(vol, x2, x1, r2, r1, c2, c1, other, w, bias):
    vmem = pl.BlockSpec(memory_space=pltpu.VMEM)
    return pl.pallas_call(
        fine_kernel,
        out_shape=jax.ShapeDtypeStruct((8, 2, 64, 128), BF16),
        in_specs=[vmem] * 7 + [pl.BlockSpec(memory_space=pl.ANY)] + [vmem] * 2,
        out_specs=vmem,
        scratch_shapes=[pltpu.VMEM((4, 6, 128, 128), BF16), pltpu.VMEM((128, 128), F32)],
        compiler_params=pltpu.CompilerParams(vmem_limit_bytes=32 * 1024 * 1024),
    )(vol, x2, x1, r2, r1, c2, c1, other, w, bias)


def coarse_kernel(both, near, pair, other, o0, o1, o2, o3, cells):
    pd = lax.rem(lax.axis_index("depth"), 2)
    inner_d = inner("depth")
    for a in range(3):
        for i in (0, 1, 10, 11):
            cells[a, i] = jnp.zeros((64, 128), BF16)
    for k in range(4):
        far = both[pd, k]
        cells[0, 2 + 2 * k : 4 + 2 * k] = jnp.where(inner_d, far, jnp.zeros_like(far))
        cells[1, 2 + 2 * k : 4 + 2 * k] = both[1 - pd, k]
        cells[2, 2 + 2 * k : 4 + 2 * k] = near[k]
    lhs = jnp.concatenate(
        [
            jnp.concatenate(
                [w[m, 9 * (a + pd * (2 - 2 * a)) + 3 * b + c] for a in range(3) for b in range(3)], axis=1
            )
            for c in range(3)
            for w, m in ((pair, 0), (pair, 1), (other, 0), (other, 1))
        ],
        axis=0,
    )
    for start, size in ((0, 256), (256, 256), (512, 128)):
        if start < 512:
            first = start // 64 + 1
            blocks = [
                cells[a, first + b : first + b + 4].reshape(256, 128) for a in range(3) for b in range(3)
            ]
        else:
            blocks = [
                jnp.concatenate([cells[a, 9 + b], cells[a, b]], axis=0) for a in range(3) for b in range(3)
            ]
        rhs = jnp.concatenate(blocks, axis=1)
        term = lax.dot_general(lhs, rhs, (((1,), (1,)), ((), ())), preferred_element_type=F32)
        lane = lax.rem(lax.broadcasted_iota(jnp.int32, (64, size), 1), 64)
        left = jnp.where(lane == 0, 0.0, pltpu.roll(term[:64], 1, 1))
        right = jnp.where(lane == 63, 0.0, pltpu.roll(term[128:], size - 1, 1))
        value = term[64:128] + left + right
        for k, out in enumerate((o0, o1, o2, o3)):
            out[:, start : start + size] = value[16 * k : 16 * k + 16]


def coarse_level(both, near, pair, other):
    vmem = pl.BlockSpec(memory_space=pltpu.VMEM)
    return pl.pallas_call(
        coarse_kernel,
        out_shape=[jax.ShapeDtypeStruct((16, 640), F32)] * 4,
        in_specs=[vmem] * 4,
        out_specs=[vmem] * 4,
        scratch_shapes=[pltpu.VMEM((3, 12, 64, 128), BF16)],
        compiler_params=pltpu.CompilerParams(vmem_limit_bytes=32 * 1024 * 1024),
    )(both, near, pair, other)


def join_kernel(s0, s2, s1, s3, bias, out, held):
    y = lax.div(lax.axis_index("rows"), 4)
    for k, part in enumerate((s0, s1, s2, s3)):
        held[y ^ k] = part[...]
    low = lax.broadcasted_iota(jnp.int32, (16, 128), 1) < 64
    for m in range(4):
        tiles = [held[m, :, 128 * i : 128 * i + 128] for i in range(4)]
        if m > 0:
            tiles[0] = tiles[0] + jnp.where(low, held[m - 1, :, 512:], 0.0)
        if m < 3:
            tiles[3] = tiles[3] + jnp.where(low, 0.0, held[m + 1, :, 512:])
        for i in range(4):
            value = jnp.maximum(tiles[i] + bias[...], 0.0).astype(BF16)
            out[:, 512 * m + 128 * i : 512 * m + 128 * i + 128] = value


def join(parts, bias):
    vmem = pl.BlockSpec(memory_space=pltpu.VMEM)
    return pl.pallas_call(
        join_kernel,
        out_shape=jax.ShapeDtypeStruct((16, 2048), BF16),
        in_specs=[vmem] * 5,
        out_specs=vmem,
        scratch_shapes=[pltpu.VMEM((4, 16, 640), F32)],
        compiler_params=pltpu.CompilerParams(vmem_limit_bytes=32 * 1024 * 1024),
    )(*parts, bias)


def body(volume, fine_filters, fine_bias, coarse_filters, coarse_bias):
    d = lax.axis_index("depth")
    r = lax.axis_index("rows")
    pd = lax.rem(d, 2)
    pr = lax.rem(r, 2)
    depth_near, depth_far = near_pairs(16), far_pairs(16)
    rows_near, rows_far = near_pairs(16), far_pairs(16)

    x2 = lax.ppermute(lax.dynamic_index_in_dim(volume, pd, 0, False), "depth", depth_far)
    x1 = lax.ppermute(lax.dynamic_index_in_dim(volume, 1 - pd, 0, False), "depth", depth_near)
    r2 = lax.ppermute(lax.dynamic_index_in_dim(volume, 3 * pr, 1, False), "rows", rows_far)
    r1 = lax.ppermute(lax.dynamic_index_in_dim(volume, 3 - 3 * pr, 1, False), "rows", rows_near)
    sides = jnp.stack([x2, x1])
    c2 = lax.ppermute(lax.dynamic_index_in_dim(sides, 3 * pr, 1, False), "rows", rows_far)
    c1 = lax.ppermute(lax.dynamic_index_in_dim(sides, 3 - 3 * pr, 1, False), "rows", rows_near)

    def along_y(k):
        return [(i, i ^ (4 * k)) for i in range(16)]

    w = jnp.transpose(coarse_filters, (0, 1, 2, 4, 3)).reshape(27, 16, 128)
    pair = jnp.stack([w, lax.ppermute(w, "rows", along_y(1))])
    other = lax.ppermute(pair, "rows", along_y(2))
    pooled = fine_level(
        volume, x2, x1, r2, r1, c2, c1, other, fine_filters, fine_bias.reshape(1, 128)
    )

    both = lax.all_to_all(
        pooled, ("depth", "rows"), 0, 0, axis_index_groups=far_and_z(), tiled=True
    ).reshape(2, 4, 2, 64, 128)
    near = lax.ppermute(lax.dynamic_index_in_dim(both, 1 - pd, 0, False), "depth", depth_near)
    sums = coarse_level(both, near, pair, other)
    parts = [sums[0]] + [lax.ppermute(sums[k], "rows", along_y(k)) for k in (2, 1, 3)]
    result = join(parts, jnp.broadcast_to(coarse_bias[:, None], (16, 128)))
    return result.reshape(16, 1, 2048)


def solution(mesh):
    placed = (
        P("depth", "rows", None, None),
        P(),
        P(),
        P(None, None, None, None, "rows"),
        P("rows"),
    )
    return jax.shard_map(
        body, mesh=mesh, in_specs=placed, out_specs=P("rows", "depth", None), check_vma=False
    )
```

```python
import jax
import jax.numpy as jnp
from jax import lax
from jax.experimental import pallas as pl
from jax.experimental.pallas import tpu as pltpu
from jax.sharding import PartitionSpec as P

BF16 = jnp.bfloat16
F32 = jnp.float32


def near_pairs(count):
    return [(i, i ^ 1) for i in range(count)]


def far_pairs(count):
    return [(i, min(max(((i - 1) ^ 1) + 1, 0), count - 1)) for i in range(count)]


def far_and_z():
    pairs = [(d, d + 1) for d in range(1, 15, 2)] + [(15, 0)]
    return [[d * 16 + 4 * y + z for d in pair for z in range(4)] for pair in pairs for y in range(4)]


def inner(axis):
    i = lax.axis_index(axis)
    return (i > 0) & (i < 15)


def spread(line, col):
    left = jnp.where(col == 0, 0.0, pltpu.roll(line[:, :128], 1, 0))
    right = jnp.where(col == 127, 0.0, pltpu.roll(line[:, 256:], 127, 0))
    return line[:, 128:256] + left + right


def fine_kernel(vol, x2, x1, r2, r1, w, out, cells):
    pd = lax.rem(lax.axis_index("depth"), 2)
    pr = lax.rem(lax.axis_index("rows"), 2)
    inner_d = inner("depth")
    inner_r = inner("rows")
    zero = jnp.zeros((128, 128), BF16)
    for j in range(4):
        for i in range(6):
            row = (i - 1) + pr * (5 - 2 * i)
            if j in (1, 2):
                plane = (j - 1) + pd * (3 - 2 * j)
                piece = r2[plane] if i == 0 else r1[plane] if i == 5 else vol[plane, row]
            elif i in (0, 5):
                piece = zero
            else:
                piece = (x2 if j == 0 else x1)[row]
            if i == 0:
                piece = jnp.where(inner_r, piece, zero)
            if j == 0:
                piece = jnp.where(inner_d, piece, zero)
            cells[j, i] = piece
    taps = [(a, b) for a in range(3) for b in range(3)]
    groups = [taps[i : i + 2] for i in range(0, 9, 2)]
    col = lax.broadcasted_iota(jnp.int32, (128, 128), 0)
    for s in range(2):
        total = None
        for group in groups:
            lhs = jnp.concatenate(
                [cells[s + a, b : b + 4].reshape(512, 128) for a, b in group], axis=1
            )
            rhs = jnp.concatenate(
                [
                    jnp.concatenate(
                        [w[a + pd * (2 - 2 * a), b + pr * (2 - 2 * b), c] for c in range(3)], axis=1
                    )
                    for a, b in group
                ],
                axis=0,
            )
            term = jnp.dot(lhs, rhs, preferred_element_type=F32)
            total = term if total is None else total + term
        for t in range(4):
            out[s, t] = spread(total[t * 128 : (t + 1) * 128], col)


def fine_level(vol, x2, x1, r2, r1, w):
    vmem = pl.BlockSpec(memory_space=pltpu.VMEM)
    return pl.pallas_call(
        fine_kernel,
        out_shape=jax.ShapeDtypeStruct((2, 4, 128, 128), F32),
        in_specs=[vmem] * 6,
        out_specs=vmem,
        scratch_shapes=[pltpu.VMEM((4, 6, 128, 128), BF16)],
        compiler_params=pltpu.CompilerParams(vmem_limit_bytes=32 * 1024 * 1024),
        cost_estimate=pl.CostEstimate(flops=20_000_000_000, bytes_accessed=0, transcendentals=0),
    )(vol, x2, x1, r2, r1, w)


def finish_kernel(sums, c2, c1, w, bias, out, peak):
    pd = lax.rem(lax.axis_index("depth"), 2)
    pr = lax.rem(lax.axis_index("rows"), 2)
    inner_d = inner("depth")
    inner_r = inner("rows")
    zero = jnp.zeros((128, 128), BF16)
    col = lax.broadcasted_iota(jnp.int32, (128, 128), 0)
    for q in range(2):
        edge = 2 * q
        best = None
        for s in range(2):
            side = 2 * s
            piece = (c2, c1)[q][s]
            if q == 0:
                piece = jnp.where(inner_r, piece, zero)
            if s == 0:
                piece = jnp.where(inner_d, piece, zero)
            rhs = jnp.concatenate(
                [w[side + pd * (2 - 2 * side), edge + pr * (2 - 2 * edge), c] for c in range(3)], axis=1
            )
            corner = spread(jnp.dot(piece, rhs, preferred_element_type=F32), col)
            value = jnp.maximum(sums[s, 3 * q] + corner, sums[s, q + 1])
            best = value if best is None else jnp.maximum(best, value)
        peak[...] = best
        pooled = jnp.maximum(peak[pl.ds(0, 64, stride=2), :], peak[pl.ds(1, 64, stride=2), :])
        pooled = jnp.maximum(pooled + bias[...], 0.0).astype(BF16)
        for k in range(8):
            out[k, q + pr * (1 - 2 * q)] = pooled


def finish(sums, c2, c1, w, bias):
    vmem = pl.BlockSpec(memory_space=pltpu.VMEM)
    return pl.pallas_call(
        finish_kernel,
        out_shape=jax.ShapeDtypeStruct((8, 2, 64, 128), BF16),
        in_specs=[vmem] * 5,
        out_specs=vmem,
        scratch_shapes=[pltpu.VMEM((128, 128), F32)],
        compiler_params=pltpu.CompilerParams(vmem_limit_bytes=32 * 1024 * 1024),
    )(sums, c2, c1, w, bias)


def coarse_kernel(both, near, pair, other, out, cells):
    pd = lax.rem(lax.axis_index("depth"), 2)
    y = lax.div(lax.axis_index("rows"), 4)
    inner_d = inner("depth")
    for a in range(3):
        for i in (0, 1, 10, 11):
            cells[a, i] = jnp.zeros((64, 128), BF16)
    for k in range(4):
        far = both[pd, k]
        cells[0, 2 + 2 * k : 4 + 2 * k] = jnp.where(inner_d, far, jnp.zeros_like(far))
        cells[1, 2 + 2 * k : 4 + 2 * k] = both[1 - pd, k]
        cells[2, 2 + 2 * k : 4 + 2 * k] = near[k]
    lhs = jnp.concatenate(
        [
            jnp.concatenate(
                [w[m, 9 * (a + pd * (2 - 2 * a)) + 3 * b + c] for a in range(3) for b in range(3)], axis=1
            )
            for c in range(3)
            for w, m in ((pair, 0), (pair, 1), (other, 0), (other, 1))
        ],
        axis=0,
    )
    for start, size in ((0, 256), (256, 256), (512, 128)):
        if start < 512:
            first = start // 64 + 1
            blocks = [
                cells[a, first + b : first + b + 4].reshape(256, 128) for a in range(3) for b in range(3)
            ]
        else:
            blocks = [
                jnp.concatenate([cells[a, 9 + b], cells[a, b]], axis=0) for a in range(3) for b in range(3)
            ]
        rhs = jnp.concatenate(blocks, axis=1)
        term = lax.dot_general(lhs, rhs, (((1,), (1,)), ((), ())), preferred_element_type=F32)
        lane = lax.rem(lax.broadcasted_iota(jnp.int32, (64, size), 1), 64)
        left = jnp.where(lane == 0, 0.0, pltpu.roll(term[:64], 1, 1))
        right = jnp.where(lane == 63, 0.0, pltpu.roll(term[128:], size - 1, 1))
        value = term[64:128] + left + right
        for k in range(4):
            out[y ^ k, :, start : start + size] = value[16 * k : 16 * k + 16]


def coarse_level(both, near, pair, other):
    vmem = pl.BlockSpec(memory_space=pltpu.VMEM)
    return pl.pallas_call(
        coarse_kernel,
        out_shape=jax.ShapeDtypeStruct((4, 16, 640), F32),
        in_specs=[vmem] * 4,
        out_specs=vmem,
        scratch_shapes=[pltpu.VMEM((3, 12, 64, 128), BF16)],
        compiler_params=pltpu.CompilerParams(vmem_limit_bytes=32 * 1024 * 1024),
    )(both, near, pair, other)


def join_kernel(held, bias, out):
    low = lax.broadcasted_iota(jnp.int32, (16, 128), 1) < 64
    for m in range(4):
        tiles = [held[m, :, 128 * i : 128 * i + 128] for i in range(4)]
        if m > 0:
            tiles[0] = tiles[0] + jnp.where(low, held[m - 1, :, 512:], 0.0)
        if m < 3:
            tiles[3] = tiles[3] + jnp.where(low, 0.0, held[m + 1, :, 512:])
        for i in range(4):
            value = jnp.maximum(tiles[i] + bias[...], 0.0).astype(BF16)
            out[:, 512 * m + 128 * i : 512 * m + 128 * i + 128] = value


def join(parts, bias):
    vmem = pl.BlockSpec(memory_space=pltpu.VMEM)
    return pl.pallas_call(
        join_kernel,
        out_shape=jax.ShapeDtypeStruct((16, 2048), BF16),
        in_specs=[vmem] * 2,
        out_specs=vmem,
        compiler_params=pltpu.CompilerParams(vmem_limit_bytes=32 * 1024 * 1024),
    )(parts, bias)


def body(volume, fine_filters, fine_bias, coarse_filters, coarse_bias):
    d = lax.axis_index("depth")
    r = lax.axis_index("rows")
    pd = lax.rem(d, 2)
    pr = lax.rem(r, 2)
    depth_near, depth_far = near_pairs(16), far_pairs(16)
    rows_near, rows_far = near_pairs(16), far_pairs(16)

    x2 = lax.ppermute(lax.dynamic_index_in_dim(volume, pd, 0, False), "depth", depth_far)
    x1 = lax.ppermute(lax.dynamic_index_in_dim(volume, 1 - pd, 0, False), "depth", depth_near)
    r2 = lax.ppermute(lax.dynamic_index_in_dim(volume, 3 * pr, 1, False), "rows", rows_far)
    r1 = lax.ppermute(lax.dynamic_index_in_dim(volume, 3 - 3 * pr, 1, False), "rows", rows_near)
    sides = jnp.stack([x2, x1])
    c2 = lax.ppermute(lax.dynamic_index_in_dim(sides, 3 * pr, 1, False), "rows", rows_far)
    c1 = lax.ppermute(lax.dynamic_index_in_dim(sides, 3 - 3 * pr, 1, False), "rows", rows_near)

    def along_y(k):
        return [(i, i ^ (4 * k)) for i in range(16)]

    w = jnp.transpose(coarse_filters, (0, 1, 2, 4, 3)).reshape(27, 16, 128)
    pair = jnp.stack([w, lax.ppermute(w, "rows", along_y(1))])
    other = lax.ppermute(pair, "rows", along_y(2))
    main = fine_level(volume, x2, x1, r2, r1, fine_filters)
    pooled = finish(main, c2, c1, fine_filters, fine_bias.reshape(1, 128))

    both = lax.all_to_all(
        pooled, ("depth", "rows"), 0, 0, axis_index_groups=far_and_z(), tiled=True
    ).reshape(2, 4, 2, 64, 128)
    near = lax.ppermute(lax.dynamic_index_in_dim(both, 1 - pd, 0, False), "depth", depth_near)
    sums = coarse_level(both, near, pair, other)
    parts = lax.all_to_all(
        sums, "rows", 0, 0, axis_index_groups=[[4 * y + z for y in range(4)] for z in range(4)], tiled=True
    )
    result = join(parts, jnp.broadcast_to(coarse_bias[:, None], (16, 128)))
    return result.reshape(16, 1, 2048)


def solution(mesh):
    placed = (
        P("depth", "rows", None, None),
        P(),
        P(),
        P(None, None, None, None, "rows"),
        P("rows"),
    )
    return jax.shard_map(
        body, mesh=mesh, in_specs=placed, out_specs=P("rows", "depth", None), check_vma=False
    )
```

```python
import jax
import jax.numpy as jnp
from jax import lax
from jax.experimental import pallas as pl
from jax.experimental.pallas import tpu as pltpu
from jax.sharding import PartitionSpec as P

BF16 = jnp.bfloat16
F32 = jnp.float32


def near_pairs(count):
    return [(i, i ^ 1) for i in range(count)]


def far_pairs(count):
    return [(i, min(max(((i - 1) ^ 1) + 1, 0), count - 1)) for i in range(count)]


def far_and_z():
    pairs = [(d, d + 1) for d in range(1, 15, 2)] + [(15, 0)]
    return [[d * 16 + 4 * y + z for d in pair for z in range(4)] for pair in pairs for y in range(4)]


def inner(axis):
    i = lax.axis_index(axis)
    return (i > 0) & (i < 15)


def spread(line, col):
    left = jnp.where(col == 0, 0.0, pltpu.roll(line[:, :128], 1, 0))
    right = jnp.where(col == 127, 0.0, pltpu.roll(line[:, 256:], 127, 0))
    return line[:, 128:256] + left + right


def fine_kernel(vol, x2, x1, r2, r1, w, bias, ends, best, corner_w, cells):
    pd = lax.rem(lax.axis_index("depth"), 2)
    pr = lax.rem(lax.axis_index("rows"), 2)
    inner_d = inner("depth")
    inner_r = inner("rows")
    zero = jnp.zeros((128, 128), BF16)
    for j in range(4):
        for i in range(6):
            row = (i - 1) + pr * (5 - 2 * i)
            if j in (1, 2):
                plane = (j - 1) + pd * (3 - 2 * j)
                piece = r2[plane] if i == 0 else r1[plane] if i == 5 else vol[plane, row]
            elif i in (0, 5):
                piece = zero
            else:
                piece = (x2 if j == 0 else x1)[row]
            if i == 0:
                piece = jnp.where(inner_r, piece, zero)
            if j == 0:
                piece = jnp.where(inner_d, piece, zero)
            cells[j, i] = piece
    taps = [(a, b) for a in range(3) for b in range(3)]
    groups = [taps[i : i + 2] for i in range(0, 9, 2)]
    col = lax.broadcasted_iota(jnp.int32, (128, 128), 0)
    for s in range(2):
        total = None
        for group in groups:
            lhs = jnp.concatenate(
                [cells[s + a, b : b + 4].reshape(512, 128) for a, b in group], axis=1
            )
            rhs = jnp.concatenate(
                [
                    jnp.concatenate(
                        [w[a + pd * (2 - 2 * a), b + pr * (2 - 2 * b), c] for c in range(3)], axis=1
                    )
                    for a, b in group
                ],
                axis=0,
            )
            term = jnp.dot(lhs, rhs, preferred_element_type=F32)
            total = term if total is None else total + term
        for q in range(2):
            ends[s, q] = spread(total[3 * q * 128 : (3 * q + 1) * 128], col) + bias[...]
            middle = spread(total[(q + 1) * 128 : (q + 2) * 128], col) + bias[...]
            best[q] = middle if s == 0 else jnp.maximum(best[q], middle)
            a, b = 2 * s, 2 * q
            for c in range(3):
                corner_w[s, q, :, 128 * c : 128 * c + 128] = w[a + pd * (2 - 2 * a), b + pr * (2 - 2 * b), c]


def fine_level(vol, x2, x1, r2, r1, w, bias):
    vmem = pl.BlockSpec(memory_space=pltpu.VMEM)
    return pl.pallas_call(
        fine_kernel,
        out_shape=[
            jax.ShapeDtypeStruct((2, 2, 128, 128), F32),
            jax.ShapeDtypeStruct((2, 128, 128), F32),
            jax.ShapeDtypeStruct((2, 2, 128, 384), BF16),
        ],
        in_specs=[vmem] * 7,
        out_specs=[vmem] * 3,
        scratch_shapes=[pltpu.VMEM((4, 6, 128, 128), BF16)],
        compiler_params=pltpu.CompilerParams(vmem_limit_bytes=32 * 1024 * 1024),
        cost_estimate=pl.CostEstimate(flops=20_000_000_000, bytes_accessed=0, transcendentals=0),
    )(vol, x2, x1, r2, r1, w, bias)


def finish_kernel(ends, best, corner_w, c2, c1, other, out, peak):
    pr = lax.rem(lax.axis_index("rows"), 2)
    inner_d = inner("depth")
    inner_r = inner("rows")
    zero = jnp.zeros((128, 128), BF16)
    col = lax.broadcasted_iota(jnp.int32, (128, 128), 0)
    for q in range(2):
        value = best[q]
        for s in range(2):
            piece = (c2, c1)[q][s]
            if q == 0:
                piece = jnp.where(inner_r, piece, zero)
            if s == 0:
                piece = jnp.where(inner_d, piece, zero)
            corner = jnp.dot(piece, corner_w[s, q], preferred_element_type=F32)
            value = jnp.maximum(value, ends[s, q] + spread(corner, col))
        peak[...] = value
        pooled = jnp.maximum(peak[pl.ds(0, 64, stride=2), :], peak[pl.ds(1, 64, stride=2), :])
        pooled = jnp.maximum(pooled, 0.0).astype(BF16)
        for k in range(8):
            out[k, q + pr * (1 - 2 * q)] = pooled


def finish(main, c2, c1, other):
    vmem = pl.BlockSpec(memory_space=pltpu.VMEM)
    return pl.pallas_call(
        finish_kernel,
        out_shape=jax.ShapeDtypeStruct((8, 2, 64, 128), BF16),
        in_specs=[vmem] * 5 + [pl.BlockSpec(memory_space=pl.ANY)],
        out_specs=vmem,
        scratch_shapes=[pltpu.VMEM((128, 128), F32)],
        compiler_params=pltpu.CompilerParams(vmem_limit_bytes=32 * 1024 * 1024),
    )(*main, c2, c1, other)


def coarse_kernel(both, near, pair, other, out, cells):
    pd = lax.rem(lax.axis_index("depth"), 2)
    y = lax.div(lax.axis_index("rows"), 4)
    inner_d = inner("depth")
    for a in range(3):
        for i in (0, 1, 10, 11):
            cells[a, i] = jnp.zeros((64, 128), BF16)
    for k in range(4):
        far = both[pd, k]
        cells[0, 2 + 2 * k : 4 + 2 * k] = jnp.where(inner_d, far, jnp.zeros_like(far))
        cells[1, 2 + 2 * k : 4 + 2 * k] = both[1 - pd, k]
        cells[2, 2 + 2 * k : 4 + 2 * k] = near[k]
    lhs = jnp.concatenate(
        [
            jnp.concatenate(
                [w[m, 9 * (a + pd * (2 - 2 * a)) + 3 * b + c] for a in range(3) for b in range(3)], axis=1
            )
            for c in range(3)
            for w, m in ((pair, 0), (pair, 1), (other, 0), (other, 1))
        ],
        axis=0,
    )
    for start, size in ((0, 256), (256, 256), (512, 128)):
        if start < 512:
            first = start // 64 + 1
            blocks = [
                cells[a, first + b : first + b + 4].reshape(256, 128) for a in range(3) for b in range(3)
            ]
        else:
            blocks = [
                jnp.concatenate([cells[a, 9 + b], cells[a, b]], axis=0) for a in range(3) for b in range(3)
            ]
        rhs = jnp.concatenate(blocks, axis=1)
        term = lax.dot_general(lhs, rhs, (((1,), (1,)), ((), ())), preferred_element_type=F32)
        lane = lax.rem(lax.broadcasted_iota(jnp.int32, (64, size), 1), 64)
        left = jnp.where(lane == 0, 0.0, pltpu.roll(term[:64], 1, 1))
        right = jnp.where(lane == 63, 0.0, pltpu.roll(term[128:], size - 1, 1))
        value = term[64:128] + left + right
        for k in range(4):
            out[y ^ k, :, start : start + size] = value[16 * k : 16 * k + 16]


def coarse_level(both, near, pair, other):
    vmem = pl.BlockSpec(memory_space=pltpu.VMEM)
    return pl.pallas_call(
        coarse_kernel,
        out_shape=jax.ShapeDtypeStruct((4, 16, 640), F32),
        in_specs=[vmem] * 4,
        out_specs=vmem,
        scratch_shapes=[pltpu.VMEM((3, 12, 64, 128), BF16)],
        compiler_params=pltpu.CompilerParams(vmem_limit_bytes=32 * 1024 * 1024),
    )(both, near, pair, other)


def join_kernel(held, bias, out):
    low = lax.broadcasted_iota(jnp.int32, (16, 128), 1) < 64
    for m in range(4):
        tiles = [held[m, :, 128 * i : 128 * i + 128] for i in range(4)]
        if m > 0:
            tiles[0] = tiles[0] + jnp.where(low, held[m - 1, :, 512:], 0.0)
        if m < 3:
            tiles[3] = tiles[3] + jnp.where(low, 0.0, held[m + 1, :, 512:])
        for i in range(4):
            value = jnp.maximum(tiles[i] + bias[...], 0.0).astype(BF16)
            out[:, 512 * m + 128 * i : 512 * m + 128 * i + 128] = value


def join(parts, bias):
    vmem = pl.BlockSpec(memory_space=pltpu.VMEM)
    return pl.pallas_call(
        join_kernel,
        out_shape=jax.ShapeDtypeStruct((16, 2048), BF16),
        in_specs=[vmem] * 2,
        out_specs=vmem,
        compiler_params=pltpu.CompilerParams(vmem_limit_bytes=32 * 1024 * 1024),
    )(parts, bias)


def body(volume, fine_filters, fine_bias, coarse_filters, coarse_bias):
    d = lax.axis_index("depth")
    r = lax.axis_index("rows")
    pd = lax.rem(d, 2)
    pr = lax.rem(r, 2)
    depth_near, depth_far = near_pairs(16), far_pairs(16)
    rows_near, rows_far = near_pairs(16), far_pairs(16)

    x2 = lax.ppermute(lax.dynamic_index_in_dim(volume, pd, 0, False), "depth", depth_far)
    x1 = lax.ppermute(lax.dynamic_index_in_dim(volume, 1 - pd, 0, False), "depth", depth_near)
    r2 = lax.ppermute(lax.dynamic_index_in_dim(volume, 3 * pr, 1, False), "rows", rows_far)
    r1 = lax.ppermute(lax.dynamic_index_in_dim(volume, 3 - 3 * pr, 1, False), "rows", rows_near)
    sides = jnp.stack([x2, x1])
    c2 = lax.ppermute(lax.dynamic_index_in_dim(sides, 3 * pr, 1, False), "rows", rows_far)
    c1 = lax.ppermute(lax.dynamic_index_in_dim(sides, 3 - 3 * pr, 1, False), "rows", rows_near)

    def along_y(k):
        return [(i, i ^ (4 * k)) for i in range(16)]

    w = jnp.transpose(coarse_filters, (0, 1, 2, 4, 3)).reshape(27, 16, 128)
    pair = jnp.stack([w, lax.ppermute(w, "rows", along_y(1))])
    other = lax.ppermute(pair, "rows", along_y(2))
    main = fine_level(volume, x2, x1, r2, r1, fine_filters, fine_bias.reshape(1, 128))
    pooled = finish(main, c2, c1, other)

    both = lax.all_to_all(
        pooled, ("depth", "rows"), 0, 0, axis_index_groups=far_and_z(), tiled=True
    ).reshape(2, 4, 2, 64, 128)
    near = lax.ppermute(lax.dynamic_index_in_dim(both, 1 - pd, 0, False), "depth", depth_near)
    sums = coarse_level(both, near, pair, other)
    parts = lax.all_to_all(
        sums, "rows", 0, 0, axis_index_groups=[[4 * y + z for y in range(4)] for z in range(4)], tiled=True
    )
    result = join(parts, jnp.broadcast_to(coarse_bias[:, None], (16, 128)))
    return result.reshape(16, 1, 2048)


def solution(mesh):
    placed = (
        P("depth", "rows", None, None),
        P(),
        P(),
        P(None, None, None, None, "rows"),
        P("rows"),
    )
    return jax.shard_map(
        body, mesh=mesh, in_specs=placed, out_specs=P("rows", "depth", None), check_vma=False
    )
```

```python
import jax
import jax.numpy as jnp
from jax import lax
from jax.experimental import pallas as pl
from jax.experimental.pallas import tpu as pltpu
from jax.sharding import PartitionSpec as P

BF16 = jnp.bfloat16
F32 = jnp.float32


def near_pairs(count):
    return [(i, i ^ 1) for i in range(count)]


def far_pairs(count):
    return [(i, min(max(((i - 1) ^ 1) + 1, 0), count - 1)) for i in range(count)]


def far_and_z():
    pairs = [(d, d + 1) for d in range(1, 15, 2)] + [(15, 0)]
    return [[d * 16 + 4 * y + z for d in pair for z in range(4)] for pair in pairs for y in range(4)]


def inner(axis):
    i = lax.axis_index(axis)
    return (i > 0) & (i < 15)


def spread(line, col):
    left = jnp.where(col == 0, 0.0, pltpu.roll(line[:, :128], 1, 0))
    right = jnp.where(col == 127, 0.0, pltpu.roll(line[:, 256:], 127, 0))
    return line[:, 128:256] + left + right


def fine_kernel(vol, x2, x1, w, bias, ends, best, edge_w, cells):
    pd = lax.rem(lax.axis_index("depth"), 2)
    pr = lax.rem(lax.axis_index("rows"), 2)
    inner_d = inner("depth")
    zero = jnp.zeros((128, 128), BF16)
    for j in range(4):
        for i in range(6):
            row = (i - 1) + pr * (5 - 2 * i)
            if i in (0, 5):
                piece = zero
            elif j == 0:
                piece = jnp.where(inner_d, x2[row], zero)
            elif j == 3:
                piece = x1[row]
            else:
                piece = vol[(j - 1) + pd * (3 - 2 * j), row]
            cells[j, i] = piece
    taps = [(a, b) for a in range(3) for b in range(3)]
    groups = [taps[i : i + 2] for i in range(0, 9, 2)]
    col = lax.broadcasted_iota(jnp.int32, (128, 128), 0)
    for s in range(2):
        total = None
        for group in groups:
            lhs = jnp.concatenate(
                [cells[s + a, b : b + 4].reshape(512, 128) for a, b in group], axis=1
            )
            rhs = jnp.concatenate(
                [
                    jnp.concatenate(
                        [w[a + pd * (2 - 2 * a), b + pr * (2 - 2 * b), c] for c in range(3)], axis=1
                    )
                    for a, b in group
                ],
                axis=0,
            )
            term = jnp.dot(lhs, rhs, preferred_element_type=F32)
            total = term if total is None else total + term
        for q in range(2):
            ends[s, q] = spread(total[3 * q * 128 : (3 * q + 1) * 128], col) + bias[...]
            middle = spread(total[(q + 1) * 128 : (q + 2) * 128], col) + bias[...]
            best[q] = middle if s == 0 else jnp.maximum(best[q], middle)
    for q in range(2):
        b = 2 * q
        for a in range(3):
            for c in range(3):
                edge_w[q, 128 * a : 128 * a + 128, 128 * c : 128 * c + 128] = w[
                    a + pd * (2 - 2 * a), b + pr * (2 - 2 * b), c
                ]


def fine_level(vol, x2, x1, w, bias):
    vmem = pl.BlockSpec(memory_space=pltpu.VMEM)
    return pl.pallas_call(
        fine_kernel,
        out_shape=[
            jax.ShapeDtypeStruct((2, 2, 128, 128), F32),
            jax.ShapeDtypeStruct((2, 128, 128), F32),
            jax.ShapeDtypeStruct((2, 384, 384), BF16),
        ],
        in_specs=[vmem] * 5,
        out_specs=[vmem] * 3,
        scratch_shapes=[pltpu.VMEM((4, 6, 128, 128), BF16)],
        compiler_params=pltpu.CompilerParams(vmem_limit_bytes=32 * 1024 * 1024),
        cost_estimate=pl.CostEstimate(flops=400_000_000_000, bytes_accessed=0, transcendentals=0),
    )(vol, x2, x1, w, bias)


def finish_kernel(ends, best, edge_w, c2, c1, other, out, peak):
    pd = lax.rem(lax.axis_index("depth"), 2)
    pr = lax.rem(lax.axis_index("rows"), 2)
    inner_d = inner("depth")
    inner_r = inner("rows")
    zero = jnp.zeros((128, 128), BF16)
    col = lax.broadcasted_iota(jnp.int32, (128, 128), 0)
    for q in range(2):
        rows = []
        for j in range(4):
            plane = j if j in (0, 3) else j + pd * (3 - 2 * j)
            piece = (c2, c1)[q][plane]
            if q == 0:
                piece = jnp.where(inner_r, piece, zero)
            if j == 0:
                piece = jnp.where(inner_d, piece, zero)
            rows.append(piece)
        lhs = jnp.concatenate([jnp.concatenate(rows[s : s + 3], axis=1) for s in range(2)], axis=0)
        edge = jnp.dot(lhs, edge_w[q], preferred_element_type=F32)
        value = best[q]
        for s in range(2):
            value = jnp.maximum(value, ends[s, q] + spread(edge[128 * s : 128 * s + 128], col))
        peak[...] = value
        pooled = jnp.maximum(peak[pl.ds(0, 64, stride=2), :], peak[pl.ds(1, 64, stride=2), :])
        pooled = jnp.maximum(pooled, 0.0).astype(BF16)
        for k in range(8):
            out[k, q + pr * (1 - 2 * q)] = pooled


def finish(main, c2, c1, other):
    vmem = pl.BlockSpec(memory_space=pltpu.VMEM)
    return pl.pallas_call(
        finish_kernel,
        out_shape=jax.ShapeDtypeStruct((8, 2, 64, 128), BF16),
        in_specs=[vmem] * 5 + [pl.BlockSpec(memory_space=pl.ANY)],
        out_specs=vmem,
        scratch_shapes=[pltpu.VMEM((128, 128), F32)],
        compiler_params=pltpu.CompilerParams(vmem_limit_bytes=32 * 1024 * 1024),
    )(*main, c2, c1, other)


def coarse_sums(cells, taps, pair, other, add):
    lhs = jnp.concatenate(
        [
            jnp.concatenate([w[m, 9 * a + 3 * b + c] for a in taps for b in range(3)], axis=1)
            for c in range(3)
            for w, m in ((pair, 0), (pair, 1), (other, 0), (other, 1))
        ],
        axis=0,
    )
    count = len(taps)
    for start, size in ((0, 256), (256, 256), (512, 128)):
        if start < 512:
            first = start // 64 + 1
            blocks = [
                cells[i, first + b : first + b + 4].reshape(256, 128) for i in range(count) for b in range(3)
            ]
        else:
            blocks = [
                jnp.concatenate([cells[i, 9 + b], cells[i, b]], axis=0) for i in range(count) for b in range(3)
            ]
        rhs = jnp.concatenate(blocks, axis=1)
        term = lax.dot_general(lhs, rhs, (((1,), (1,)), ((), ())), preferred_element_type=F32)
        lane = lax.rem(lax.broadcasted_iota(jnp.int32, (64, size), 1), 64)
        left = jnp.where(lane == 0, 0.0, pltpu.roll(term[:64], 1, 1))
        right = jnp.where(lane == 63, 0.0, pltpu.roll(term[128:], size - 1, 1))
        add(start, size, term[64:128] + left + right)


def coarse_kernel(both, pair, other, out, cells):
    pd = lax.rem(lax.axis_index("depth"), 2)
    inner_d = inner("depth")
    for a in range(2):
        for i in (0, 1, 10, 11):
            cells[a, i] = jnp.zeros((64, 128), BF16)
    for k in range(4):
        far = both[pd, k]
        cells[0, 2 + 2 * k : 4 + 2 * k] = jnp.where(inner_d, far, jnp.zeros_like(far))
        cells[1, 2 + 2 * k : 4 + 2 * k] = both[1 - pd, k]

    def put(start, size, value):
        out[:, start : start + size] = value

    coarse_sums(cells, (2 * pd, 1), pair, other, put)


def coarse_level(both, pair, other):
    vmem = pl.BlockSpec(memory_space=pltpu.VMEM)
    return pl.pallas_call(
        coarse_kernel,
        out_shape=jax.ShapeDtypeStruct((64, 640), F32),
        in_specs=[vmem] * 3,
        out_specs=vmem,
        scratch_shapes=[pltpu.VMEM((2, 12, 64, 128), BF16)],
        compiler_params=pltpu.CompilerParams(vmem_limit_bytes=32 * 1024 * 1024),
        cost_estimate=pl.CostEstimate(flops=1_000_000_000, bytes_accessed=0, transcendentals=0),
    )(both, pair, other)


def near_kernel(near, sums, pair, other, out, cells):
    pd = lax.rem(lax.axis_index("depth"), 2)
    y = lax.div(lax.axis_index("rows"), 4)
    for i in (0, 1, 10, 11):
        cells[0, i] = jnp.zeros((64, 128), BF16)
    for k in range(4):
        cells[0, 2 + 2 * k : 4 + 2 * k] = near[k]

    def put(start, size, value):
        value = value + sums[:, start : start + size]
        for k in range(4):
            out[y ^ k, :, start : start + size] = value[16 * k : 16 * k + 16]

    coarse_sums(cells, (2 - 2 * pd,), pair, other, put)


def near_level(near, sums, pair, other):
    vmem = pl.BlockSpec(memory_space=pltpu.VMEM)
    return pl.pallas_call(
        near_kernel,
        out_shape=jax.ShapeDtypeStruct((4, 16, 640), F32),
        in_specs=[vmem] * 4,
        out_specs=vmem,
        scratch_shapes=[pltpu.VMEM((1, 12, 64, 128), BF16)],
        compiler_params=pltpu.CompilerParams(vmem_limit_bytes=32 * 1024 * 1024),
    )(near, sums, pair, other)


def join_kernel(held, bias, out):
    low = lax.broadcasted_iota(jnp.int32, (16, 128), 1) < 64
    for m in range(4):
        tiles = [held[m, :, 128 * i : 128 * i + 128] for i in range(4)]
        if m > 0:
            tiles[0] = tiles[0] + jnp.where(low, held[m - 1, :, 512:], 0.0)
        if m < 3:
            tiles[3] = tiles[3] + jnp.where(low, 0.0, held[m + 1, :, 512:])
        for i in range(4):
            value = jnp.maximum(tiles[i] + bias[...], 0.0).astype(BF16)
            out[:, 512 * m + 128 * i : 512 * m + 128 * i + 128] = value


def join(parts, bias):
    vmem = pl.BlockSpec(memory_space=pltpu.VMEM)
    return pl.pallas_call(
        join_kernel,
        out_shape=jax.ShapeDtypeStruct((16, 2048), BF16),
        in_specs=[vmem] * 2,
        out_specs=vmem,
        compiler_params=pltpu.CompilerParams(vmem_limit_bytes=32 * 1024 * 1024),
    )(parts, bias)


def body(volume, fine_filters, fine_bias, coarse_filters, coarse_bias):
    d = lax.axis_index("depth")
    r = lax.axis_index("rows")
    pd = lax.rem(d, 2)
    pr = lax.rem(r, 2)
    depth_near, depth_far = near_pairs(16), far_pairs(16)
    rows_near, rows_far = near_pairs(16), far_pairs(16)

    far_plane = lax.dynamic_index_in_dim(volume, pd, 0, False)
    x2 = lax.ppermute(far_plane, "depth", depth_far)
    x1 = lax.ppermute(lax.dynamic_index_in_dim(volume, 1 - pd, 0, False), "depth", depth_near)
    def row_of(k):
        return jnp.stack(
            [lax.dynamic_index_in_dim(p, k, 0, False) for p in (x2, volume[0], volume[1], x1)]
        )

    c2 = lax.ppermute(row_of(3 * pr), "rows", rows_far)
    c1 = lax.ppermute(row_of(3 - 3 * pr), "rows", rows_near)

    def along_y(k):
        return [(i, i ^ (4 * k)) for i in range(16)]

    w = jnp.transpose(coarse_filters, (0, 1, 2, 4, 3)).reshape(27, 16, 128)
    w = w + far_plane[0, 0, 0] * jnp.bfloat16(0)
    pair = jnp.stack([w, lax.ppermute(w, "rows", along_y(1))])
    other = lax.ppermute(pair, "rows", along_y(2))
    main = fine_level(volume, x2, x1, fine_filters, fine_bias.reshape(1, 128))
    pooled = finish(main, c2, c1, other)

    both = lax.all_to_all(
        pooled, ("depth", "rows"), 0, 0, axis_index_groups=far_and_z(), tiled=True
    ).reshape(2, 4, 2, 64, 128)
    near = lax.ppermute(lax.dynamic_index_in_dim(both, 1 - pd, 0, False), "depth", depth_near)
    sums = near_level(near, coarse_level(both, pair, other), pair, other)
    parts = lax.all_to_all(
        sums, "rows", 0, 0, axis_index_groups=[[4 * y + z for y in range(4)] for z in range(4)], tiled=True
    )
    result = join(parts, jnp.broadcast_to(coarse_bias[:, None], (16, 128)))
    return result.reshape(16, 1, 2048)


def solution(mesh):
    placed = (
        P("depth", "rows", None, None),
        P(),
        P(),
        P(None, None, None, None, "rows"),
        P("rows"),
    )
    return jax.shard_map(
        body, mesh=mesh, in_specs=placed, out_specs=P("rows", "depth", None), check_vma=False
    )
```

```python
import jax
import jax.numpy as jnp
from jax import lax
from jax.experimental import pallas as pl
from jax.experimental.pallas import tpu as pltpu
from jax.sharding import PartitionSpec as P

BF16 = jnp.bfloat16
F32 = jnp.float32


def near_pairs(count):
    return [(i, i ^ 1) for i in range(count)]


def far_pairs(count):
    return [(i, min(max(((i - 1) ^ 1) + 1, 0), count - 1)) for i in range(count)]


def far_and_z():
    pairs = [(d, d + 1) for d in range(1, 15, 2)] + [(15, 0)]
    return [[d * 16 + 4 * y + z for d in pair for z in range(4)] for pair in pairs for y in range(4)]


def inner(axis):
    i = lax.axis_index(axis)
    return (i > 0) & (i < 15)


def spread(line, col):
    left = jnp.where(col == 0, 0.0, pltpu.roll(line[:, :128], 1, 0))
    right = jnp.where(col == 127, 0.0, pltpu.roll(line[:, 256:], 127, 0))
    return line[:, 128:256] + left + right


def fine_kernel(vol, x2, x1, r2, r1, w, bias, ends, best, corner_w, cells):
    pd = lax.rem(lax.axis_index("depth"), 2)
    pr = lax.rem(lax.axis_index("rows"), 2)
    inner_d = inner("depth")
    inner_r = inner("rows")
    zero = jnp.zeros((128, 128), BF16)
    for j in range(4):
        for i in range(6):
            row = (i - 1) + pr * (5 - 2 * i)
            if j in (1, 2):
                plane = (j - 1) + pd * (3 - 2 * j)
                piece = r2[plane] if i == 0 else r1[plane] if i == 5 else vol[plane, row]
            elif i in (0, 5):
                piece = zero
            else:
                piece = (x2 if j == 0 else x1)[row]
            if i == 0:
                piece = jnp.where(inner_r, piece, zero)
            if j == 0:
                piece = jnp.where(inner_d, piece, zero)
            cells[j, i] = piece
    taps = [(a, b) for a in range(3) for b in range(3)]
    groups = [taps[i : i + 2] for i in range(0, 9, 2)]
    col = lax.broadcasted_iota(jnp.int32, (128, 128), 0)
    for s in range(2):
        total = None
        for group in groups:
            lhs = jnp.concatenate(
                [cells[s + a, b : b + 4].reshape(512, 128) for a, b in group], axis=1
            )
            rhs = jnp.concatenate(
                [
                    jnp.concatenate(
                        [w[a + pd * (2 - 2 * a), b + pr * (2 - 2 * b), c] for c in range(3)], axis=1
                    )
                    for a, b in group
                ],
                axis=0,
            )
            term = jnp.dot(lhs, rhs, preferred_element_type=F32)
            total = term if total is None else total + term
        for q in range(2):
            ends[s, q] = spread(total[3 * q * 128 : (3 * q + 1) * 128], col) + bias[...]
            middle = spread(total[(q + 1) * 128 : (q + 2) * 128], col) + bias[...]
            best[q] = middle if s == 0 else jnp.maximum(best[q], middle)
            a, b = 2 * s, 2 * q
            for c in range(3):
                corner_w[s, q, :, 128 * c : 128 * c + 128] = w[a + pd * (2 - 2 * a), b + pr * (2 - 2 * b), c]


def fine_level(vol, x2, x1, r2, r1, w, bias):
    vmem = pl.BlockSpec(memory_space=pltpu.VMEM)
    return pl.pallas_call(
        fine_kernel,
        out_shape=[
            jax.ShapeDtypeStruct((2, 2, 128, 128), F32),
            jax.ShapeDtypeStruct((2, 128, 128), F32),
            jax.ShapeDtypeStruct((2, 2, 128, 384), BF16),
        ],
        in_specs=[vmem] * 7,
        out_specs=[vmem] * 3,
        scratch_shapes=[pltpu.VMEM((4, 6, 128, 128), BF16)],
        compiler_params=pltpu.CompilerParams(vmem_limit_bytes=12 * 1024 * 1024),
        cost_estimate=pl.CostEstimate(flops=20_000_000_000, bytes_accessed=0, transcendentals=0),
    )(vol, x2, x1, r2, r1, w, bias)


def finish_kernel(ends, best, corner_w, c2, c1, other, out, peak):
    pr = lax.rem(lax.axis_index("rows"), 2)
    inner_d = inner("depth")
    inner_r = inner("rows")
    zero = jnp.zeros((128, 128), BF16)
    col = lax.broadcasted_iota(jnp.int32, (128, 128), 0)
    for q in range(2):
        value = best[q]
        for s in range(2):
            piece = (c2, c1)[q][s]
            if q == 0:
                piece = jnp.where(inner_r, piece, zero)
            if s == 0:
                piece = jnp.where(inner_d, piece, zero)
            corner = jnp.dot(piece, corner_w[s, q], preferred_element_type=F32)
            value = jnp.maximum(value, ends[s, q] + spread(corner, col))
        peak[...] = value
        pooled = jnp.maximum(peak[pl.ds(0, 64, stride=2), :], peak[pl.ds(1, 64, stride=2), :])
        pooled = jnp.maximum(pooled, 0.0).astype(BF16)
        for k in range(8):
            out[k, q + pr * (1 - 2 * q)] = pooled


def finish(main, c2, c1, other):
    vmem = pl.BlockSpec(memory_space=pltpu.VMEM)
    return pl.pallas_call(
        finish_kernel,
        out_shape=jax.ShapeDtypeStruct((8, 2, 64, 128), BF16),
        in_specs=[vmem] * 5 + [pl.BlockSpec(memory_space=pl.ANY)],
        out_specs=vmem,
        scratch_shapes=[pltpu.VMEM((128, 128), F32)],
        compiler_params=pltpu.CompilerParams(vmem_limit_bytes=6 * 1024 * 1024),
    )(*main, c2, c1, other)


def coarse_kernel(both, near, pair, other, out, cells):
    pd = lax.rem(lax.axis_index("depth"), 2)
    y = lax.div(lax.axis_index("rows"), 4)
    inner_d = inner("depth")
    for a in range(3):
        for i in (0, 1, 10, 11):
            cells[a, i] = jnp.zeros((64, 128), BF16)
    for k in range(4):
        far = both[pd, k]
        cells[0, 2 + 2 * k : 4 + 2 * k] = jnp.where(inner_d, far, jnp.zeros_like(far))
        cells[1, 2 + 2 * k : 4 + 2 * k] = both[1 - pd, k]
        cells[2, 2 + 2 * k : 4 + 2 * k] = near[k]
    lhs = jnp.concatenate(
        [
            jnp.concatenate(
                [w[m, 9 * (a + pd * (2 - 2 * a)) + 3 * b + c] for a in range(3) for b in range(3)], axis=1
            )
            for c in range(3)
            for w, m in ((pair, 0), (pair, 1), (other, 1), (other, 0))
        ],
        axis=0,
    )
    for start, size in ((0, 256), (256, 256), (512, 128)):
        if start < 512:
            first = start // 64 + 1
            blocks = [
                cells[a, first + b : first + b + 4].reshape(256, 128) for a in range(3) for b in range(3)
            ]
        else:
            blocks = [
                jnp.concatenate([cells[a, 9 + b], cells[a, b]], axis=0) for a in range(3) for b in range(3)
            ]
        rhs = jnp.concatenate(blocks, axis=1)
        term = lax.dot_general(lhs, rhs, (((1,), (1,)), ((), ())), preferred_element_type=F32)
        lane = lax.rem(lax.broadcasted_iota(jnp.int32, (64, size), 1), 64)
        left = jnp.where(lane == 0, 0.0, pltpu.roll(term[:64], 1, 1))
        right = jnp.where(lane == 63, 0.0, pltpu.roll(term[128:], size - 1, 1))
        value = term[64:128] + left + right
        for k in range(4):
            out[y ^ k, :, start : start + size] = value[16 * k : 16 * k + 16]


def coarse_level(both, near, pair, other):
    vmem = pl.BlockSpec(memory_space=pltpu.VMEM)
    return pl.pallas_call(
        coarse_kernel,
        out_shape=jax.ShapeDtypeStruct((4, 16, 640), F32),
        in_specs=[vmem] * 4,
        out_specs=vmem,
        scratch_shapes=[pltpu.VMEM((3, 12, 64, 128), BF16)],
        compiler_params=pltpu.CompilerParams(vmem_limit_bytes=8 * 1024 * 1024),
    )(both, near, pair, other)


def join_kernel(held, bias, out):
    low = lax.broadcasted_iota(jnp.int32, (16, 128), 1) < 64
    for m in range(4):
        tiles = [held[m, :, 128 * i : 128 * i + 128] for i in range(4)]
        if m > 0:
            tiles[0] = tiles[0] + jnp.where(low, held[m - 1, :, 512:], 0.0)
        if m < 3:
            tiles[3] = tiles[3] + jnp.where(low, 0.0, held[m + 1, :, 512:])
        for i in range(4):
            value = jnp.maximum(tiles[i] + bias[...], 0.0).astype(BF16)
            out[:, 512 * m + 128 * i : 512 * m + 128 * i + 128] = value


def join(parts, bias):
    vmem = pl.BlockSpec(memory_space=pltpu.VMEM)
    return pl.pallas_call(
        join_kernel,
        out_shape=jax.ShapeDtypeStruct((16, 2048), BF16),
        in_specs=[vmem] * 2,
        out_specs=vmem,
        compiler_params=pltpu.CompilerParams(vmem_limit_bytes=4 * 1024 * 1024),
    )(parts, bias)


def body(volume, fine_filters, fine_bias, coarse_filters, coarse_bias):
    d = lax.axis_index("depth")
    r = lax.axis_index("rows")
    pd = lax.rem(d, 2)
    pr = lax.rem(r, 2)
    depth_near, depth_far = near_pairs(16), far_pairs(16)
    rows_near, rows_far = near_pairs(16), far_pairs(16)

    x2 = lax.ppermute(lax.dynamic_index_in_dim(volume, pd, 0, False), "depth", depth_far)
    x1 = lax.ppermute(lax.dynamic_index_in_dim(volume, 1 - pd, 0, False), "depth", depth_near)
    r2 = lax.ppermute(lax.dynamic_index_in_dim(volume, 3 * pr, 1, False), "rows", rows_far)
    r1 = lax.ppermute(lax.dynamic_index_in_dim(volume, 3 - 3 * pr, 1, False), "rows", rows_near)
    sides = jnp.stack([x2, x1])
    c2 = lax.ppermute(lax.dynamic_index_in_dim(sides, 3 * pr, 1, False), "rows", rows_far)
    c1 = lax.ppermute(lax.dynamic_index_in_dim(sides, 3 - 3 * pr, 1, False), "rows", rows_near)

    def along_y(k):
        return [(i, i ^ (4 * k)) for i in range(16)]

    w = jnp.transpose(coarse_filters, (0, 1, 2, 4, 3)).reshape(27, 16, 128)
    pair = jnp.stack([w, lax.ppermute(w, "rows", along_y(1))])
    other = lax.ppermute(pair, "rows", along_y(3))
    main = fine_level(volume, x2, x1, r2, r1, fine_filters, fine_bias.reshape(1, 128))
    pooled = finish(main, c2, c1, other)

    both = lax.all_to_all(
        pooled, ("depth", "rows"), 0, 0, axis_index_groups=far_and_z(), tiled=True
    ).reshape(2, 4, 2, 64, 128)
    near = lax.ppermute(lax.dynamic_index_in_dim(both, 1 - pd, 0, False), "depth", depth_near)
    sums = coarse_level(both, near, pair, other)
    parts = lax.all_to_all(
        sums, "rows", 0, 0, axis_index_groups=[[4 * y + z for y in range(4)] for z in range(4)], tiled=True
    )
    result = join(parts, jnp.broadcast_to(coarse_bias[:, None], (16, 128)))
    return result.reshape(16, 1, 2048)


def solution(mesh):
    placed = (
        P("depth", "rows", None, None),
        P(),
        P(),
        P(None, None, None, None, "rows"),
        P("rows"),
    )
    return jax.shard_map(
        body, mesh=mesh, in_specs=placed, out_specs=P("rows", "depth", None), check_vma=False
    )
```

```python
import jax
import jax.numpy as jnp
from jax import lax
from jax.experimental import pallas as pl
from jax.experimental.pallas import tpu as pltpu
from jax.sharding import PartitionSpec as P

BF16 = jnp.bfloat16
F32 = jnp.float32


def near_pairs(count):
    return [(i, i ^ 1) for i in range(count)]


def far_pairs(count):
    return [(i, min(max(((i - 1) ^ 1) + 1, 0), count - 1)) for i in range(count)]


def far_and_z():
    pairs = [(d, d + 1) for d in range(1, 15, 2)] + [(15, 0)]
    return [[d * 16 + 4 * y + z for d in pair for z in range(4)] for pair in pairs for y in range(4)]


def inner(axis):
    i = lax.axis_index(axis)
    return (i > 0) & (i < 15)


def spread(line, col):
    left = jnp.where(col == 0, 0.0, pltpu.roll(line[:, :128], 1, 0))
    right = jnp.where(col == 127, 0.0, pltpu.roll(line[:, 256:], 127, 0))
    return line[:, 128:256] + left + right


def fine_kernel(vol, x2, x1, w, bias, ends, best, edge_w, cells):
    pd = lax.rem(lax.axis_index("depth"), 2)
    pr = lax.rem(lax.axis_index("rows"), 2)
    inner_d = inner("depth")
    zero = jnp.zeros((128, 128), BF16)
    for j in range(4):
        for i in range(6):
            row = (i - 1) + pr * (5 - 2 * i)
            if i in (0, 5):
                piece = zero
            elif j == 0:
                piece = jnp.where(inner_d, x2[row], zero)
            elif j == 3:
                piece = x1[row]
            else:
                piece = vol[(j - 1) + pd * (3 - 2 * j), row]
            cells[j, i] = piece
    taps = [(a, b) for a in range(3) for b in range(3)]
    groups = [taps[i : i + 2] for i in range(0, 9, 2)]
    col = lax.broadcasted_iota(jnp.int32, (128, 128), 0)
    for s in range(2):
        total = None
        for group in groups:
            lhs = jnp.concatenate(
                [cells[s + a, b : b + 4].reshape(512, 128) for a, b in group], axis=1
            )
            rhs = jnp.concatenate(
                [
                    jnp.concatenate(
                        [w[a + pd * (2 - 2 * a), b + pr * (2 - 2 * b), c] for c in range(3)], axis=1
                    )
                    for a, b in group
                ],
                axis=0,
            )
            term = jnp.dot(lhs, rhs, preferred_element_type=F32)
            total = term if total is None else total + term
        for q in range(2):
            ends[s, q] = spread(total[3 * q * 128 : (3 * q + 1) * 128], col) + bias[...]
            middle = spread(total[(q + 1) * 128 : (q + 2) * 128], col) + bias[...]
            best[q] = middle if s == 0 else jnp.maximum(best[q], middle)
    for q in range(2):
        b = 2 * q
        for a in range(3):
            for c in range(3):
                edge_w[q, 128 * a : 128 * a + 128, 128 * c : 128 * c + 128] = w[
                    a + pd * (2 - 2 * a), b + pr * (2 - 2 * b), c
                ]


def fine_level(vol, x2, x1, w, bias):
    vmem = pl.BlockSpec(memory_space=pltpu.VMEM)
    return pl.pallas_call(
        fine_kernel,
        out_shape=[
            jax.ShapeDtypeStruct((2, 2, 128, 128), F32),
            jax.ShapeDtypeStruct((2, 128, 128), F32),
            jax.ShapeDtypeStruct((2, 384, 384), BF16),
        ],
        in_specs=[vmem] * 5,
        out_specs=[vmem] * 3,
        scratch_shapes=[pltpu.VMEM((4, 6, 128, 128), BF16)],
        compiler_params=pltpu.CompilerParams(vmem_limit_bytes=12 * 1024 * 1024),
        cost_estimate=pl.CostEstimate(flops=20_000_000_000, bytes_accessed=0, transcendentals=0),
    )(vol, x2, x1, w, bias)


def finish_kernel(ends, best, edge_w, c1, c2, w2, w1, w3, out, peak):
    pd = lax.rem(lax.axis_index("depth"), 2)
    pr = lax.rem(lax.axis_index("rows"), 2)
    inner_d = inner("depth")
    inner_r = inner("rows")
    zero = jnp.zeros((128, 128), BF16)
    col = lax.broadcasted_iota(jnp.int32, (128, 128), 0)
    for q in range(2):
        rows = []
        for j in range(4):
            plane = j if j in (0, 3) else j + pd * (3 - 2 * j)
            piece = (c2, c1)[q][plane]
            if q == 0:
                piece = jnp.where(inner_r, piece, zero)
            if j == 0:
                piece = jnp.where(inner_d, piece, zero)
            rows.append(piece)
        lhs = jnp.concatenate([jnp.concatenate(rows[s : s + 3], axis=1) for s in range(2)], axis=0)
        edge = jnp.dot(lhs, edge_w[q], preferred_element_type=F32)
        value = best[q]
        for s in range(2):
            value = jnp.maximum(value, ends[s, q] + spread(edge[128 * s : 128 * s + 128], col))
        peak[...] = value
        pooled = jnp.maximum(peak[pl.ds(0, 64, stride=2), :], peak[pl.ds(1, 64, stride=2), :])
        pooled = jnp.maximum(pooled, 0.0).astype(BF16)
        for k in range(8):
            out[k, q + pr * (1 - 2 * q)] = pooled


def finish(main, c2, c1, weights):
    vmem = pl.BlockSpec(memory_space=pltpu.VMEM)
    return pl.pallas_call(
        finish_kernel,
        out_shape=jax.ShapeDtypeStruct((8, 2, 64, 128), BF16),
        in_specs=[vmem] * 5 + [pl.BlockSpec(memory_space=pl.ANY)] * 3,
        out_specs=vmem,
        scratch_shapes=[pltpu.VMEM((128, 128), F32)],
        compiler_params=pltpu.CompilerParams(vmem_limit_bytes=6 * 1024 * 1024),
    )(*main, c1, c2, *weights)


def coarse_kernel(both, near, w0, w1, w2, w3, out, cells):
    pd = lax.rem(lax.axis_index("depth"), 2)
    y = lax.div(lax.axis_index("rows"), 4)
    inner_d = inner("depth")
    for a in range(3):
        for i in (0, 1, 10, 11):
            cells[a, i] = jnp.zeros((64, 128), BF16)
    for k in range(4):
        far = both[pd, k]
        cells[0, 2 + 2 * k : 4 + 2 * k] = jnp.where(inner_d, far, jnp.zeros_like(far))
        cells[1, 2 + 2 * k : 4 + 2 * k] = both[1 - pd, k]
        cells[2, 2 + 2 * k : 4 + 2 * k] = near[k]
    lhs = jnp.concatenate(
        [
            jnp.concatenate(
                [w[9 * (a + pd * (2 - 2 * a)) + 3 * b + c] for a in range(3) for b in range(3)], axis=1
            )
            for c in range(3)
            for w in (w0, w1, w2, w3)
        ],
        axis=0,
    )
    for start, size in ((0, 256), (256, 256), (512, 128)):
        if start < 512:
            first = start // 64 + 1
            blocks = [
                cells[a, first + b : first + b + 4].reshape(256, 128) for a in range(3) for b in range(3)
            ]
        else:
            blocks = [
                jnp.concatenate([cells[a, 9 + b], cells[a, b]], axis=0) for a in range(3) for b in range(3)
            ]
        rhs = jnp.concatenate(blocks, axis=1)
        term = lax.dot_general(lhs, rhs, (((1,), (1,)), ((), ())), preferred_element_type=F32)
        lane = lax.rem(lax.broadcasted_iota(jnp.int32, (64, size), 1), 64)
        left = jnp.where(lane == 0, 0.0, pltpu.roll(term[:64], 1, 1))
        right = jnp.where(lane == 63, 0.0, pltpu.roll(term[128:], size - 1, 1))
        value = term[64:128] + left + right
        for k in range(4):
            out[y ^ k, :, start : start + size] = value[16 * k : 16 * k + 16]


def coarse_level(both, near, weights):
    vmem = pl.BlockSpec(memory_space=pltpu.VMEM)
    return pl.pallas_call(
        coarse_kernel,
        out_shape=jax.ShapeDtypeStruct((4, 16, 640), F32),
        in_specs=[vmem] * 6,
        out_specs=vmem,
        scratch_shapes=[pltpu.VMEM((3, 12, 64, 128), BF16)],
        compiler_params=pltpu.CompilerParams(vmem_limit_bytes=8 * 1024 * 1024),
    )(both, near, *weights)


def join_kernel(held, bias, out):
    low = lax.broadcasted_iota(jnp.int32, (16, 128), 1) < 64
    for m in range(4):
        tiles = [held[m, :, 128 * i : 128 * i + 128] for i in range(4)]
        if m > 0:
            tiles[0] = tiles[0] + jnp.where(low, held[m - 1, :, 512:], 0.0)
        if m < 3:
            tiles[3] = tiles[3] + jnp.where(low, 0.0, held[m + 1, :, 512:])
        for i in range(4):
            value = jnp.maximum(tiles[i] + bias[...], 0.0).astype(BF16)
            out[:, 512 * m + 128 * i : 512 * m + 128 * i + 128] = value


def join(parts, bias):
    vmem = pl.BlockSpec(memory_space=pltpu.VMEM)
    return pl.pallas_call(
        join_kernel,
        out_shape=jax.ShapeDtypeStruct((16, 2048), BF16),
        in_specs=[vmem] * 2,
        out_specs=vmem,
        compiler_params=pltpu.CompilerParams(vmem_limit_bytes=4 * 1024 * 1024),
    )(parts, bias)


def body(volume, fine_filters, fine_bias, coarse_filters, coarse_bias):
    d = lax.axis_index("depth")
    r = lax.axis_index("rows")
    pd = lax.rem(d, 2)
    pr = lax.rem(r, 2)
    depth_near, depth_far = near_pairs(16), far_pairs(16)
    rows_near, rows_far = near_pairs(16), far_pairs(16)

    far_plane = lax.dynamic_index_in_dim(volume, pd, 0, False)
    x2 = lax.ppermute(far_plane, "depth", depth_far)
    x1 = lax.ppermute(lax.dynamic_index_in_dim(volume, 1 - pd, 0, False), "depth", depth_near)

    def row_of(k):
        return jnp.stack(
            [lax.dynamic_index_in_dim(p, k, 0, False) for p in (x2, volume[0], volume[1], x1)]
        )

    c2 = lax.ppermute(row_of(3 * pr), "rows", rows_far)
    c1 = lax.ppermute(row_of(3 - 3 * pr), "rows", rows_near)

    def along_y(k):
        return [(i, i ^ (4 * k)) for i in range(16)]

    w = jnp.transpose(coarse_filters, (0, 1, 2, 4, 3)).reshape(27, 16, 128)
    w2, w1, w3 = [lax.ppermute(w, "rows", along_y(k)) for k in (2, 1, 3)]
    main = fine_level(volume, x2, x1, fine_filters, fine_bias.reshape(1, 128))
    pooled = finish(main, c2, c1, (w2, w1, w3))

    both = lax.all_to_all(
        pooled, ("depth", "rows"), 0, 0, axis_index_groups=far_and_z(), tiled=True
    ).reshape(2, 4, 2, 64, 128)
    near = lax.ppermute(lax.dynamic_index_in_dim(both, 1 - pd, 0, False), "depth", depth_near)
    sums = coarse_level(both, near, (w, w1, w2, w3))
    parts = lax.all_to_all(
        sums, "rows", 0, 0, axis_index_groups=[[4 * y + z for y in range(4)] for z in range(4)], tiled=True
    )
    result = join(parts, jnp.broadcast_to(coarse_bias[:, None], (16, 128)))
    return result.reshape(16, 1, 2048)


def solution(mesh):
    placed = (
        P("depth", "rows", None, None),
        P(),
        P(),
        P(None, None, None, None, "rows"),
        P("rows"),
    )
    return jax.shard_map(
        body, mesh=mesh, in_specs=placed, out_specs=P("rows", "depth", None), check_vma=False
    )
```

```python
import jax
import jax.numpy as jnp
from jax import lax
from jax.experimental import pallas as pl
from jax.experimental.pallas import tpu as pltpu
from jax.sharding import PartitionSpec as P

BF16 = jnp.bfloat16
F32 = jnp.float32


def near_pairs(count):
    return [(i, i ^ 1) for i in range(count)]


def far_pairs(count):
    return [(i, min(max(((i - 1) ^ 1) + 1, 0), count - 1)) for i in range(count)]


def far_and_z():
    pairs = [(d, d + 1) for d in range(1, 15, 2)] + [(15, 0)]
    return [[d * 16 + 4 * y + z for d in pair for z in range(4)] for pair in pairs for y in range(4)]


def inner(axis):
    i = lax.axis_index(axis)
    return (i > 0) & (i < 15)


def spread(line, col):
    left = jnp.where(col == 0, 0.0, pltpu.roll(line[:, :128], 1, 0))
    right = jnp.where(col == 127, 0.0, pltpu.roll(line[:, 256:], 127, 0))
    return line[:, 128:256] + left + right


def fine_kernel(vol, x2, x1, r2, r1, w, bias, ends, best, corner_w, cells):
    pd = lax.rem(lax.axis_index("depth"), 2)
    pr = lax.rem(lax.axis_index("rows"), 2)
    inner_d = inner("depth")
    inner_r = inner("rows")
    zero = jnp.zeros((128, 128), BF16)
    for j in range(4):
        for i in range(6):
            row = (i - 1) + pr * (5 - 2 * i)
            if j in (1, 2):
                plane = (j - 1) + pd * (3 - 2 * j)
                piece = r2[plane] if i == 0 else r1[plane] if i == 5 else vol[plane, row]
            elif i in (0, 5):
                piece = zero
            else:
                piece = (x2 if j == 0 else x1)[row]
            if i == 0:
                piece = jnp.where(inner_r, piece, zero)
            if j == 0:
                piece = jnp.where(inner_d, piece, zero)
            cells[j, i] = piece
    taps = [(a, b) for a in range(3) for b in range(3)]
    groups = [taps[i : i + 2] for i in range(0, 9, 2)]
    col = lax.broadcasted_iota(jnp.int32, (128, 128), 0)
    for s in range(2):
        total = None
        for group in groups:
            lhs = jnp.concatenate(
                [cells[s + a, b : b + 4].reshape(512, 128) for a, b in group], axis=1
            )
            rhs = jnp.concatenate(
                [
                    jnp.concatenate(
                        [w[a + pd * (2 - 2 * a), b + pr * (2 - 2 * b), c] for c in range(3)], axis=1
                    )
                    for a, b in group
                ],
                axis=0,
            )
            term = jnp.dot(lhs, rhs, preferred_element_type=F32)
            total = term if total is None else total + term
        for q in range(2):
            ends[s, q] = spread(total[3 * q * 128 : (3 * q + 1) * 128], col) + bias[...]
            middle = spread(total[(q + 1) * 128 : (q + 2) * 128], col) + bias[...]
            best[q] = middle if s == 0 else jnp.maximum(best[q], middle)
            a, b = 2 * s, 2 * q
            for c in range(3):
                corner_w[s, q, :, 128 * c : 128 * c + 128] = w[a + pd * (2 - 2 * a), b + pr * (2 - 2 * b), c]


def fine_level(vol, x2, x1, r2, r1, w, bias):
    vmem = pl.BlockSpec(memory_space=pltpu.VMEM)
    return pl.pallas_call(
        fine_kernel,
        out_shape=[
            jax.ShapeDtypeStruct((2, 2, 128, 128), F32),
            jax.ShapeDtypeStruct((2, 128, 128), F32),
            jax.ShapeDtypeStruct((2, 2, 128, 384), BF16),
        ],
        in_specs=[vmem] * 7,
        out_specs=[vmem] * 3,
        scratch_shapes=[pltpu.VMEM((4, 6, 128, 128), BF16)],
        compiler_params=pltpu.CompilerParams(vmem_limit_bytes=12 * 1024 * 1024),
        cost_estimate=pl.CostEstimate(flops=20_000_000_000, bytes_accessed=0, transcendentals=0),
    )(vol, x2, x1, r2, r1, w, bias)


def finish_kernel(ends, best, corner_w, c2, c1, other, out, peak):
    pr = lax.rem(lax.axis_index("rows"), 2)
    inner_d = inner("depth")
    inner_r = inner("rows")
    zero = jnp.zeros((128, 128), BF16)
    col = lax.broadcasted_iota(jnp.int32, (128, 128), 0)
    for q in range(2):
        value = best[q]
        for s in range(2):
            piece = (c2, c1)[q][s]
            if q == 0:
                piece = jnp.where(inner_r, piece, zero)
            if s == 0:
                piece = jnp.where(inner_d, piece, zero)
            corner = jnp.dot(piece, corner_w[s, q], preferred_element_type=F32)
            value = jnp.maximum(value, ends[s, q] + spread(corner, col))
        peak[...] = value
        pooled = jnp.maximum(peak[pl.ds(0, 64, stride=2), :], peak[pl.ds(1, 64, stride=2), :])
        pooled = jnp.maximum(pooled, 0.0).astype(BF16)
        for k in range(8):
            out[k, q + pr * (1 - 2 * q)] = pooled


def finish(main, c2, c1, other):
    vmem = pl.BlockSpec(memory_space=pltpu.VMEM)
    return pl.pallas_call(
        finish_kernel,
        out_shape=jax.ShapeDtypeStruct((8, 2, 64, 128), BF16),
        in_specs=[vmem] * 5 + [pl.BlockSpec(memory_space=pl.ANY)],
        out_specs=vmem,
        scratch_shapes=[pltpu.VMEM((128, 128), F32)],
        compiler_params=pltpu.CompilerParams(vmem_limit_bytes=6 * 1024 * 1024),
    )(*main, c2, c1, other)


def coarse_sums(cells, taps, pair, other, add):
    lhs = jnp.concatenate(
        [
            jnp.concatenate([w[m, 9 * a + 3 * b + c] for a in taps for b in range(3)], axis=1)
            for c in range(3)
            for w, m in ((pair, 0), (pair, 1), (other, 1), (other, 0))
        ],
        axis=0,
    )
    count = len(taps)
    for start, size in ((0, 256), (256, 256), (512, 128)):
        if start < 512:
            first = start // 64 + 1
            blocks = [
                cells[i, first + b : first + b + 4].reshape(256, 128) for i in range(count) for b in range(3)
            ]
        else:
            blocks = [
                jnp.concatenate([cells[i, 9 + b], cells[i, b]], axis=0) for i in range(count) for b in range(3)
            ]
        rhs = jnp.concatenate(blocks, axis=1)
        term = lax.dot_general(lhs, rhs, (((1,), (1,)), ((), ())), preferred_element_type=F32)
        lane = lax.rem(lax.broadcasted_iota(jnp.int32, (64, size), 1), 64)
        left = jnp.where(lane == 0, 0.0, pltpu.roll(term[:64], 1, 1))
        right = jnp.where(lane == 63, 0.0, pltpu.roll(term[128:], size - 1, 1))
        add(start, size, term[64:128] + left + right)


def coarse_kernel(both, pair, other, out, cells):
    pd = lax.rem(lax.axis_index("depth"), 2)
    inner_d = inner("depth")
    for a in range(2):
        for i in (0, 1, 10, 11):
            cells[a, i] = jnp.zeros((64, 128), BF16)
    for k in range(4):
        far = both[pd, k]
        cells[0, 2 + 2 * k : 4 + 2 * k] = jnp.where(inner_d, far, jnp.zeros_like(far))
        cells[1, 2 + 2 * k : 4 + 2 * k] = both[1 - pd, k]

    def put(start, size, value):
        out[:, start : start + size] = value

    coarse_sums(cells, (2 * pd, 1), pair, other, put)


def coarse_level(both, pair, other):
    vmem = pl.BlockSpec(memory_space=pltpu.VMEM)
    return pl.pallas_call(
        coarse_kernel,
        out_shape=jax.ShapeDtypeStruct((64, 640), F32),
        in_specs=[vmem] * 3,
        out_specs=vmem,
        scratch_shapes=[pltpu.VMEM((2, 12, 64, 128), BF16)],
        compiler_params=pltpu.CompilerParams(vmem_limit_bytes=6 * 1024 * 1024),
        cost_estimate=pl.CostEstimate(flops=150_000_000, bytes_accessed=0, transcendentals=0),
    )(both, pair, other)


def near_kernel(near, sums, pair, other, o0, o1, o2, o3, cells):
    pd = lax.rem(lax.axis_index("depth"), 2)
    for i in (0, 1, 10, 11):
        cells[0, i] = jnp.zeros((64, 128), BF16)
    for k in range(4):
        cells[0, 2 + 2 * k : 4 + 2 * k] = near[k]

    def put(start, size, value):
        value = value + sums[:, start : start + size]
        for k, out in enumerate((o0, o1, o2, o3)):
            out[:, start : start + size] = value[16 * k : 16 * k + 16]

    coarse_sums(cells, (2 - 2 * pd,), pair, other, put)


def near_level(near, sums, pair, other):
    vmem = pl.BlockSpec(memory_space=pltpu.VMEM)
    return pl.pallas_call(
        near_kernel,
        out_shape=[jax.ShapeDtypeStruct((16, 640), F32)] * 4,
        in_specs=[vmem] * 4,
        out_specs=[vmem] * 4,
        scratch_shapes=[pltpu.VMEM((1, 12, 64, 128), BF16)],
        compiler_params=pltpu.CompilerParams(vmem_limit_bytes=6 * 1024 * 1024),
    )(near, sums, pair, other)


def join_kernel(s0, s1, s2, s3, bias, out, held):
    y = lax.div(lax.axis_index("rows"), 4)
    for k, part in enumerate((s0, s1, s2, s3)):
        held[y ^ k] = part[...]
    low = lax.broadcasted_iota(jnp.int32, (16, 128), 1) < 64
    for m in range(4):
        tiles = [held[m, :, 128 * i : 128 * i + 128] for i in range(4)]
        if m > 0:
            tiles[0] = tiles[0] + jnp.where(low, held[m - 1, :, 512:], 0.0)
        if m < 3:
            tiles[3] = tiles[3] + jnp.where(low, 0.0, held[m + 1, :, 512:])
        for i in range(4):
            value = jnp.maximum(tiles[i] + bias[...], 0.0).astype(BF16)
            out[:, 512 * m + 128 * i : 512 * m + 128 * i + 128] = value


def join(parts, bias):
    vmem = pl.BlockSpec(memory_space=pltpu.VMEM)
    return pl.pallas_call(
        join_kernel,
        out_shape=jax.ShapeDtypeStruct((16, 2048), BF16),
        in_specs=[vmem] * 5,
        out_specs=vmem,
        scratch_shapes=[pltpu.VMEM((4, 16, 640), F32)],
        compiler_params=pltpu.CompilerParams(vmem_limit_bytes=4 * 1024 * 1024),
    )(*parts, bias)


def body(volume, fine_filters, fine_bias, coarse_filters, coarse_bias):
    d = lax.axis_index("depth")
    r = lax.axis_index("rows")
    pd = lax.rem(d, 2)
    pr = lax.rem(r, 2)
    depth_near, depth_far = near_pairs(16), far_pairs(16)
    rows_near, rows_far = near_pairs(16), far_pairs(16)

    x2 = lax.ppermute(lax.dynamic_index_in_dim(volume, pd, 0, False), "depth", depth_far)
    x1 = lax.ppermute(lax.dynamic_index_in_dim(volume, 1 - pd, 0, False), "depth", depth_near)
    r2 = lax.ppermute(lax.dynamic_index_in_dim(volume, 3 * pr, 1, False), "rows", rows_far)
    r1 = lax.ppermute(lax.dynamic_index_in_dim(volume, 3 - 3 * pr, 1, False), "rows", rows_near)
    sides = jnp.stack([x2, x1])
    c2 = lax.ppermute(lax.dynamic_index_in_dim(sides, 3 * pr, 1, False), "rows", rows_far)
    c1 = lax.ppermute(lax.dynamic_index_in_dim(sides, 3 - 3 * pr, 1, False), "rows", rows_near)

    def along_y(k):
        return [(i, i ^ (4 * k)) for i in range(16)]

    w = jnp.transpose(coarse_filters, (0, 1, 2, 4, 3)).reshape(27, 16, 128)
    pair = jnp.stack([w, lax.ppermute(w, "rows", along_y(1))])
    other = lax.ppermute(pair, "rows", along_y(3))
    main = fine_level(volume, x2, x1, r2, r1, fine_filters, fine_bias.reshape(1, 128))
    pooled = finish(main, c2, c1, other)

    both = lax.all_to_all(
        pooled, ("depth", "rows"), 0, 0, axis_index_groups=far_and_z(), tiled=True
    ).reshape(2, 4, 2, 64, 128)
    near = lax.ppermute(lax.dynamic_index_in_dim(both, 1 - pd, 0, False), "depth", depth_near)
    sums = near_level(near, coarse_level(both, pair, other), pair, other)
    parts = [sums[0]] + [lax.ppermute(sums[k], "rows", along_y(k)) for k in (1, 2, 3)]
    result = join(parts, jnp.broadcast_to(coarse_bias[:, None], (16, 128)))
    return result.reshape(16, 1, 2048)


def solution(mesh):
    placed = (
        P("depth", "rows", None, None),
        P(),
        P(),
        P(None, None, None, None, "rows"),
        P("rows"),
    )
    return jax.shard_map(
        body, mesh=mesh, in_specs=placed, out_specs=P("rows", "depth", None), check_vma=False
    )
```

```python
import jax
import jax.numpy as jnp
from jax import lax
from jax.experimental import pallas as pl
from jax.experimental.pallas import tpu as pltpu
from jax.sharding import PartitionSpec as P

BF16 = jnp.bfloat16
F32 = jnp.float32


def near_pairs(count):
    return [(i, i ^ 1) for i in range(count)]


def far_pairs(count):
    return [(i, min(max(((i - 1) ^ 1) + 1, 0), count - 1)) for i in range(count)]


def far_and_z():
    groups = [
        [d * 16 + 4 * y + z for d in (k, k + 1) for z in range(4)] for k in range(1, 15, 2) for y in range(4)
    ]
    groups += [[d * 16 + 4 * y + z for y in (k, k + 1) for z in range(4)] for d in (0, 15) for k in (0, 2)]
    return groups


def own_half():
    y = lax.div(lax.axis_index("rows"), 4)
    return jnp.where(inner("depth"), 1 - lax.rem(lax.axis_index("depth"), 2), lax.rem(y, 2))


def inner(axis):
    i = lax.axis_index(axis)
    return (i > 0) & (i < 15)


def spread(line, col):
    left = jnp.where(col == 0, 0.0, pltpu.roll(line[:, :128], 1, 0))
    right = jnp.where(col == 127, 0.0, pltpu.roll(line[:, 256:], 127, 0))
    return line[:, 128:256] + left + right


def fine_kernel(vol, x2, x1, r2, r1, w, bias, ends, best, corner_w, cells):
    pd = lax.rem(lax.axis_index("depth"), 2)
    pr = lax.rem(lax.axis_index("rows"), 2)
    inner_d = inner("depth")
    inner_r = inner("rows")
    zero = jnp.zeros((128, 128), BF16)
    for j in range(4):
        for i in range(6):
            row = (i - 1) + pr * (5 - 2 * i)
            if j in (1, 2):
                plane = (j - 1) + pd * (3 - 2 * j)
                piece = r2[plane] if i == 0 else r1[plane] if i == 5 else vol[plane, row]
            elif i in (0, 5):
                piece = zero
            else:
                piece = (x2 if j == 0 else x1)[row]
            if i == 0:
                piece = jnp.where(inner_r, piece, zero)
            if j == 0:
                piece = jnp.where(inner_d, piece, zero)
            cells[j, i] = piece
    taps = [(a, b) for a in range(3) for b in range(3)]
    groups = [taps[i : i + 2] for i in range(0, 9, 2)]
    col = lax.broadcasted_iota(jnp.int32, (128, 128), 0)
    for s in range(2):
        total = None
        for group in groups:
            lhs = jnp.concatenate(
                [cells[s + a, b : b + 4].reshape(512, 128) for a, b in group], axis=1
            )
            rhs = jnp.concatenate(
                [
                    jnp.concatenate(
                        [w[a + pd * (2 - 2 * a), b + pr * (2 - 2 * b), c] for c in range(3)], axis=1
                    )
                    for a, b in group
                ],
                axis=0,
            )
            term = jnp.dot(lhs, rhs, preferred_element_type=F32)
            total = term if total is None else total + term
        for q in range(2):
            ends[s, q] = spread(total[3 * q * 128 : (3 * q + 1) * 128], col) + bias[...]
            middle = spread(total[(q + 1) * 128 : (q + 2) * 128], col) + bias[...]
            best[q] = middle if s == 0 else jnp.maximum(best[q], middle)
            a, b = 2 * s, 2 * q
            for c in range(3):
                corner_w[s, q, :, 128 * c : 128 * c + 128] = w[a + pd * (2 - 2 * a), b + pr * (2 - 2 * b), c]


def fine_level(vol, x2, x1, r2, r1, w, bias):
    vmem = pl.BlockSpec(memory_space=pltpu.VMEM)
    return pl.pallas_call(
        fine_kernel,
        out_shape=[
            jax.ShapeDtypeStruct((2, 2, 128, 128), F32),
            jax.ShapeDtypeStruct((2, 128, 128), F32),
            jax.ShapeDtypeStruct((2, 2, 128, 384), BF16),
        ],
        in_specs=[vmem] * 7,
        out_specs=[vmem] * 3,
        scratch_shapes=[pltpu.VMEM((4, 6, 128, 128), BF16)],
        compiler_params=pltpu.CompilerParams(vmem_limit_bytes=12 * 1024 * 1024),
        cost_estimate=pl.CostEstimate(flops=20_000_000_000, bytes_accessed=0, transcendentals=0),
    )(vol, x2, x1, r2, r1, w, bias)


def finish_kernel(ends, best, corner_w, c2, c1, other, out, peak):
    pr = lax.rem(lax.axis_index("rows"), 2)
    inner_d = inner("depth")
    inner_r = inner("rows")
    zero = jnp.zeros((128, 128), BF16)
    col = lax.broadcasted_iota(jnp.int32, (128, 128), 0)
    for q in range(2):
        value = best[q]
        for s in range(2):
            piece = (c2, c1)[q][s]
            if q == 0:
                piece = jnp.where(inner_r, piece, zero)
            if s == 0:
                piece = jnp.where(inner_d, piece, zero)
            corner = jnp.dot(piece, corner_w[s, q], preferred_element_type=F32)
            value = jnp.maximum(value, ends[s, q] + spread(corner, col))
        peak[...] = value
        pooled = jnp.maximum(peak[pl.ds(0, 64, stride=2), :], peak[pl.ds(1, 64, stride=2), :])
        pooled = jnp.maximum(pooled, 0.0).astype(BF16)
        for k in range(8):
            out[k, q + pr * (1 - 2 * q)] = pooled


def finish(main, c2, c1, other):
    vmem = pl.BlockSpec(memory_space=pltpu.VMEM)
    return pl.pallas_call(
        finish_kernel,
        out_shape=jax.ShapeDtypeStruct((8, 2, 64, 128), BF16),
        in_specs=[vmem] * 5 + [pl.BlockSpec(memory_space=pl.ANY)],
        out_specs=vmem,
        scratch_shapes=[pltpu.VMEM((128, 128), F32)],
        compiler_params=pltpu.CompilerParams(vmem_limit_bytes=6 * 1024 * 1024),
    )(*main, c2, c1, other)


def coarse_sums(cells, taps, pair, other, add):
    lhs = jnp.concatenate(
        [
            jnp.concatenate([w[m, 9 * a + 3 * b + c] for a in taps for b in range(3)], axis=1)
            for c in range(3)
            for w, m in ((pair, 0), (pair, 1), (other, 1), (other, 0))
        ],
        axis=0,
    )
    count = len(taps)
    for start, size in ((0, 256), (256, 256), (512, 128)):
        if start < 512:
            first = start // 64 + 1
            blocks = [
                cells[i, first + b : first + b + 4].reshape(256, 128) for i in range(count) for b in range(3)
            ]
        else:
            blocks = [
                jnp.concatenate([cells[i, 9 + b], cells[i, b]], axis=0) for i in range(count) for b in range(3)
            ]
        rhs = jnp.concatenate(blocks, axis=1)
        term = lax.dot_general(lhs, rhs, (((1,), (1,)), ((), ())), preferred_element_type=F32)
        lane = lax.rem(lax.broadcasted_iota(jnp.int32, (64, size), 1), 64)
        left = jnp.where(lane == 0, 0.0, pltpu.roll(term[:64], 1, 1))
        right = jnp.where(lane == 63, 0.0, pltpu.roll(term[128:], size - 1, 1))
        add(start, size, term[64:128] + left + right)


def coarse_kernel(both, pair, other, out, cells):
    pd = lax.rem(lax.axis_index("depth"), 2)
    inner_d = inner("depth")
    for a in range(2):
        for i in (0, 1, 10, 11):
            cells[a, i] = jnp.zeros((64, 128), BF16)
    own = own_half()
    for k in range(4):
        far = both[1 - own, k]
        cells[0, 2 + 2 * k : 4 + 2 * k] = jnp.where(inner_d, far, jnp.zeros_like(far))
        cells[1, 2 + 2 * k : 4 + 2 * k] = both[own, k]

    def put(start, size, value):
        out[:, start : start + size] = value

    coarse_sums(cells, (2 * pd, 1), pair, other, put)


def coarse_level(both, pair, other):
    vmem = pl.BlockSpec(memory_space=pltpu.VMEM)
    return pl.pallas_call(
        coarse_kernel,
        out_shape=jax.ShapeDtypeStruct((64, 640), F32),
        in_specs=[vmem] * 3,
        out_specs=vmem,
        scratch_shapes=[pltpu.VMEM((2, 12, 64, 128), BF16)],
        compiler_params=pltpu.CompilerParams(vmem_limit_bytes=6 * 1024 * 1024),
        cost_estimate=pl.CostEstimate(flops=150_000_000, bytes_accessed=0, transcendentals=0),
    )(both, pair, other)


def near_kernel(near, sums, pair, other, o0, o1, o2, o3, cells):
    pd = lax.rem(lax.axis_index("depth"), 2)
    for i in (0, 1, 10, 11):
        cells[0, i] = jnp.zeros((64, 128), BF16)
    for k in range(4):
        cells[0, 2 + 2 * k : 4 + 2 * k] = near[k]

    def put(start, size, value):
        value = value + sums[:, start : start + size]
        for k, out in enumerate((o0, o1, o2, o3)):
            out[:, start : start + size] = value[16 * k : 16 * k + 16]

    coarse_sums(cells, (2 - 2 * pd,), pair, other, put)


def near_level(near, sums, pair, other):
    vmem = pl.BlockSpec(memory_space=pltpu.VMEM)
    return pl.pallas_call(
        near_kernel,
        out_shape=[jax.ShapeDtypeStruct((16, 640), F32)] * 4,
        in_specs=[vmem] * 4,
        out_specs=[vmem] * 4,
        scratch_shapes=[pltpu.VMEM((1, 12, 64, 128), BF16)],
        compiler_params=pltpu.CompilerParams(vmem_limit_bytes=6 * 1024 * 1024),
    )(near, sums, pair, other)


def join_kernel(s0, s1, s2, s3, bias, out, held):
    y = lax.div(lax.axis_index("rows"), 4)
    for k, part in enumerate((s0, s1, s2, s3)):
        held[y ^ k] = part[...]
    low = lax.broadcasted_iota(jnp.int32, (16, 128), 1) < 64
    for m in range(4):
        tiles = [held[m, :, 128 * i : 128 * i + 128] for i in range(4)]
        if m > 0:
            tiles[0] = tiles[0] + jnp.where(low, held[m - 1, :, 512:], 0.0)
        if m < 3:
            tiles[3] = tiles[3] + jnp.where(low, 0.0, held[m + 1, :, 512:])
        for i in range(4):
            value = jnp.maximum(tiles[i] + bias[...], 0.0).astype(BF16)
            out[:, 512 * m + 128 * i : 512 * m + 128 * i + 128] = value


def join(parts, bias):
    vmem = pl.BlockSpec(memory_space=pltpu.VMEM)
    return pl.pallas_call(
        join_kernel,
        out_shape=jax.ShapeDtypeStruct((16, 2048), BF16),
        in_specs=[vmem] * 5,
        out_specs=vmem,
        scratch_shapes=[pltpu.VMEM((4, 16, 640), F32)],
        compiler_params=pltpu.CompilerParams(vmem_limit_bytes=4 * 1024 * 1024),
    )(*parts, bias)


def body(volume, fine_filters, fine_bias, coarse_filters, coarse_bias):
    d = lax.axis_index("depth")
    r = lax.axis_index("rows")
    pd = lax.rem(d, 2)
    pr = lax.rem(r, 2)
    depth_near, depth_far = near_pairs(16), far_pairs(16)
    rows_near, rows_far = near_pairs(16), far_pairs(16)

    x2 = lax.ppermute(lax.dynamic_index_in_dim(volume, pd, 0, False), "depth", depth_far)
    x1 = lax.ppermute(lax.dynamic_index_in_dim(volume, 1 - pd, 0, False), "depth", depth_near)
    r2 = lax.ppermute(lax.dynamic_index_in_dim(volume, 3 * pr, 1, False), "rows", rows_far)
    r1 = lax.ppermute(lax.dynamic_index_in_dim(volume, 3 - 3 * pr, 1, False), "rows", rows_near)
    sides = jnp.stack([x2, x1])
    c2 = lax.ppermute(lax.dynamic_index_in_dim(sides, 3 * pr, 1, False), "rows", rows_far)
    c1 = lax.ppermute(lax.dynamic_index_in_dim(sides, 3 - 3 * pr, 1, False), "rows", rows_near)

    def along_y(k):
        return [(i, i ^ (4 * k)) for i in range(16)]

    w = jnp.transpose(coarse_filters, (0, 1, 2, 4, 3)).reshape(27, 16, 128)
    pair = jnp.stack([w, lax.ppermute(w, "rows", along_y(1))])
    other = lax.ppermute(pair, "rows", along_y(3))
    main = fine_level(volume, x2, x1, r2, r1, fine_filters, fine_bias.reshape(1, 128))
    pooled = finish(main, c2, c1, other)

    both = lax.all_to_all(
        pooled, ("depth", "rows"), 0, 0, axis_index_groups=far_and_z(), tiled=True
    ).reshape(2, 4, 2, 64, 128)
    near = lax.ppermute(lax.dynamic_index_in_dim(both, own_half(), 0, False), "depth", depth_near)
    sums = near_level(near, coarse_level(both, pair, other), pair, other)
    parts = [sums[0]] + [lax.ppermute(sums[k], "rows", along_y(k)) for k in (1, 2, 3)]
    result = join(parts, jnp.broadcast_to(coarse_bias[:, None], (16, 128)))
    return result.reshape(16, 1, 2048)


def solution(mesh):
    placed = (
        P("depth", "rows", None, None),
        P(),
        P(),
        P(None, None, None, None, "rows"),
        P("rows"),
    )
    return jax.shard_map(
        body, mesh=mesh, in_specs=placed, out_specs=P("rows", "depth", None), check_vma=False
    )
```

```python
import jax
import jax.numpy as jnp
from jax import lax
from jax.experimental import pallas as pl
from jax.experimental.pallas import tpu as pltpu
from jax.sharding import PartitionSpec as P

BF16 = jnp.bfloat16
F32 = jnp.float32


def near_pairs(count):
    return [(i, i ^ 1) for i in range(count)]


def far_pairs(count):
    return [(i, min(max(((i - 1) ^ 1) + 1, 0), count - 1)) for i in range(count)]


def far_and_z():
    pairs = [(d, d + 1) for d in range(1, 15, 2)] + [(15, 0)]
    return [[d * 16 + 4 * y + z for d in pair for z in range(4)] for pair in pairs for y in range(4)]


def inner(axis):
    i = lax.axis_index(axis)
    return (i > 0) & (i < 15)


def spread(line, col):
    left = jnp.where(col == 0, 0.0, pltpu.roll(line[:, :128], 1, 0))
    right = jnp.where(col == 127, 0.0, pltpu.roll(line[:, 256:], 127, 0))
    return line[:, 128:256] + left + right


def fine_kernel(vol, x2, x1, r2, r1, w, bias, ends, best, corner_w, cells):
    pd = lax.rem(lax.axis_index("depth"), 2)
    pr = lax.rem(lax.axis_index("rows"), 2)
    inner_d = inner("depth")
    inner_r = inner("rows")
    zero = jnp.zeros((128, 128), BF16)
    for j in range(4):
        for i in range(6):
            row = (i - 1) + pr * (5 - 2 * i)
            if j in (1, 2):
                plane = (j - 1) + pd * (3 - 2 * j)
                piece = r2[plane] if i == 0 else r1[plane] if i == 5 else vol[plane, row]
            elif i in (0, 5):
                piece = zero
            else:
                piece = (x2 if j == 0 else x1)[row]
            if i == 0:
                piece = jnp.where(inner_r, piece, zero)
            if j == 0:
                piece = jnp.where(inner_d, piece, zero)
            cells[j, i] = piece
    taps = [(a, b) for a in range(3) for b in range(3)]
    groups = [taps[i : i + 2] for i in range(0, 9, 2)]
    col = lax.broadcasted_iota(jnp.int32, (128, 128), 0)
    for s in range(2):
        total = None
        for group in groups:
            lhs = jnp.concatenate(
                [cells[s + a, b : b + 4].reshape(512, 128) for a, b in group], axis=1
            )
            rhs = jnp.concatenate(
                [
                    jnp.concatenate(
                        [w[a + pd * (2 - 2 * a), b + pr * (2 - 2 * b), c] for c in range(3)], axis=1
                    )
                    for a, b in group
                ],
                axis=0,
            )
            term = jnp.dot(lhs, rhs, preferred_element_type=F32)
            total = term if total is None else total + term
        for q in range(2):
            ends[s, q] = spread(total[3 * q * 128 : (3 * q + 1) * 128], col) + bias[...]
            middle = spread(total[(q + 1) * 128 : (q + 2) * 128], col) + bias[...]
            best[q] = middle if s == 0 else jnp.maximum(best[q], middle)
            a, b = 2 * s, 2 * q
            for c in range(3):
                corner_w[s, q, :, 128 * c : 128 * c + 128] = w[a + pd * (2 - 2 * a), b + pr * (2 - 2 * b), c]


def fine_level(vol, x2, x1, r2, r1, w, bias):
    vmem = pl.BlockSpec(memory_space=pltpu.VMEM)
    return pl.pallas_call(
        fine_kernel,
        out_shape=[
            jax.ShapeDtypeStruct((2, 2, 128, 128), F32),
            jax.ShapeDtypeStruct((2, 128, 128), F32),
            jax.ShapeDtypeStruct((2, 2, 128, 384), BF16),
        ],
        in_specs=[vmem] * 7,
        out_specs=[vmem] * 3,
        scratch_shapes=[pltpu.VMEM((4, 6, 128, 128), BF16)],
        compiler_params=pltpu.CompilerParams(vmem_limit_bytes=12 * 1024 * 1024),
        cost_estimate=pl.CostEstimate(flops=20_000_000_000, bytes_accessed=0, transcendentals=0),
    )(vol, x2, x1, r2, r1, w, bias)


def outer_kernel(far_row, near_row, r2, r1, out):
    pd = lax.rem(lax.axis_index("depth"), 2)
    out[0] = r2[1 - pd]
    out[1] = r1[1 - pd]


def outer_rows(far_row, near_row, r2, r1):
    vmem = pl.BlockSpec(memory_space=pltpu.VMEM)
    return pl.pallas_call(
        outer_kernel,
        out_shape=jax.ShapeDtypeStruct((2, 128, 128), BF16),
        in_specs=[pl.BlockSpec(memory_space=pl.ANY)] * 2 + [vmem] * 2,
        out_specs=vmem,
        compiler_params=pltpu.CompilerParams(vmem_limit_bytes=2 * 1024 * 1024),
    )(far_row, near_row, r2, r1)


def finish_kernel(ends, best, corner_w, c2, c1, e, other, out, peak):
    pr = lax.rem(lax.axis_index("rows"), 2)
    inner_d = inner("depth")
    inner_r = inner("rows")
    zero = jnp.zeros((128, 128), BF16)
    col = lax.broadcasted_iota(jnp.int32, (128, 128), 0)
    for q in range(2):
        value = best[q]
        for s in range(2):
            piece = e[q] if s == 1 else (c2, c1)[q][...]
            if q == 0:
                piece = jnp.where(inner_r, piece, zero)
            if s == 0:
                piece = jnp.where(inner_d, piece, zero)
            corner = jnp.dot(piece, corner_w[s, q], preferred_element_type=F32)
            value = jnp.maximum(value, ends[s, q] + spread(corner, col))
        peak[...] = value
        pooled = jnp.maximum(peak[pl.ds(0, 64, stride=2), :], peak[pl.ds(1, 64, stride=2), :])
        pooled = jnp.maximum(pooled, 0.0).astype(BF16)
        for k in range(8):
            out[k, q + pr * (1 - 2 * q)] = pooled


def finish(main, c2, c1, e, other):
    vmem = pl.BlockSpec(memory_space=pltpu.VMEM)
    return pl.pallas_call(
        finish_kernel,
        out_shape=jax.ShapeDtypeStruct((8, 2, 64, 128), BF16),
        in_specs=[vmem] * 6 + [pl.BlockSpec(memory_space=pl.ANY)],
        out_specs=vmem,
        scratch_shapes=[pltpu.VMEM((128, 128), F32)],
        compiler_params=pltpu.CompilerParams(vmem_limit_bytes=6 * 1024 * 1024),
    )(*main, c2, c1, e, other)


def coarse_sums(cells, taps, pair, other, add):
    lhs = jnp.concatenate(
        [
            jnp.concatenate([w[m, 9 * a + 3 * b + c] for a in taps for b in range(3)], axis=1)
            for c in range(3)
            for w, m in ((pair, 0), (pair, 1), (other, 1), (other, 0))
        ],
        axis=0,
    )
    count = len(taps)
    for start, size in ((0, 256), (256, 256), (512, 128)):
        if start < 512:
            first = start // 64 + 1
            blocks = [
                cells[i, first + b : first + b + 4].reshape(256, 128) for i in range(count) for b in range(3)
            ]
        else:
            blocks = [
                jnp.concatenate([cells[i, 9 + b], cells[i, b]], axis=0) for i in range(count) for b in range(3)
            ]
        rhs = jnp.concatenate(blocks, axis=1)
        term = lax.dot_general(lhs, rhs, (((1,), (1,)), ((), ())), preferred_element_type=F32)
        lane = lax.rem(lax.broadcasted_iota(jnp.int32, (64, size), 1), 64)
        left = jnp.where(lane == 0, 0.0, pltpu.roll(term[:64], 1, 1))
        right = jnp.where(lane == 63, 0.0, pltpu.roll(term[128:], size - 1, 1))
        add(start, size, term[64:128] + left + right)


def coarse_kernel(both, pair, other, out, cells):
    pd = lax.rem(lax.axis_index("depth"), 2)
    inner_d = inner("depth")
    for a in range(2):
        for i in (0, 1, 10, 11):
            cells[a, i] = jnp.zeros((64, 128), BF16)
    for k in range(4):
        far = both[pd, k]
        cells[0, 2 + 2 * k : 4 + 2 * k] = jnp.where(inner_d, far, jnp.zeros_like(far))
        cells[1, 2 + 2 * k : 4 + 2 * k] = both[1 - pd, k]

    def put(start, size, value):
        out[:, start : start + size] = value

    coarse_sums(cells, (2 * pd, 1), pair, other, put)


def coarse_level(both, pair, other):
    vmem = pl.BlockSpec(memory_space=pltpu.VMEM)
    return pl.pallas_call(
        coarse_kernel,
        out_shape=jax.ShapeDtypeStruct((64, 640), F32),
        in_specs=[vmem] * 3,
        out_specs=vmem,
        scratch_shapes=[pltpu.VMEM((2, 12, 64, 128), BF16)],
        compiler_params=pltpu.CompilerParams(vmem_limit_bytes=6 * 1024 * 1024),
        cost_estimate=pl.CostEstimate(flops=150_000_000, bytes_accessed=0, transcendentals=0),
    )(both, pair, other)


def near_kernel(near, sums, pair, other, o0, o1, o2, o3, cells):
    pd = lax.rem(lax.axis_index("depth"), 2)
    for i in (0, 1, 10, 11):
        cells[0, i] = jnp.zeros((64, 128), BF16)
    for k in range(4):
        cells[0, 2 + 2 * k : 4 + 2 * k] = near[k]

    def put(start, size, value):
        value = value + sums[:, start : start + size]
        for k, out in enumerate((o0, o1, o2, o3)):
            out[:, start : start + size] = value[16 * k : 16 * k + 16]

    coarse_sums(cells, (2 - 2 * pd,), pair, other, put)


def near_level(near, sums, pair, other):
    vmem = pl.BlockSpec(memory_space=pltpu.VMEM)
    return pl.pallas_call(
        near_kernel,
        out_shape=[jax.ShapeDtypeStruct((16, 640), F32)] * 4,
        in_specs=[vmem] * 4,
        out_specs=[vmem] * 4,
        scratch_shapes=[pltpu.VMEM((1, 12, 64, 128), BF16)],
        compiler_params=pltpu.CompilerParams(vmem_limit_bytes=6 * 1024 * 1024),
    )(near, sums, pair, other)


def join_kernel(s0, s1, s2, s3, bias, out, held):
    y = lax.div(lax.axis_index("rows"), 4)
    for k, part in enumerate((s0, s1, s2, s3)):
        held[y ^ k] = part[...]
    low = lax.broadcasted_iota(jnp.int32, (16, 128), 1) < 64
    for m in range(4):
        tiles = [held[m, :, 128 * i : 128 * i + 128] for i in range(4)]
        if m > 0:
            tiles[0] = tiles[0] + jnp.where(low, held[m - 1, :, 512:], 0.0)
        if m < 3:
            tiles[3] = tiles[3] + jnp.where(low, 0.0, held[m + 1, :, 512:])
        for i in range(4):
            value = jnp.maximum(tiles[i] + bias[...], 0.0).astype(BF16)
            out[:, 512 * m + 128 * i : 512 * m + 128 * i + 128] = value


def join(parts, bias):
    vmem = pl.BlockSpec(memory_space=pltpu.VMEM)
    return pl.pallas_call(
        join_kernel,
        out_shape=jax.ShapeDtypeStruct((16, 2048), BF16),
        in_specs=[vmem] * 5,
        out_specs=vmem,
        scratch_shapes=[pltpu.VMEM((4, 16, 640), F32)],
        compiler_params=pltpu.CompilerParams(vmem_limit_bytes=4 * 1024 * 1024),
    )(*parts, bias)


def body(volume, fine_filters, fine_bias, coarse_filters, coarse_bias):
    d = lax.axis_index("depth")
    r = lax.axis_index("rows")
    pd = lax.rem(d, 2)
    pr = lax.rem(r, 2)
    depth_near, depth_far = near_pairs(16), far_pairs(16)
    rows_near, rows_far = near_pairs(16), far_pairs(16)

    x2 = lax.ppermute(lax.dynamic_index_in_dim(volume, pd, 0, False), "depth", depth_far)
    x1 = lax.ppermute(lax.dynamic_index_in_dim(volume, 1 - pd, 0, False), "depth", depth_near)
    r2 = lax.ppermute(lax.dynamic_index_in_dim(volume, 3 * pr, 1, False), "rows", rows_far)
    r1 = lax.ppermute(lax.dynamic_index_in_dim(volume, 3 - 3 * pr, 1, False), "rows", rows_near)
    far_row = lax.dynamic_index_in_dim(x2, 3 * pr, 0, False)
    near_row = lax.dynamic_index_in_dim(x2, 3 - 3 * pr, 0, False)
    c2 = lax.ppermute(far_row, "rows", rows_far)
    c1 = lax.ppermute(near_row, "rows", rows_near)
    e = lax.ppermute(outer_rows(far_row, near_row, r2, r1), "depth", depth_near)

    def along_y(k):
        return [(i, i ^ (4 * k)) for i in range(16)]

    w = jnp.transpose(coarse_filters, (0, 1, 2, 4, 3)).reshape(27, 16, 128)
    pair = jnp.stack([w, lax.ppermute(w, "rows", along_y(1))])
    other = lax.ppermute(pair, "rows", along_y(3))
    main = fine_level(volume, x2, x1, r2, r1, fine_filters, fine_bias.reshape(1, 128))
    pooled = finish(main, c2, c1, e, other)

    both = lax.all_to_all(
        pooled, ("depth", "rows"), 0, 0, axis_index_groups=far_and_z(), tiled=True
    ).reshape(2, 4, 2, 64, 128)
    near = lax.ppermute(lax.dynamic_index_in_dim(both, 1 - pd, 0, False), "depth", depth_near)
    sums = near_level(near, coarse_level(both, pair, other), pair, other)
    parts = [sums[0]] + [lax.ppermute(sums[k], "rows", along_y(k)) for k in (1, 2, 3)]
    result = join(parts, jnp.broadcast_to(coarse_bias[:, None], (16, 128)))
    return result.reshape(16, 1, 2048)


def solution(mesh):
    placed = (
        P("depth", "rows", None, None),
        P(),
        P(),
        P(None, None, None, None, "rows"),
        P("rows"),
    )
    return jax.shard_map(
        body, mesh=mesh, in_specs=placed, out_specs=P("rows", "depth", None), check_vma=False
    )
```

```python
import jax
import jax.numpy as jnp
from jax import lax
from jax.experimental import pallas as pl
from jax.experimental.pallas import tpu as pltpu
from jax.sharding import PartitionSpec as P

BF16 = jnp.bfloat16
F32 = jnp.float32


def near_pairs(count):
    return [(i, i ^ 1) for i in range(count)]


def far_pairs(count):
    return [(i, min(max(((i - 1) ^ 1) + 1, 0), count - 1)) for i in range(count)]


def far_and_z():
    pairs = [(d, d + 1) for d in range(1, 15, 2)] + [(15, 0)]
    return [[d * 16 + 4 * y + z for d in pair for z in range(4)] for pair in pairs for y in range(4)]


def inner(axis):
    i = lax.axis_index(axis)
    return (i > 0) & (i < 15)


def spread(line, col):
    left = jnp.where(col == 0, 0.0, pltpu.roll(line[:, :128], 1, 0))
    right = jnp.where(col == 127, 0.0, pltpu.roll(line[:, 256:], 127, 0))
    return line[:, 128:256] + left + right


def fine_kernel(vol, x2, x1, r2, r1, w, bias, ends, best, corner_w, cells):
    pd = lax.rem(lax.axis_index("depth"), 2)
    pr = lax.rem(lax.axis_index("rows"), 2)
    inner_d = inner("depth")
    inner_r = inner("rows")
    zero = jnp.zeros((128, 128), BF16)
    for j in range(4):
        for i in range(6):
            row = (i - 1) + pr * (5 - 2 * i)
            if j in (1, 2):
                plane = (j - 1) + pd * (3 - 2 * j)
                piece = r2[plane] if i == 0 else r1[plane] if i == 5 else vol[plane, row]
            elif i in (0, 5):
                piece = zero
            else:
                piece = (x2 if j == 0 else x1)[row]
            if i == 0:
                piece = jnp.where(inner_r, piece, zero)
            if j == 0:
                piece = jnp.where(inner_d, piece, zero)
            cells[j, i] = piece
    taps = [(a, b) for a in range(3) for b in range(3)]
    groups = [taps[i : i + 2] for i in range(0, 9, 2)]
    col = lax.broadcasted_iota(jnp.int32, (128, 128), 0)
    for s in range(2):
        total = None
        for group in groups:
            lhs = jnp.concatenate(
                [cells[s + a, b : b + 4].reshape(512, 128) for a, b in group], axis=1
            )
            rhs = jnp.concatenate(
                [
                    jnp.concatenate(
                        [w[a + pd * (2 - 2 * a), b + pr * (2 - 2 * b), c] for c in range(3)], axis=1
                    )
                    for a, b in group
                ],
                axis=0,
            )
            term = jnp.dot(lhs, rhs, preferred_element_type=F32)
            total = term if total is None else total + term
        for q in range(2):
            ends[s, q] = spread(total[3 * q * 128 : (3 * q + 1) * 128], col) + bias[...]
            middle = spread(total[(q + 1) * 128 : (q + 2) * 128], col) + bias[...]
            best[q] = middle if s == 0 else jnp.maximum(best[q], middle)
            a, b = 2 * s, 2 * q
            for c in range(3):
                corner_w[s, q, :, 128 * c : 128 * c + 128] = w[a + pd * (2 - 2 * a), b + pr * (2 - 2 * b), c]


def fine_level(vol, x2, x1, r2, r1, w, bias):
    vmem = pl.BlockSpec(memory_space=pltpu.VMEM)
    return pl.pallas_call(
        fine_kernel,
        out_shape=[
            jax.ShapeDtypeStruct((2, 2, 128, 128), F32),
            jax.ShapeDtypeStruct((2, 128, 128), F32),
            jax.ShapeDtypeStruct((2, 2, 128, 384), BF16),
        ],
        in_specs=[vmem] * 7,
        out_specs=[vmem] * 3,
        scratch_shapes=[pltpu.VMEM((4, 6, 128, 128), BF16)],
        compiler_params=pltpu.CompilerParams(vmem_limit_bytes=12 * 1024 * 1024),
        cost_estimate=pl.CostEstimate(flops=20_000_000_000, bytes_accessed=0, transcendentals=0),
    )(vol, x2, x1, r2, r1, w, bias)


def outer_kernel(far_row, near_row, r2, r1, out):
    pd = lax.rem(lax.axis_index("depth"), 2)
    out[0] = r2[1 - pd]
    out[1] = r1[1 - pd]


def outer_rows(far_row, near_row, r2, r1):
    vmem = pl.BlockSpec(memory_space=pltpu.VMEM)
    return pl.pallas_call(
        outer_kernel,
        out_shape=jax.ShapeDtypeStruct((2, 128, 128), BF16),
        in_specs=[pl.BlockSpec(memory_space=pl.ANY)] * 2 + [vmem] * 2,
        out_specs=vmem,
        compiler_params=pltpu.CompilerParams(vmem_limit_bytes=2 * 1024 * 1024),
    )(far_row, near_row, r2, r1)


def finish_kernel(ends, best, corner_w, c2, c1, e, other, out, peak):
    pr = lax.rem(lax.axis_index("rows"), 2)
    inner_d = inner("depth")
    inner_r = inner("rows")
    zero = jnp.zeros((128, 128), BF16)
    col = lax.broadcasted_iota(jnp.int32, (128, 128), 0)
    for q in range(2):
        value = best[q]
        for s in range(2):
            piece = e[q] if s == 1 else (c2, c1)[q][...]
            if q == 0:
                piece = jnp.where(inner_r, piece, zero)
            if s == 0:
                piece = jnp.where(inner_d, piece, zero)
            corner = jnp.dot(piece, corner_w[s, q], preferred_element_type=F32)
            value = jnp.maximum(value, ends[s, q] + spread(corner, col))
        peak[...] = value
        pooled = jnp.maximum(peak[pl.ds(0, 64, stride=2), :], peak[pl.ds(1, 64, stride=2), :])
        pooled = jnp.maximum(pooled, 0.0).astype(BF16)
        for k in range(8):
            out[k, q + pr * (1 - 2 * q)] = pooled


def finish(main, c2, c1, e, other):
    vmem = pl.BlockSpec(memory_space=pltpu.VMEM)
    return pl.pallas_call(
        finish_kernel,
        out_shape=jax.ShapeDtypeStruct((8, 2, 64, 128), BF16),
        in_specs=[vmem] * 6 + [pl.BlockSpec(memory_space=pl.ANY)],
        out_specs=vmem,
        scratch_shapes=[pltpu.VMEM((128, 128), F32)],
        compiler_params=pltpu.CompilerParams(vmem_limit_bytes=6 * 1024 * 1024),
    )(*main, c2, c1, e, other)


def coarse_sums(cells, taps, pair, other, add):
    lhs = jnp.concatenate(
        [
            jnp.concatenate([w[m, 9 * a + 3 * b + c] for a in taps for b in range(3)], axis=1)
            for c in range(3)
            for w, m in ((pair, 0), (pair, 1), (other, 1), (other, 0))
        ],
        axis=0,
    )
    count = len(taps)
    for start, size in ((0, 256), (256, 256), (512, 128)):
        if start < 512:
            first = start // 64 + 1
            blocks = [
                cells[i, first + b : first + b + 4].reshape(256, 128) for i in range(count) for b in range(3)
            ]
        else:
            blocks = [
                jnp.concatenate([cells[i, 9 + b], cells[i, b]], axis=0) for i in range(count) for b in range(3)
            ]
        rhs = jnp.concatenate(blocks, axis=1)
        term = lax.dot_general(lhs, rhs, (((1,), (1,)), ((), ())), preferred_element_type=F32)
        lane = lax.rem(lax.broadcasted_iota(jnp.int32, (64, size), 1), 64)
        left = jnp.where(lane == 0, 0.0, pltpu.roll(term[:64], 1, 1))
        right = jnp.where(lane == 63, 0.0, pltpu.roll(term[128:], size - 1, 1))
        add(start, size, term[64:128] + left + right)


def coarse_kernel(both, pair, other, out, cells):
    pd = lax.rem(lax.axis_index("depth"), 2)
    inner_d = inner("depth")
    for a in range(2):
        for i in (0, 1, 10, 11):
            cells[a, i] = jnp.zeros((64, 128), BF16)
    for k in range(4):
        far = both[pd, k]
        cells[0, 2 + 2 * k : 4 + 2 * k] = jnp.where(inner_d, far, jnp.zeros_like(far))
        cells[1, 2 + 2 * k : 4 + 2 * k] = both[1 - pd, k]

    def put(start, size, value):
        out[:, start : start + size] = value

    coarse_sums(cells, (2 * pd, 1), pair, other, put)


def coarse_level(both, pair, other):
    vmem = pl.BlockSpec(memory_space=pltpu.VMEM)
    return pl.pallas_call(
        coarse_kernel,
        out_shape=jax.ShapeDtypeStruct((64, 640), F32),
        in_specs=[vmem] * 3,
        out_specs=vmem,
        scratch_shapes=[pltpu.VMEM((2, 12, 64, 128), BF16)],
        compiler_params=pltpu.CompilerParams(vmem_limit_bytes=6 * 1024 * 1024),
        cost_estimate=pl.CostEstimate(flops=150_000_000, bytes_accessed=0, transcendentals=0),
    )(both, pair, other)


def near_kernel(near, sums, pair, other, o0, o1, o2, o3, cells):
    pd = lax.rem(lax.axis_index("depth"), 2)
    for i in (0, 1, 10, 11):
        cells[0, i] = jnp.zeros((64, 128), BF16)
    for k in range(4):
        cells[0, 2 + 2 * k : 4 + 2 * k] = near[k]

    def put(start, size, value):
        value = value + sums[:, start : start + size]
        for k, out in enumerate((o0, o1, o2, o3)):
            out[:, start : start + size] = value[16 * k : 16 * k + 16]

    coarse_sums(cells, (2 - 2 * pd,), pair, other, put)


def near_level(near, sums, pair, other):
    vmem = pl.BlockSpec(memory_space=pltpu.VMEM)
    return pl.pallas_call(
        near_kernel,
        out_shape=[jax.ShapeDtypeStruct((16, 640), F32)] * 4,
        in_specs=[vmem] * 4,
        out_specs=[vmem] * 4,
        scratch_shapes=[pltpu.VMEM((1, 12, 64, 128), BF16)],
        compiler_params=pltpu.CompilerParams(vmem_limit_bytes=6 * 1024 * 1024),
    )(near, sums, pair, other)


def join_kernel(s0, s2, s3, s1, bias, out, held):
    y = lax.div(lax.axis_index("rows"), 4)
    for k, part in enumerate((s0, s1, s2, s3)):
        held[y ^ k] = part[...]
    low = lax.broadcasted_iota(jnp.int32, (16, 128), 1) < 64
    for m in range(4):
        tiles = [held[m, :, 128 * i : 128 * i + 128] for i in range(4)]
        if m > 0:
            tiles[0] = tiles[0] + jnp.where(low, held[m - 1, :, 512:], 0.0)
        if m < 3:
            tiles[3] = tiles[3] + jnp.where(low, 0.0, held[m + 1, :, 512:])
        for i in range(4):
            value = jnp.maximum(tiles[i] + bias[...], 0.0).astype(BF16)
            out[:, 512 * m + 128 * i : 512 * m + 128 * i + 128] = value


def join(parts, bias):
    vmem = pl.BlockSpec(memory_space=pltpu.VMEM)
    return pl.pallas_call(
        join_kernel,
        out_shape=jax.ShapeDtypeStruct((16, 2048), BF16),
        in_specs=[vmem] * 5,
        out_specs=vmem,
        scratch_shapes=[pltpu.VMEM((4, 16, 640), F32)],
        compiler_params=pltpu.CompilerParams(vmem_limit_bytes=4 * 1024 * 1024),
    )(*parts, bias)


def body(volume, fine_filters, fine_bias, coarse_filters, coarse_bias):
    d = lax.axis_index("depth")
    r = lax.axis_index("rows")
    pd = lax.rem(d, 2)
    pr = lax.rem(r, 2)
    depth_near, depth_far = near_pairs(16), far_pairs(16)
    rows_near, rows_far = near_pairs(16), far_pairs(16)

    x2 = lax.ppermute(lax.dynamic_index_in_dim(volume, pd, 0, False), "depth", depth_far)
    x1 = lax.ppermute(lax.dynamic_index_in_dim(volume, 1 - pd, 0, False), "depth", depth_near)
    r2 = lax.ppermute(lax.dynamic_index_in_dim(volume, 3 * pr, 1, False), "rows", rows_far)
    r1 = lax.ppermute(lax.dynamic_index_in_dim(volume, 3 - 3 * pr, 1, False), "rows", rows_near)
    far_row = lax.dynamic_index_in_dim(x2, 3 * pr, 0, False)
    near_row = lax.dynamic_index_in_dim(x2, 3 - 3 * pr, 0, False)
    c2 = lax.ppermute(far_row, "rows", rows_far)
    c1 = lax.ppermute(near_row, "rows", rows_near)
    e = lax.ppermute(outer_rows(far_row, near_row, r2, r1), "depth", depth_near)

    def along_y(k):
        return [(i, i ^ (4 * k)) for i in range(16)]

    w = jnp.transpose(coarse_filters, (0, 1, 2, 4, 3)).reshape(27, 16, 128)
    pair = jnp.stack([w, lax.ppermute(w, "rows", along_y(1))])
    other = lax.ppermute(pair, "rows", along_y(3))
    main = fine_level(volume, x2, x1, r2, r1, fine_filters, fine_bias.reshape(1, 128))
    pooled = finish(main, c2, c1, e, other)

    both = lax.all_to_all(
        pooled, ("depth", "rows"), 0, 0, axis_index_groups=far_and_z(), tiled=True
    ).reshape(2, 4, 2, 64, 128)
    near = lax.ppermute(lax.dynamic_index_in_dim(both, 1 - pd, 0, False), "depth", depth_near)
    sums = near_level(near, coarse_level(both, pair, other), pair, other)
    parts = [sums[0]] + [lax.ppermute(sums[k], "rows", along_y(k)) for k in (2, 3, 1)]
    result = join(parts, jnp.broadcast_to(coarse_bias[:, None], (16, 128)))
    return result.reshape(16, 1, 2048)


def solution(mesh):
    placed = (
        P("depth", "rows", None, None),
        P(),
        P(),
        P(None, None, None, None, "rows"),
        P("rows"),
    )
    return jax.shard_map(
        body, mesh=mesh, in_specs=placed, out_specs=P("rows", "depth", None), check_vma=False
    )
```

```python
import jax
import jax.numpy as jnp
from jax import lax
from jax.experimental import pallas as pl
from jax.experimental.pallas import tpu as pltpu
from jax.sharding import PartitionSpec as P

BF16 = jnp.bfloat16
F32 = jnp.float32


def near_pairs(count):
    return [(i, i ^ 1) for i in range(count)]


def far_pairs(count):
    return [(i, min(max(((i - 1) ^ 1) + 1, 0), count - 1)) for i in range(count)]


def far_and_z():
    pairs = [(d, d + 1) for d in range(1, 15, 2)] + [(15, 0)]
    return [[d * 16 + 4 * y + z for d in pair for z in range(4)] for pair in pairs for y in range(4)]


def inner(axis):
    i = lax.axis_index(axis)
    return (i > 0) & (i < 15)


def far_plane_kernel(vol, out):
    out[...] = vol[lax.rem(lax.axis_index("depth"), 2)]


def far_plane(vol):
    return pl.pallas_call(
        far_plane_kernel,
        out_shape=jax.ShapeDtypeStruct(vol.shape[1:], BF16),
        in_specs=[pl.BlockSpec(memory_space=pltpu.VMEM)],
        out_specs=pl.BlockSpec(memory_space=pltpu.VMEM),
        compiler_params=pltpu.CompilerParams(vmem_limit_bytes=2 * 1024 * 1024),
    )(vol)


def spread(line, col):
    left = jnp.where(col == 0, 0.0, pltpu.roll(line[:, :128], 1, 0))
    right = jnp.where(col == 127, 0.0, pltpu.roll(line[:, 256:], 127, 0))
    return line[:, 128:256] + left + right


def fine_kernel(vol, x2, x1, r2, r1, w, bias, ends, best, corner_w, cells):
    pd = lax.rem(lax.axis_index("depth"), 2)
    pr = lax.rem(lax.axis_index("rows"), 2)
    inner_d = inner("depth")
    inner_r = inner("rows")
    zero = jnp.zeros((128, 128), BF16)
    for j in range(4):
        for i in range(6):
            row = (i - 1) + pr * (5 - 2 * i)
            if j in (1, 2):
                plane = (j - 1) + pd * (3 - 2 * j)
                piece = r2[plane] if i == 0 else r1[plane] if i == 5 else vol[plane, row]
            elif i in (0, 5):
                piece = zero
            else:
                piece = (x2 if j == 0 else x1)[row]
            if i == 0:
                piece = jnp.where(inner_r, piece, zero)
            if j == 0:
                piece = jnp.where(inner_d, piece, zero)
            cells[j, i] = piece
    taps = [(a, b) for a in range(3) for b in range(3)]
    groups = [taps[i : i + 2] for i in range(0, 9, 2)]
    col = lax.broadcasted_iota(jnp.int32, (128, 128), 0)
    for s in range(2):
        total = None
        for group in groups:
            lhs = jnp.concatenate(
                [cells[s + a, b : b + 4].reshape(512, 128) for a, b in group], axis=1
            )
            rhs = jnp.concatenate(
                [
                    jnp.concatenate(
                        [w[a + pd * (2 - 2 * a), b + pr * (2 - 2 * b), c] for c in range(3)], axis=1
                    )
                    for a, b in group
                ],
                axis=0,
            )
            term = jnp.dot(lhs, rhs, preferred_element_type=F32)
            total = term if total is None else total + term
        for q in range(2):
            ends[s, q] = spread(total[3 * q * 128 : (3 * q + 1) * 128], col) + bias[...]
            middle = spread(total[(q + 1) * 128 : (q + 2) * 128], col) + bias[...]
            best[q] = middle if s == 0 else jnp.maximum(best[q], middle)
            a, b = 2 * s, 2 * q
            for c in range(3):
                corner_w[s, q, :, 128 * c : 128 * c + 128] = w[a + pd * (2 - 2 * a), b + pr * (2 - 2 * b), c]


def fine_level(vol, x2, x1, r2, r1, w, bias):
    vmem = pl.BlockSpec(memory_space=pltpu.VMEM)
    return pl.pallas_call(
        fine_kernel,
        out_shape=[
            jax.ShapeDtypeStruct((2, 2, 128, 128), F32),
            jax.ShapeDtypeStruct((2, 128, 128), F32),
            jax.ShapeDtypeStruct((2, 2, 128, 384), BF16),
        ],
        in_specs=[vmem] * 7,
        out_specs=[vmem] * 3,
        scratch_shapes=[pltpu.VMEM((4, 6, 128, 128), BF16)],
        compiler_params=pltpu.CompilerParams(vmem_limit_bytes=12 * 1024 * 1024),
        cost_estimate=pl.CostEstimate(flops=20_000_000_000, bytes_accessed=0, transcendentals=0),
    )(vol, x2, x1, r2, r1, w, bias)


def outer_kernel(far_row, near_row, r2, r1, out):
    pd = lax.rem(lax.axis_index("depth"), 2)
    out[0] = r2[1 - pd]
    out[1] = r1[1 - pd]


def outer_rows(far_row, near_row, r2, r1):
    vmem = pl.BlockSpec(memory_space=pltpu.VMEM)
    return pl.pallas_call(
        outer_kernel,
        out_shape=jax.ShapeDtypeStruct((2, 128, 128), BF16),
        in_specs=[pl.BlockSpec(memory_space=pl.ANY)] * 2 + [vmem] * 2,
        out_specs=vmem,
        compiler_params=pltpu.CompilerParams(vmem_limit_bytes=2 * 1024 * 1024),
    )(far_row, near_row, r2, r1)


def finish_kernel(ends, best, corner_w, c2, c1, e, other, out, peak):
    pr = lax.rem(lax.axis_index("rows"), 2)
    inner_d = inner("depth")
    inner_r = inner("rows")
    zero = jnp.zeros((128, 128), BF16)
    col = lax.broadcasted_iota(jnp.int32, (128, 128), 0)
    for q in range(2):
        value = best[q]
        for s in range(2):
            piece = e[q] if s == 1 else (c2, c1)[q][...]
            if q == 0:
                piece = jnp.where(inner_r, piece, zero)
            if s == 0:
                piece = jnp.where(inner_d, piece, zero)
            corner = jnp.dot(piece, corner_w[s, q], preferred_element_type=F32)
            value = jnp.maximum(value, ends[s, q] + spread(corner, col))
        peak[...] = value
        pooled = jnp.maximum(peak[pl.ds(0, 64, stride=2), :], peak[pl.ds(1, 64, stride=2), :])
        pooled = jnp.maximum(pooled, 0.0).astype(BF16)
        for k in range(8):
            out[k, q + pr * (1 - 2 * q)] = pooled


def finish(main, c2, c1, e, other):
    vmem = pl.BlockSpec(memory_space=pltpu.VMEM)
    return pl.pallas_call(
        finish_kernel,
        out_shape=jax.ShapeDtypeStruct((8, 2, 64, 128), BF16),
        in_specs=[vmem] * 6 + [pl.BlockSpec(memory_space=pl.ANY)],
        out_specs=vmem,
        scratch_shapes=[pltpu.VMEM((128, 128), F32)],
        compiler_params=pltpu.CompilerParams(vmem_limit_bytes=6 * 1024 * 1024),
    )(*main, c2, c1, e, other)


def coarse_sums(cells, taps, pair, other, add):
    lhs = jnp.concatenate(
        [
            jnp.concatenate([w[m, 9 * a + 3 * b + c] for a in taps for b in range(3)], axis=1)
            for c in range(3)
            for w, m in ((pair, 0), (pair, 1), (other, 1), (other, 0))
        ],
        axis=0,
    )
    count = len(taps)
    for start, size in ((0, 256), (256, 256), (512, 128)):
        if start < 512:
            first = start // 64 + 1
            blocks = [
                cells[i, first + b : first + b + 4].reshape(256, 128) for i in range(count) for b in range(3)
            ]
        else:
            blocks = [
                jnp.concatenate([cells[i, 9 + b], cells[i, b]], axis=0) for i in range(count) for b in range(3)
            ]
        rhs = jnp.concatenate(blocks, axis=1)
        term = lax.dot_general(lhs, rhs, (((1,), (1,)), ((), ())), preferred_element_type=F32)
        lane = lax.rem(lax.broadcasted_iota(jnp.int32, (64, size), 1), 64)
        left = jnp.where(lane == 0, 0.0, pltpu.roll(term[:64], 1, 1))
        right = jnp.where(lane == 63, 0.0, pltpu.roll(term[128:], size - 1, 1))
        add(start, size, term[64:128] + left + right)


def coarse_kernel(both, pair, other, out, cells):
    pd = lax.rem(lax.axis_index("depth"), 2)
    inner_d = inner("depth")
    for a in range(2):
        for i in (0, 1, 10, 11):
            cells[a, i] = jnp.zeros((64, 128), BF16)
    for k in range(4):
        far = both[pd, k]
        cells[0, 2 + 2 * k : 4 + 2 * k] = jnp.where(inner_d, far, jnp.zeros_like(far))
        cells[1, 2 + 2 * k : 4 + 2 * k] = both[1 - pd, k]

    def put(start, size, value):
        out[:, start : start + size] = value

    coarse_sums(cells, (2 * pd, 1), pair, other, put)


def coarse_level(both, pair, other):
    vmem = pl.BlockSpec(memory_space=pltpu.VMEM)
    return pl.pallas_call(
        coarse_kernel,
        out_shape=jax.ShapeDtypeStruct((64, 640), F32),
        in_specs=[vmem] * 3,
        out_specs=vmem,
        scratch_shapes=[pltpu.VMEM((2, 12, 64, 128), BF16)],
        compiler_params=pltpu.CompilerParams(vmem_limit_bytes=6 * 1024 * 1024),
        cost_estimate=pl.CostEstimate(flops=150_000_000, bytes_accessed=0, transcendentals=0),
    )(both, pair, other)


def near_kernel(near, sums, pair, other, o0, o1, o2, o3, cells):
    pd = lax.rem(lax.axis_index("depth"), 2)
    for i in (0, 1, 10, 11):
        cells[0, i] = jnp.zeros((64, 128), BF16)
    for k in range(4):
        cells[0, 2 + 2 * k : 4 + 2 * k] = near[k]

    def put(start, size, value):
        value = value + sums[:, start : start + size]
        for k, out in enumerate((o0, o1, o2, o3)):
            out[:, start : start + size] = value[16 * k : 16 * k + 16]

    coarse_sums(cells, (2 - 2 * pd,), pair, other, put)


def near_level(near, sums, pair, other):
    vmem = pl.BlockSpec(memory_space=pltpu.VMEM)
    return pl.pallas_call(
        near_kernel,
        out_shape=[jax.ShapeDtypeStruct((16, 640), F32)] * 4,
        in_specs=[vmem] * 4,
        out_specs=[vmem] * 4,
        scratch_shapes=[pltpu.VMEM((1, 12, 64, 128), BF16)],
        compiler_params=pltpu.CompilerParams(vmem_limit_bytes=6 * 1024 * 1024),
    )(near, sums, pair, other)


def join_kernel(s0, s2, s3, s1, bias, out, held):
    y = lax.div(lax.axis_index("rows"), 4)
    for k, part in enumerate((s0, s1, s2, s3)):
        held[y ^ k] = part[...]
    low = lax.broadcasted_iota(jnp.int32, (16, 128), 1) < 64
    for m in range(4):
        tiles = [held[m, :, 128 * i : 128 * i + 128] for i in range(4)]
        if m > 0:
            tiles[0] = tiles[0] + jnp.where(low, held[m - 1, :, 512:], 0.0)
        if m < 3:
            tiles[3] = tiles[3] + jnp.where(low, 0.0, held[m + 1, :, 512:])
        for i in range(4):
            value = jnp.maximum(tiles[i] + bias[...], 0.0).astype(BF16)
            out[:, 512 * m + 128 * i : 512 * m + 128 * i + 128] = value


def join(parts, bias):
    vmem = pl.BlockSpec(memory_space=pltpu.VMEM)
    return pl.pallas_call(
        join_kernel,
        out_shape=jax.ShapeDtypeStruct((16, 2048), BF16),
        in_specs=[vmem] * 5,
        out_specs=vmem,
        scratch_shapes=[pltpu.VMEM((4, 16, 640), F32)],
        compiler_params=pltpu.CompilerParams(vmem_limit_bytes=4 * 1024 * 1024),
    )(*parts, bias)


def body(volume, fine_filters, fine_bias, coarse_filters, coarse_bias):
    d = lax.axis_index("depth")
    r = lax.axis_index("rows")
    pd = lax.rem(d, 2)
    pr = lax.rem(r, 2)
    depth_near, depth_far = near_pairs(16), far_pairs(16)
    rows_near, rows_far = near_pairs(16), far_pairs(16)

    x2 = lax.ppermute(far_plane(volume), "depth", depth_far)
    x1 = lax.ppermute(lax.dynamic_index_in_dim(volume, 1 - pd, 0, False), "depth", depth_near)
    r2 = lax.ppermute(lax.dynamic_index_in_dim(volume, 3 * pr, 1, False), "rows", rows_far)
    r1 = lax.ppermute(lax.dynamic_index_in_dim(volume, 3 - 3 * pr, 1, False), "rows", rows_near)
    far_row = lax.dynamic_index_in_dim(x2, 3 * pr, 0, False)
    near_row = lax.dynamic_index_in_dim(x2, 3 - 3 * pr, 0, False)
    c2 = lax.ppermute(far_row, "rows", rows_far)
    c1 = lax.ppermute(near_row, "rows", rows_near)
    e = lax.ppermute(outer_rows(far_row, near_row, r2, r1), "depth", depth_near)

    def along_y(k):
        return [(i, i ^ (4 * k)) for i in range(16)]

    w = jnp.transpose(coarse_filters, (0, 1, 2, 4, 3)).reshape(27, 16, 128)
    pair = jnp.stack([w, lax.ppermute(w, "rows", along_y(1))])
    other = lax.ppermute(pair, "rows", along_y(3))
    main = fine_level(volume, x2, x1, r2, r1, fine_filters, fine_bias.reshape(1, 128))
    pooled = finish(main, c2, c1, e, other)

    both = lax.all_to_all(
        pooled, ("depth", "rows"), 0, 0, axis_index_groups=far_and_z(), tiled=True
    ).reshape(2, 4, 2, 64, 128)
    near = lax.ppermute(lax.dynamic_index_in_dim(both, 1 - pd, 0, False), "depth", depth_near)
    sums = near_level(near, coarse_level(both, pair, other), pair, other)
    parts = [sums[0]] + [lax.ppermute(sums[k], "rows", along_y(k)) for k in (2, 3, 1)]
    result = join(parts, jnp.broadcast_to(coarse_bias[:, None], (16, 128)))
    return result.reshape(16, 1, 2048)


def solution(mesh):
    placed = (
        P("depth", "rows", None, None),
        P(),
        P(),
        P(None, None, None, None, "rows"),
        P("rows"),
    )
    return jax.shard_map(
        body, mesh=mesh, in_specs=placed, out_specs=P("rows", "depth", None), check_vma=False
    )
```

```python
import jax
import jax.numpy as jnp
from jax import lax
from jax.experimental import pallas as pl
from jax.experimental.pallas import tpu as pltpu
from jax.sharding import PartitionSpec as P

BF16 = jnp.bfloat16
F32 = jnp.float32


def near_pairs(count):
    return [(i, i ^ 1) for i in range(count)]


def far_pairs(count):
    return [(i, min(max(((i - 1) ^ 1) + 1, 0), count - 1)) for i in range(count)]


def far_and_z():
    pairs = [(d, d + 1) for d in range(1, 15, 2)] + [(15, 0)]
    return [[d * 16 + 4 * y + z for d in pair for z in range(4)] for pair in pairs for y in range(4)]


def inner(axis):
    i = lax.axis_index(axis)
    return (i > 0) & (i < 15)


def spread(line, col):
    left = jnp.where(col == 0, 0.0, pltpu.roll(line[:, :128], 1, 0))
    right = jnp.where(col == 127, 0.0, pltpu.roll(line[:, 256:], 127, 0))
    return line[:, 128:256] + left + right


def fine_kernel(vol, x2, x1, r2, r1, w, bias, ends, best, corner_w, cells):
    pd = lax.rem(lax.axis_index("depth"), 2)
    pr = lax.rem(lax.axis_index("rows"), 2)
    inner_d = inner("depth")
    inner_r = inner("rows")
    zero = jnp.zeros((128, 128), BF16)
    for j in range(4):
        for i in range(6):
            row = (i - 1) + pr * (5 - 2 * i)
            if j in (1, 2):
                plane = (j - 1) + pd * (3 - 2 * j)
                piece = r2[plane] if i == 0 else r1[plane] if i == 5 else vol[plane, row]
            elif i in (0, 5):
                piece = zero
            else:
                piece = (x2 if j == 0 else x1)[row]
            if i == 0:
                piece = jnp.where(inner_r, piece, zero)
            if j == 0:
                piece = jnp.where(inner_d, piece, zero)
            cells[j, i] = piece
    taps = [(a, b) for a in range(3) for b in range(3)]
    groups = [taps[i : i + 2] for i in range(0, 9, 2)]
    col = lax.broadcasted_iota(jnp.int32, (128, 128), 0)
    for s in range(2):
        total = None
        for group in groups:
            lhs = jnp.concatenate(
                [cells[s + a, b : b + 4].reshape(512, 128) for a, b in group], axis=1
            )
            rhs = jnp.concatenate(
                [
                    jnp.concatenate(
                        [w[a + pd * (2 - 2 * a), b + pr * (2 - 2 * b), c] for c in range(3)], axis=1
                    )
                    for a, b in group
                ],
                axis=0,
            )
            term = jnp.dot(lhs, rhs, preferred_element_type=F32)
            total = term if total is None else total + term
        for q in range(2):
            ends[s, q] = spread(total[3 * q * 128 : (3 * q + 1) * 128], col) + bias[...]
            middle = spread(total[(q + 1) * 128 : (q + 2) * 128], col) + bias[...]
            best[q] = middle if s == 0 else jnp.maximum(best[q], middle)
            a, b = 2 * s, 2 * q
            for c in range(3):
                corner_w[s, q, :, 128 * c : 128 * c + 128] = w[a + pd * (2 - 2 * a), b + pr * (2 - 2 * b), c]


def fine_level(vol, x2, x1, r2, r1, w, bias):
    vmem = pl.BlockSpec(memory_space=pltpu.VMEM)
    return pl.pallas_call(
        fine_kernel,
        out_shape=[
            jax.ShapeDtypeStruct((2, 2, 128, 128), F32),
            jax.ShapeDtypeStruct((2, 128, 128), F32),
            jax.ShapeDtypeStruct((2, 2, 128, 384), BF16),
        ],
        in_specs=[vmem] * 7,
        out_specs=[vmem] * 3,
        scratch_shapes=[pltpu.VMEM((4, 6, 128, 128), BF16)],
        compiler_params=pltpu.CompilerParams(vmem_limit_bytes=12 * 1024 * 1024),
        cost_estimate=pl.CostEstimate(flops=20_000_000_000, bytes_accessed=0, transcendentals=0),
    )(vol, x2, x1, r2, r1, w, bias)


def outer_kernel(far_row, near_row, r2, r1, out):
    pd = lax.rem(lax.axis_index("depth"), 2)
    out[0] = r2[1 - pd]
    out[1] = r1[1 - pd]


def outer_rows(far_row, near_row, r2, r1):
    vmem = pl.BlockSpec(memory_space=pltpu.VMEM)
    return pl.pallas_call(
        outer_kernel,
        out_shape=jax.ShapeDtypeStruct((2, 128, 128), BF16),
        in_specs=[pl.BlockSpec(memory_space=pl.ANY)] * 2 + [vmem] * 2,
        out_specs=vmem,
        compiler_params=pltpu.CompilerParams(vmem_limit_bytes=2 * 1024 * 1024),
    )(far_row, near_row, r2, r1)


def finish_kernel(ends, best, corner_w, c2, c1, e, other, out, peak):
    pr = lax.rem(lax.axis_index("rows"), 2)
    inner_d = inner("depth")
    inner_r = inner("rows")
    zero = jnp.zeros((128, 128), BF16)
    col = lax.broadcasted_iota(jnp.int32, (128, 128), 0)
    for q in range(2):
        value = best[q]
        for s in range(2):
            piece = e[q] if s == 1 else (c2, c1)[q][...]
            if q == 0:
                piece = jnp.where(inner_r, piece, zero)
            if s == 0:
                piece = jnp.where(inner_d, piece, zero)
            corner = jnp.dot(piece, corner_w[s, q], preferred_element_type=F32)
            value = jnp.maximum(value, ends[s, q] + spread(corner, col))
        peak[...] = value
        pooled = jnp.maximum(peak[pl.ds(0, 64, stride=2), :], peak[pl.ds(1, 64, stride=2), :])
        pooled = jnp.maximum(pooled, 0.0).astype(BF16)
        for k in range(8):
            out[k, q + pr * (1 - 2 * q)] = pooled


def finish(main, c2, c1, e, other):
    vmem = pl.BlockSpec(memory_space=pltpu.VMEM)
    return pl.pallas_call(
        finish_kernel,
        out_shape=jax.ShapeDtypeStruct((8, 2, 64, 128), BF16),
        in_specs=[vmem] * 6 + [pl.BlockSpec(memory_space=pl.ANY)],
        out_specs=vmem,
        scratch_shapes=[pltpu.VMEM((128, 128), F32)],
        compiler_params=pltpu.CompilerParams(vmem_limit_bytes=6 * 1024 * 1024),
    )(*main, c2, c1, e, other)


def coarse_sums(cells, taps, pair, other, add):
    lhs = jnp.concatenate(
        [
            jnp.concatenate([w[m, 9 * a + 3 * b + c] for a in taps for b in range(3)], axis=1)
            for c in range(3)
            for w, m in ((pair, 0), (pair, 1), (other, 1), (other, 0))
        ],
        axis=0,
    )
    count = len(taps)
    for start, size in ((0, 256), (256, 256), (512, 128)):
        if start < 512:
            first = start // 64 + 1
            blocks = [
                cells[i, first + b : first + b + 4].reshape(256, 128) for i in range(count) for b in range(3)
            ]
        else:
            blocks = [
                jnp.concatenate([cells[i, 9 + b], cells[i, b]], axis=0) for i in range(count) for b in range(3)
            ]
        rhs = jnp.concatenate(blocks, axis=1)
        term = lax.dot_general(lhs, rhs, (((1,), (1,)), ((), ())), preferred_element_type=F32)
        lane = lax.rem(lax.broadcasted_iota(jnp.int32, (64, size), 1), 64)
        left = jnp.where(lane == 0, 0.0, pltpu.roll(term[:64], 1, 1))
        right = jnp.where(lane == 63, 0.0, pltpu.roll(term[128:], size - 1, 1))
        add(start, size, term[64:128] + left + right)


def coarse_kernel(both, pair, other, out, cells):
    pd = lax.rem(lax.axis_index("depth"), 2)
    inner_d = inner("depth")
    for a in range(2):
        for i in (0, 1, 10, 11):
            cells[a, i] = jnp.zeros((64, 128), BF16)
    for k in range(4):
        far = both[pd, k]
        cells[0, 2 + 2 * k : 4 + 2 * k] = jnp.where(inner_d, far, jnp.zeros_like(far))
        cells[1, 2 + 2 * k : 4 + 2 * k] = both[1 - pd, k]

    def put(start, size, value):
        out[:, start : start + size] = value

    coarse_sums(cells, (2 * pd, 1), pair, other, put)


def coarse_level(both, pair, other):
    vmem = pl.BlockSpec(memory_space=pltpu.VMEM)
    return pl.pallas_call(
        coarse_kernel,
        out_shape=jax.ShapeDtypeStruct((64, 640), F32),
        in_specs=[vmem] * 3,
        out_specs=vmem,
        scratch_shapes=[pltpu.VMEM((2, 12, 64, 128), BF16)],
        compiler_params=pltpu.CompilerParams(vmem_limit_bytes=6 * 1024 * 1024),
        cost_estimate=pl.CostEstimate(flops=150_000_000, bytes_accessed=0, transcendentals=0),
    )(both, pair, other)


def near_kernel(near, sums, pair, other, o0, o1, o2, o3, cells):
    pd = lax.rem(lax.axis_index("depth"), 2)
    for i in (0, 1, 10, 11):
        cells[0, i] = jnp.zeros((64, 128), BF16)
    for k in range(4):
        cells[0, 2 + 2 * k : 4 + 2 * k] = near[k]

    def put(start, size, value):
        value = value + sums[:, start : start + size]
        for k, out in enumerate((o0, o1, o2, o3)):
            out[:, start : start + size] = value[16 * k : 16 * k + 16]

    coarse_sums(cells, (2 - 2 * pd,), pair, other, put)


def near_level(near, sums, pair, other):
    vmem = pl.BlockSpec(memory_space=pltpu.VMEM)
    return pl.pallas_call(
        near_kernel,
        out_shape=[jax.ShapeDtypeStruct((16, 640), F32)] * 4,
        in_specs=[vmem] * 4,
        out_specs=[vmem] * 4,
        scratch_shapes=[pltpu.VMEM((1, 12, 64, 128), BF16)],
        compiler_params=pltpu.CompilerParams(vmem_limit_bytes=6 * 1024 * 1024),
    )(near, sums, pair, other)


def join_kernel(s0, s2, s3, s1, bias, out, held):
    y = lax.div(lax.axis_index("rows"), 4)
    for k, part in enumerate((s0, s1, s2, s3)):
        held[y ^ k] = part[...]
    low = lax.broadcasted_iota(jnp.int32, (16, 128), 1) < 64
    for m in range(4):
        tiles = [held[m, :, 128 * i : 128 * i + 128] for i in range(4)]
        if m > 0:
            tiles[0] = tiles[0] + jnp.where(low, held[m - 1, :, 512:], 0.0)
        if m < 3:
            tiles[3] = tiles[3] + jnp.where(low, 0.0, held[m + 1, :, 512:])
        for i in range(4):
            value = jnp.maximum(tiles[i] + bias[...], 0.0).astype(BF16)
            out[:, 512 * m + 128 * i : 512 * m + 128 * i + 128] = value


def join(parts, bias):
    vmem = pl.BlockSpec(memory_space=pltpu.VMEM)
    return pl.pallas_call(
        join_kernel,
        out_shape=jax.ShapeDtypeStruct((16, 2048), BF16),
        in_specs=[vmem] * 5,
        out_specs=vmem,
        scratch_shapes=[pltpu.VMEM((4, 16, 640), F32)],
        compiler_params=pltpu.CompilerParams(vmem_limit_bytes=4 * 1024 * 1024),
    )(*parts, bias)


def body(volume, fine_filters, fine_bias, coarse_filters, coarse_bias):
    d = lax.axis_index("depth")
    r = lax.axis_index("rows")
    pd = lax.rem(d, 2)
    pr = lax.rem(r, 2)
    depth_near, depth_far = near_pairs(16), far_pairs(16)
    rows_near, rows_far = near_pairs(16), far_pairs(16)

    x2 = lax.ppermute(lax.dynamic_index_in_dim(volume, pd, 0, False), "depth", depth_far)
    x1 = lax.ppermute(lax.dynamic_index_in_dim(volume, 1 - pd, 0, False), "depth", depth_near)
    r2 = lax.ppermute(lax.dynamic_index_in_dim(volume, 3 * pr, 1, False), "rows", rows_far)
    r1 = lax.ppermute(lax.dynamic_index_in_dim(volume, 3 - 3 * pr, 1, False), "rows", rows_near)
    sides = jnp.stack([x2, x1])
    far_row = lax.dynamic_index_in_dim(sides, 3 * pr, 1, False)[0]
    near_row = lax.dynamic_index_in_dim(sides, 3 - 3 * pr, 1, False)[0]
    c2 = lax.ppermute(far_row, "rows", rows_far)
    c1 = lax.ppermute(near_row, "rows", rows_near)
    e = lax.ppermute(outer_rows(far_row, near_row, r2, r1), "depth", depth_near)

    def along_y(k):
        return [(i, i ^ (4 * k)) for i in range(16)]

    w = jnp.transpose(coarse_filters, (0, 1, 2, 4, 3)).reshape(27, 16, 128)
    pair = jnp.stack([w, lax.ppermute(w, "rows", along_y(1))])
    other = lax.ppermute(pair, "rows", along_y(3))
    main = fine_level(volume, x2, x1, r2, r1, fine_filters, fine_bias.reshape(1, 128))
    pooled = finish(main, c2, c1, e, other)

    both = lax.all_to_all(
        pooled, ("depth", "rows"), 0, 0, axis_index_groups=far_and_z(), tiled=True
    ).reshape(2, 4, 2, 64, 128)
    near = lax.ppermute(lax.dynamic_index_in_dim(both, 1 - pd, 0, False), "depth", depth_near)
    sums = near_level(near, coarse_level(both, pair, other), pair, other)
    parts = [sums[0]] + [lax.ppermute(sums[k], "rows", along_y(k)) for k in (2, 3, 1)]
    result = join(parts, jnp.broadcast_to(coarse_bias[:, None], (16, 128)))
    return result.reshape(16, 1, 2048)


def solution(mesh):
    placed = (
        P("depth", "rows", None, None),
        P(),
        P(),
        P(None, None, None, None, "rows"),
        P("rows"),
    )
    return jax.shard_map(
        body, mesh=mesh, in_specs=placed, out_specs=P("rows", "depth", None), check_vma=False
    )
```

```python
import jax
import jax.numpy as jnp
from jax import lax
from jax.experimental import pallas as pl
from jax.experimental.pallas import tpu as pltpu
from jax.sharding import PartitionSpec as P

BF16 = jnp.bfloat16
F32 = jnp.float32


def near_pairs(count):
    return [(i, i ^ 1) for i in range(count)]


def far_pairs(count):
    return [(i, min(max(((i - 1) ^ 1) + 1, 0), count - 1)) for i in range(count)]


def far_and_z():
    pairs = [(d, d + 1) for d in range(1, 15, 2)] + [(15, 0)]
    return [[d * 16 + 4 * y + z for d in pair for z in range(4)] for pair in pairs for y in range(4)]


def inner(axis):
    i = lax.axis_index(axis)
    return (i > 0) & (i < 15)


def spread(line, col):
    left = jnp.where(col == 0, 0.0, pltpu.roll(line[:, :128], 1, 0))
    right = jnp.where(col == 127, 0.0, pltpu.roll(line[:, 256:], 127, 0))
    return line[:, 128:256] + left + right


def fine_kernel(vol, x2, x1, r2, r1, w, bias, ends, best, corner_w, cells):
    pd = lax.rem(lax.axis_index("depth"), 2)
    pr = lax.rem(lax.axis_index("rows"), 2)
    inner_d = inner("depth")
    inner_r = inner("rows")
    zero = jnp.zeros((128, 128), BF16)
    for j in range(4):
        for i in range(6):
            row = (i - 1) + pr * (5 - 2 * i)
            if j in (1, 2):
                plane = (j - 1) + pd * (3 - 2 * j)
                piece = r2[plane] if i == 0 else r1[plane] if i == 5 else vol[plane, row]
            elif i in (0, 5):
                piece = zero
            else:
                piece = (x2 if j == 0 else x1)[row]
            if i == 0:
                piece = jnp.where(inner_r, piece, zero)
            if j == 0:
                piece = jnp.where(inner_d, piece, zero)
            cells[j, i] = piece
    taps = [(a, b) for a in range(3) for b in range(3)]
    groups = [taps[i : i + 2] for i in range(0, 9, 2)]
    col = lax.broadcasted_iota(jnp.int32, (128, 128), 0)
    for s in range(2):
        total = None
        for group in groups:
            lhs = jnp.concatenate(
                [cells[s + a, b : b + 4].reshape(512, 128) for a, b in group], axis=1
            )
            rhs = jnp.concatenate(
                [
                    jnp.concatenate(
                        [w[a + pd * (2 - 2 * a), b + pr * (2 - 2 * b), c] for c in range(3)], axis=1
                    )
                    for a, b in group
                ],
                axis=0,
            )
            term = jnp.dot(lhs, rhs, preferred_element_type=F32)
            total = term if total is None else total + term
        for q in range(2):
            ends[s, q] = spread(total[3 * q * 128 : (3 * q + 1) * 128], col) + bias[:1]
            middle = spread(total[(q + 1) * 128 : (q + 2) * 128], col) + bias[:1]
            best[q] = middle if s == 0 else jnp.maximum(best[q], middle)
            a, b = 2 * s, 2 * q
            for c in range(3):
                corner_w[s, q, :, 128 * c : 128 * c + 128] = w[a + pd * (2 - 2 * a), b + pr * (2 - 2 * b), c]


def fine_level(vol, x2, x1, r2, r1, w, bias):
    vmem = pl.BlockSpec(memory_space=pltpu.VMEM)
    return pl.pallas_call(
        fine_kernel,
        out_shape=[
            jax.ShapeDtypeStruct((2, 2, 128, 128), F32),
            jax.ShapeDtypeStruct((2, 128, 128), F32),
            jax.ShapeDtypeStruct((2, 2, 128, 384), BF16),
        ],
        in_specs=[vmem] * 7,
        out_specs=[vmem] * 3,
        scratch_shapes=[pltpu.VMEM((4, 6, 128, 128), BF16)],
        compiler_params=pltpu.CompilerParams(vmem_limit_bytes=12 * 1024 * 1024),
        cost_estimate=pl.CostEstimate(flops=20_000_000_000, bytes_accessed=0, transcendentals=0),
    )(vol, x2, x1, r2, r1, w, bias)


def outer_kernel(far_row, near_row, r2, r1, out):
    pd = lax.rem(lax.axis_index("depth"), 2)
    out[0] = r2[1 - pd]
    out[1] = r1[1 - pd]


def outer_rows(far_row, near_row, r2, r1):
    vmem = pl.BlockSpec(memory_space=pltpu.VMEM)
    return pl.pallas_call(
        outer_kernel,
        out_shape=jax.ShapeDtypeStruct((2, 128, 128), BF16),
        in_specs=[pl.BlockSpec(memory_space=pl.ANY)] * 2 + [vmem] * 2,
        out_specs=vmem,
        compiler_params=pltpu.CompilerParams(vmem_limit_bytes=2 * 1024 * 1024),
    )(far_row, near_row, r2, r1)


def finish_kernel(ends, best, corner_w, c2, c1, e, other, out, peak):
    pr = lax.rem(lax.axis_index("rows"), 2)
    inner_d = inner("depth")
    inner_r = inner("rows")
    zero = jnp.zeros((128, 128), BF16)
    col = lax.broadcasted_iota(jnp.int32, (128, 128), 0)
    for q in range(2):
        value = best[q]
        for s in range(2):
            piece = e[q] if s == 1 else (c2, c1)[q][...]
            if q == 0:
                piece = jnp.where(inner_r, piece, zero)
            if s == 0:
                piece = jnp.where(inner_d, piece, zero)
            corner = jnp.dot(piece, corner_w[s, q], preferred_element_type=F32)
            value = jnp.maximum(value, ends[s, q] + spread(corner, col))
        peak[...] = value
        pooled = jnp.maximum(peak[pl.ds(0, 64, stride=2), :], peak[pl.ds(1, 64, stride=2), :])
        pooled = jnp.maximum(pooled, 0.0).astype(BF16)
        for k in range(8):
            out[k, q + pr * (1 - 2 * q)] = pooled


def finish(main, c2, c1, e, other):
    vmem = pl.BlockSpec(memory_space=pltpu.VMEM)
    return pl.pallas_call(
        finish_kernel,
        out_shape=jax.ShapeDtypeStruct((8, 2, 64, 128), BF16),
        in_specs=[vmem] * 6 + [pl.BlockSpec(memory_space=pl.ANY)],
        out_specs=vmem,
        scratch_shapes=[pltpu.VMEM((128, 128), F32)],
        compiler_params=pltpu.CompilerParams(vmem_limit_bytes=6 * 1024 * 1024),
    )(*main, c2, c1, e, other)


def coarse_sums(cells, taps, pair, other, add):
    lhs = jnp.concatenate(
        [
            jnp.concatenate([w[m, 9 * a + 3 * b + c] for a in taps for b in range(3)], axis=1)
            for c in range(3)
            for w, m in ((pair, 0), (pair, 1), (other, 1), (other, 0))
        ],
        axis=0,
    )
    count = len(taps)
    for start, size in ((0, 256), (256, 256), (512, 128)):
        if start < 512:
            first = start // 64 + 1
            blocks = [
                cells[i, first + b : first + b + 4].reshape(256, 128) for i in range(count) for b in range(3)
            ]
        else:
            blocks = [
                jnp.concatenate([cells[i, 9 + b], cells[i, b]], axis=0) for i in range(count) for b in range(3)
            ]
        rhs = jnp.concatenate(blocks, axis=1)
        term = lax.dot_general(lhs, rhs, (((1,), (1,)), ((), ())), preferred_element_type=F32)
        lane = lax.rem(lax.broadcasted_iota(jnp.int32, (64, size), 1), 64)
        left = jnp.where(lane == 0, 0.0, pltpu.roll(term[:64], 1, 1))
        right = jnp.where(lane == 63, 0.0, pltpu.roll(term[128:], size - 1, 1))
        add(start, size, term[64:128] + left + right)


def coarse_kernel(both, pair, other, out, cells):
    pd = lax.rem(lax.axis_index("depth"), 2)
    inner_d = inner("depth")
    for a in range(2):
        for i in (0, 1, 10, 11):
            cells[a, i] = jnp.zeros((64, 128), BF16)
    for k in range(4):
        far = both[pd, k]
        cells[0, 2 + 2 * k : 4 + 2 * k] = jnp.where(inner_d, far, jnp.zeros_like(far))
        cells[1, 2 + 2 * k : 4 + 2 * k] = both[1 - pd, k]

    def put(start, size, value):
        out[:, start : start + size] = value

    coarse_sums(cells, (2 * pd, 1), pair, other, put)


def coarse_level(both, pair, other):
    vmem = pl.BlockSpec(memory_space=pltpu.VMEM)
    return pl.pallas_call(
        coarse_kernel,
        out_shape=jax.ShapeDtypeStruct((64, 640), F32),
        in_specs=[vmem] * 3,
        out_specs=vmem,
        scratch_shapes=[pltpu.VMEM((2, 12, 64, 128), BF16)],
        compiler_params=pltpu.CompilerParams(vmem_limit_bytes=6 * 1024 * 1024),
        cost_estimate=pl.CostEstimate(flops=150_000_000, bytes_accessed=0, transcendentals=0),
    )(both, pair, other)


def near_kernel(near, sums, pair, other, o0, o1, o2, o3, cells):
    pd = lax.rem(lax.axis_index("depth"), 2)
    for i in (0, 1, 10, 11):
        cells[0, i] = jnp.zeros((64, 128), BF16)
    for k in range(4):
        cells[0, 2 + 2 * k : 4 + 2 * k] = near[k]

    def put(start, size, value):
        value = value + sums[:, start : start + size]
        for k, out in enumerate((o0, o1, o2, o3)):
            out[:, start : start + size] = value[16 * k : 16 * k + 16]

    coarse_sums(cells, (2 - 2 * pd,), pair, other, put)


def near_level(near, sums, pair, other):
    vmem = pl.BlockSpec(memory_space=pltpu.VMEM)
    return pl.pallas_call(
        near_kernel,
        out_shape=[jax.ShapeDtypeStruct((16, 640), F32)] * 4,
        in_specs=[vmem] * 4,
        out_specs=[vmem] * 4,
        scratch_shapes=[pltpu.VMEM((1, 12, 64, 128), BF16)],
        compiler_params=pltpu.CompilerParams(vmem_limit_bytes=6 * 1024 * 1024),
    )(near, sums, pair, other)


def join_kernel(s0, s2, s3, s1, bias, out, held):
    y = lax.div(lax.axis_index("rows"), 4)
    for k, part in enumerate((s0, s1, s2, s3)):
        held[y ^ k] = part[...]
    low = lax.broadcasted_iota(jnp.int32, (16, 128), 1) < 64
    for m in range(4):
        tiles = [held[m, :, 128 * i : 128 * i + 128] for i in range(4)]
        if m > 0:
            tiles[0] = tiles[0] + jnp.where(low, held[m - 1, :, 512:], 0.0)
        if m < 3:
            tiles[3] = tiles[3] + jnp.where(low, 0.0, held[m + 1, :, 512:])
        for i in range(4):
            value = jnp.maximum(tiles[i] + bias[...], 0.0).astype(BF16)
            out[:, 512 * m + 128 * i : 512 * m + 128 * i + 128] = value


def join(parts, bias):
    vmem = pl.BlockSpec(memory_space=pltpu.VMEM)
    return pl.pallas_call(
        join_kernel,
        out_shape=jax.ShapeDtypeStruct((16, 2048), BF16),
        in_specs=[vmem] * 5,
        out_specs=vmem,
        scratch_shapes=[pltpu.VMEM((4, 16, 640), F32)],
        compiler_params=pltpu.CompilerParams(vmem_limit_bytes=4 * 1024 * 1024),
    )(*parts, bias)


def body(volume, fine_filters, fine_bias, coarse_filters, coarse_bias):
    d = lax.axis_index("depth")
    r = lax.axis_index("rows")
    pd = lax.rem(d, 2)
    pr = lax.rem(r, 2)
    depth_near, depth_far = near_pairs(16), far_pairs(16)
    rows_near, rows_far = near_pairs(16), far_pairs(16)

    x2 = lax.ppermute(lax.dynamic_index_in_dim(volume, pd, 0, False), "depth", depth_far)
    x1 = lax.ppermute(lax.dynamic_index_in_dim(volume, 1 - pd, 0, False), "depth", depth_near)
    r2 = lax.ppermute(lax.dynamic_index_in_dim(volume, 3 * pr, 1, False), "rows", rows_far)
    r1 = lax.ppermute(lax.dynamic_index_in_dim(volume, 3 - 3 * pr, 1, False), "rows", rows_near)
    sides = jnp.stack([x2, x1])
    far_row = lax.dynamic_index_in_dim(sides, 3 * pr, 1, False)[0]
    near_row = lax.dynamic_index_in_dim(sides, 3 - 3 * pr, 1, False)[0]
    c2 = lax.ppermute(far_row, "rows", rows_far)
    c1 = lax.ppermute(near_row, "rows", rows_near)
    e = lax.ppermute(outer_rows(far_row, near_row, r2, r1), "depth", depth_near)

    def along_y(k):
        return [(i, i ^ (4 * k)) for i in range(16)]

    w = jnp.transpose(coarse_filters, (0, 1, 2, 4, 3)).reshape(27, 16, 128)
    pair = jnp.stack([w, lax.ppermute(w, "rows", along_y(1))])
    other = lax.ppermute(pair, "rows", along_y(3))
    main = fine_level(volume, x2, x1, r2, r1, fine_filters, jnp.broadcast_to(fine_bias, (8, 128)))
    pooled = finish(main, c2, c1, e, other)

    both = lax.all_to_all(
        pooled, ("depth", "rows"), 0, 0, axis_index_groups=far_and_z(), tiled=True
    ).reshape(2, 4, 2, 64, 128)
    near = lax.ppermute(lax.dynamic_index_in_dim(both, 1 - pd, 0, False), "depth", depth_near)
    sums = near_level(near, coarse_level(both, pair, other), pair, other)
    parts = [sums[0]] + [lax.ppermute(sums[k], "rows", along_y(k)) for k in (2, 3, 1)]
    result = join(parts, jnp.broadcast_to(coarse_bias[:, None], (16, 128)))
    return result.reshape(16, 1, 2048)


def solution(mesh):
    placed = (
        P("depth", "rows", None, None),
        P(),
        P(),
        P(None, None, None, None, "rows"),
        P("rows"),
    )
    return jax.shard_map(
        body, mesh=mesh, in_specs=placed, out_specs=P("rows", "depth", None), check_vma=False
    )
```

```python
import jax
import jax.numpy as jnp
from jax import lax
from jax.experimental import pallas as pl
from jax.experimental.pallas import tpu as pltpu
from jax.sharding import PartitionSpec as P

BF16 = jnp.bfloat16
F32 = jnp.float32


def near_pairs(count):
    return [(i, i ^ 1) for i in range(count)]


def far_pairs(count):
    return [(i, min(max(((i - 1) ^ 1) + 1, 0), count - 1)) for i in range(count)]


def far_and_z():
    pairs = [(d, d + 1) for d in range(1, 15, 2)] + [(15, 0)]
    return [[d * 16 + 4 * y + z for d in pair for z in range(4)] for pair in pairs for y in range(4)]


def inner(axis):
    i = lax.axis_index(axis)
    return (i > 0) & (i < 15)


def spread(line, col):
    left = jnp.where(col == 0, 0.0, pltpu.roll(line[:, :128], 1, 0))
    right = jnp.where(col == 127, 0.0, pltpu.roll(line[:, 256:], 127, 0))
    return line[:, 128:256] + left + right


def fine_kernel(vol, x2, x1, r2, r1, w, bias, ends, best, corner_w, cells):
    pd = lax.rem(lax.axis_index("depth"), 2)
    pr = lax.rem(lax.axis_index("rows"), 2)
    inner_d = inner("depth")
    inner_r = inner("rows")
    zero = jnp.zeros((128, 128), BF16)
    for j in range(4):
        for i in range(6):
            row = (i - 1) + pr * (5 - 2 * i)
            if j in (1, 2):
                plane = (j - 1) + pd * (3 - 2 * j)
                piece = r2[plane] if i == 0 else r1[plane] if i == 5 else vol[plane, row]
            elif i in (0, 5):
                piece = zero
            else:
                piece = (x2 if j == 0 else x1)[row]
            if i == 0:
                piece = jnp.where(inner_r, piece, zero)
            if j == 0:
                piece = jnp.where(inner_d, piece, zero)
            cells[j, i] = piece
    taps = [(a, b) for a in range(3) for b in range(3)]
    groups = [taps[i : i + 2] for i in range(0, 9, 2)]
    col = lax.broadcasted_iota(jnp.int32, (128, 128), 0)
    for s in range(2):
        total = None
        for group in groups:
            lhs = jnp.concatenate(
                [cells[s + a, b : b + 4].reshape(512, 128) for a, b in group], axis=1
            )
            rhs = jnp.concatenate(
                [
                    jnp.concatenate(
                        [w[a + pd * (2 - 2 * a), b + pr * (2 - 2 * b), c] for c in range(3)], axis=1
                    )
                    for a, b in group
                ],
                axis=0,
            )
            term = jnp.dot(lhs, rhs, preferred_element_type=F32)
            total = term if total is None else total + term
        for q in range(2):
            ends[s, q] = spread(total[3 * q * 128 : (3 * q + 1) * 128], col) + bias[:1]
            middle = spread(total[(q + 1) * 128 : (q + 2) * 128], col) + bias[:1]
            best[q] = middle if s == 0 else jnp.maximum(best[q], middle)
            a, b = 2 * s, 2 * q
            for c in range(3):
                corner_w[s, q, :, 128 * c : 128 * c + 128] = w[a + pd * (2 - 2 * a), b + pr * (2 - 2 * b), c]


def fine_level(vol, x2, x1, r2, r1, w, bias):
    vmem = pl.BlockSpec(memory_space=pltpu.VMEM)
    return pl.pallas_call(
        fine_kernel,
        out_shape=[
            jax.ShapeDtypeStruct((2, 2, 128, 128), F32),
            jax.ShapeDtypeStruct((2, 128, 128), F32),
            jax.ShapeDtypeStruct((2, 2, 128, 384), BF16),
        ],
        in_specs=[vmem] * 7,
        out_specs=[vmem] * 3,
        scratch_shapes=[pltpu.VMEM((4, 6, 128, 128), BF16)],
        compiler_params=pltpu.CompilerParams(vmem_limit_bytes=12 * 1024 * 1024),
        cost_estimate=pl.CostEstimate(flops=20_000_000_000, bytes_accessed=0, transcendentals=0),
    )(vol, x2, x1, r2, r1, w, bias)


def outer_kernel(far_row, near_row, r2, r1, out):
    pd = lax.rem(lax.axis_index("depth"), 2)
    out[0] = r2[1 - pd]
    out[1] = r1[1 - pd]


def outer_rows(far_row, near_row, r2, r1):
    vmem = pl.BlockSpec(memory_space=pltpu.VMEM)
    return pl.pallas_call(
        outer_kernel,
        out_shape=jax.ShapeDtypeStruct((2, 128, 128), BF16),
        in_specs=[pl.BlockSpec(memory_space=pl.ANY)] * 2 + [vmem] * 2,
        out_specs=vmem,
        compiler_params=pltpu.CompilerParams(vmem_limit_bytes=2 * 1024 * 1024),
    )(far_row, near_row, r2, r1)


def finish_kernel(ends, best, corner_w, c2, c1, e, other, out, peak):
    pr = lax.rem(lax.axis_index("rows"), 2)
    inner_d = inner("depth")
    inner_r = inner("rows")
    zero = jnp.zeros((128, 128), BF16)
    col = lax.broadcasted_iota(jnp.int32, (128, 128), 0)
    for q in range(2):
        value = best[q]
        for s in range(2):
            piece = e[q] if s == 1 else (c2, c1)[q][...]
            if q == 0:
                piece = jnp.where(inner_r, piece, zero)
            if s == 0:
                piece = jnp.where(inner_d, piece, zero)
            corner = jnp.dot(piece, corner_w[s, q], preferred_element_type=F32)
            value = jnp.maximum(value, ends[s, q] + spread(corner, col))
        peak[...] = value
        pooled = jnp.maximum(peak[pl.ds(0, 64, stride=2), :], peak[pl.ds(1, 64, stride=2), :])
        pooled = jnp.maximum(pooled, 0.0).astype(BF16)
        for k in range(8):
            out[k, q + pr * (1 - 2 * q)] = pooled


def finish(main, c2, c1, e, other):
    vmem = pl.BlockSpec(memory_space=pltpu.VMEM)
    return pl.pallas_call(
        finish_kernel,
        out_shape=jax.ShapeDtypeStruct((8, 2, 64, 128), BF16),
        in_specs=[vmem] * 6 + [pl.BlockSpec(memory_space=pl.ANY)],
        out_specs=vmem,
        scratch_shapes=[pltpu.VMEM((128, 128), F32)],
        compiler_params=pltpu.CompilerParams(vmem_limit_bytes=6 * 1024 * 1024),
    )(*main, c2, c1, e, other)


def coarse_sums(cells, taps, pair, other, add):
    lhs = jnp.concatenate(
        [
            jnp.concatenate([w[m, 9 * a + 3 * b + c] for a in taps for b in range(3)], axis=1)
            for c in range(3)
            for w, m in ((pair, 0), (other, 0), (other, 1), (pair, 1))
        ],
        axis=0,
    )
    count = len(taps)
    for start, size in ((0, 256), (256, 256), (512, 128)):
        if start < 512:
            first = start // 64 + 1
            blocks = [
                cells[i, first + b : first + b + 4].reshape(256, 128) for i in range(count) for b in range(3)
            ]
        else:
            blocks = [
                jnp.concatenate([cells[i, 9 + b], cells[i, b]], axis=0) for i in range(count) for b in range(3)
            ]
        rhs = jnp.concatenate(blocks, axis=1)
        term = lax.dot_general(lhs, rhs, (((1,), (1,)), ((), ())), preferred_element_type=F32)
        lane = lax.rem(lax.broadcasted_iota(jnp.int32, (64, size), 1), 64)
        left = jnp.where(lane == 0, 0.0, pltpu.roll(term[:64], 1, 1))
        right = jnp.where(lane == 63, 0.0, pltpu.roll(term[128:], size - 1, 1))
        add(start, size, term[64:128] + left + right)


def coarse_kernel(both, pair, other, out, cells):
    pd = lax.rem(lax.axis_index("depth"), 2)
    inner_d = inner("depth")
    for a in range(2):
        for i in (0, 1, 10, 11):
            cells[a, i] = jnp.zeros((64, 128), BF16)
    for k in range(4):
        far = both[pd, k]
        cells[0, 2 + 2 * k : 4 + 2 * k] = jnp.where(inner_d, far, jnp.zeros_like(far))
        cells[1, 2 + 2 * k : 4 + 2 * k] = both[1 - pd, k]

    def put(start, size, value):
        out[:, start : start + size] = value

    coarse_sums(cells, (2 * pd, 1), pair, other, put)


def coarse_level(both, pair, other):
    vmem = pl.BlockSpec(memory_space=pltpu.VMEM)
    return pl.pallas_call(
        coarse_kernel,
        out_shape=jax.ShapeDtypeStruct((64, 640), F32),
        in_specs=[vmem] * 3,
        out_specs=vmem,
        scratch_shapes=[pltpu.VMEM((2, 12, 64, 128), BF16)],
        compiler_params=pltpu.CompilerParams(vmem_limit_bytes=6 * 1024 * 1024),
        cost_estimate=pl.CostEstimate(flops=150_000_000, bytes_accessed=0, transcendentals=0),
    )(both, pair, other)


def near_kernel(near, sums, pair, other, o0, o1, o2, o3, cells):
    pd = lax.rem(lax.axis_index("depth"), 2)
    for i in (0, 1, 10, 11):
        cells[0, i] = jnp.zeros((64, 128), BF16)
    for k in range(4):
        cells[0, 2 + 2 * k : 4 + 2 * k] = near[k]

    def put(start, size, value):
        value = value + sums[:, start : start + size]
        for k, out in enumerate((o0, o1, o2, o3)):
            out[:, start : start + size] = value[16 * k : 16 * k + 16]

    coarse_sums(cells, (2 - 2 * pd,), pair, other, put)


def near_level(near, sums, pair, other):
    vmem = pl.BlockSpec(memory_space=pltpu.VMEM)
    return pl.pallas_call(
        near_kernel,
        out_shape=[jax.ShapeDtypeStruct((16, 640), F32)] * 4,
        in_specs=[vmem] * 4,
        out_specs=[vmem] * 4,
        scratch_shapes=[pltpu.VMEM((1, 12, 64, 128), BF16)],
        compiler_params=pltpu.CompilerParams(vmem_limit_bytes=6 * 1024 * 1024),
    )(near, sums, pair, other)


def join_kernel(s0, s2, s3, s1, bias, out, held):
    y = lax.div(lax.axis_index("rows"), 4)
    for k, part in enumerate((s0, s1, s2, s3)):
        held[y ^ k] = part[...]
    low = lax.broadcasted_iota(jnp.int32, (16, 128), 1) < 64
    for m in range(4):
        tiles = [held[m, :, 128 * i : 128 * i + 128] for i in range(4)]
        if m > 0:
            tiles[0] = tiles[0] + jnp.where(low, held[m - 1, :, 512:], 0.0)
        if m < 3:
            tiles[3] = tiles[3] + jnp.where(low, 0.0, held[m + 1, :, 512:])
        for i in range(4):
            value = jnp.maximum(tiles[i] + bias[...], 0.0).astype(BF16)
            out[:, 512 * m + 128 * i : 512 * m + 128 * i + 128] = value


def join(parts, bias):
    vmem = pl.BlockSpec(memory_space=pltpu.VMEM)
    return pl.pallas_call(
        join_kernel,
        out_shape=jax.ShapeDtypeStruct((16, 2048), BF16),
        in_specs=[vmem] * 5,
        out_specs=vmem,
        scratch_shapes=[pltpu.VMEM((4, 16, 640), F32)],
        compiler_params=pltpu.CompilerParams(vmem_limit_bytes=4 * 1024 * 1024),
    )(*parts, bias)


def body(volume, fine_filters, fine_bias, coarse_filters, coarse_bias):
    d = lax.axis_index("depth")
    r = lax.axis_index("rows")
    pd = lax.rem(d, 2)
    pr = lax.rem(r, 2)
    depth_near, depth_far = near_pairs(16), far_pairs(16)
    rows_near, rows_far = near_pairs(16), far_pairs(16)

    x2 = lax.ppermute(lax.dynamic_index_in_dim(volume, pd, 0, False), "depth", depth_far)
    x1 = lax.ppermute(lax.dynamic_index_in_dim(volume, 1 - pd, 0, False), "depth", depth_near)
    r2 = lax.ppermute(lax.dynamic_index_in_dim(volume, 3 * pr, 1, False), "rows", rows_far)
    r1 = lax.ppermute(lax.dynamic_index_in_dim(volume, 3 - 3 * pr, 1, False), "rows", rows_near)
    sides = jnp.stack([x2, x1])
    far_row = lax.dynamic_index_in_dim(sides, 3 * pr, 1, False)[0]
    near_row = lax.dynamic_index_in_dim(sides, 3 - 3 * pr, 1, False)[0]
    c2 = lax.ppermute(far_row, "rows", rows_far)
    c1 = lax.ppermute(near_row, "rows", rows_near)
    e = lax.ppermute(outer_rows(far_row, near_row, r2, r1), "depth", depth_near)

    def along_y(k):
        return [(i, i ^ (4 * k)) for i in range(16)]

    w = jnp.transpose(coarse_filters, (0, 1, 2, 4, 3)).reshape(27, 16, 128)
    pair = jnp.stack([w, lax.ppermute(w, "rows", along_y(3))])
    other = lax.ppermute(pair, "rows", along_y(1))
    main = fine_level(volume, x2, x1, r2, r1, fine_filters, jnp.broadcast_to(fine_bias, (8, 128)))
    pooled = finish(main, c2, c1, e, other)

    both = lax.all_to_all(
        pooled, ("depth", "rows"), 0, 0, axis_index_groups=far_and_z(), tiled=True
    ).reshape(2, 4, 2, 64, 128)
    near = lax.ppermute(lax.dynamic_index_in_dim(both, 1 - pd, 0, False), "depth", depth_near)
    sums = near_level(near, coarse_level(both, pair, other), pair, other)
    parts = [sums[0]] + [lax.ppermute(sums[k], "rows", along_y(k)) for k in (2, 3, 1)]
    result = join(parts, jnp.broadcast_to(coarse_bias[:, None], (16, 128)))
    return result.reshape(16, 1, 2048)


def solution(mesh):
    placed = (
        P("depth", "rows", None, None),
        P(),
        P(),
        P(None, None, None, None, "rows"),
        P("rows"),
    )
    return jax.shard_map(
        body, mesh=mesh, in_specs=placed, out_specs=P("rows", "depth", None), check_vma=False
    )
```

```python
import jax
import jax.numpy as jnp
from jax import lax
from jax.experimental import pallas as pl
from jax.experimental.pallas import tpu as pltpu
from jax.sharding import PartitionSpec as P

BF16 = jnp.bfloat16
F32 = jnp.float32


def near_pairs(count):
    return [(i, i ^ 1) for i in range(count)]


def far_pairs(count):
    return [(i, min(max(((i - 1) ^ 1) + 1, 0), count - 1)) for i in range(count)]


def far_and_z():
    pairs = [(d, d + 1) for d in range(1, 15, 2)] + [(15, 0)]
    return [[d * 16 + 4 * y + z for d in pair for z in range(4)] for pair in pairs for y in range(4)]


def inner(axis):
    i = lax.axis_index(axis)
    return (i > 0) & (i < 15)


def spread(line, col):
    left = jnp.where(col == 0, 0.0, pltpu.roll(line[:, :128], 1, 0))
    right = jnp.where(col == 127, 0.0, pltpu.roll(line[:, 256:], 127, 0))
    return line[:, 128:256] + left + right


def fine_kernel(vol, x2, x1, r2, r1, w, bias, ends, best, corner_w, cells):
    pd = lax.rem(lax.axis_index("depth"), 2)
    pr = lax.rem(lax.axis_index("rows"), 2)
    inner_d = inner("depth")
    inner_r = inner("rows")
    zero = jnp.zeros((128, 128), BF16)
    for j in range(4):
        for i in range(6):
            row = (i - 1) + pr * (5 - 2 * i)
            if j in (1, 2):
                plane = (j - 1) + pd * (3 - 2 * j)
                piece = r2[plane] if i == 0 else r1[plane] if i == 5 else vol[plane, row]
            elif i in (0, 5):
                piece = zero
            else:
                piece = (x2 if j == 0 else x1)[row]
            if i == 0:
                piece = jnp.where(inner_r, piece, zero)
            if j == 0:
                piece = jnp.where(inner_d, piece, zero)
            cells[j, i] = piece
    taps = [(a, b) for a in range(3) for b in range(3)]
    groups = [taps[i : i + 2] for i in range(0, 9, 2)]
    col = lax.broadcasted_iota(jnp.int32, (128, 128), 0)
    for s in range(2):
        total = None
        for group in groups:
            lhs = jnp.concatenate(
                [cells[s + a, b : b + 4].reshape(512, 128) for a, b in group], axis=1
            )
            rhs = jnp.concatenate(
                [
                    jnp.concatenate(
                        [w[a + pd * (2 - 2 * a), b + pr * (2 - 2 * b), c] for c in range(3)], axis=1
                    )
                    for a, b in group
                ],
                axis=0,
            )
            term = jnp.dot(lhs, rhs, preferred_element_type=F32)
            total = term if total is None else total + term
        for q in range(2):
            ends[s, q] = spread(total[3 * q * 128 : (3 * q + 1) * 128], col) + bias[:1]
            middle = spread(total[(q + 1) * 128 : (q + 2) * 128], col) + bias[:1]
            best[q] = middle if s == 0 else jnp.maximum(best[q], middle)
            a, b = 2 * s, 2 * q
            for c in range(3):
                corner_w[s, q, :, 128 * c : 128 * c + 128] = w[a + pd * (2 - 2 * a), b + pr * (2 - 2 * b), c]


def fine_level(vol, x2, x1, r2, r1, w, bias):
    vmem = pl.BlockSpec(memory_space=pltpu.VMEM)
    return pl.pallas_call(
        fine_kernel,
        out_shape=[
            jax.ShapeDtypeStruct((2, 2, 128, 128), F32),
            jax.ShapeDtypeStruct((2, 128, 128), F32),
            jax.ShapeDtypeStruct((2, 2, 128, 384), BF16),
        ],
        in_specs=[vmem] * 7,
        out_specs=[vmem] * 3,
        scratch_shapes=[pltpu.VMEM((4, 6, 128, 128), BF16)],
        compiler_params=pltpu.CompilerParams(vmem_limit_bytes=12 * 1024 * 1024),
        cost_estimate=pl.CostEstimate(flops=20_000_000_000, bytes_accessed=0, transcendentals=0),
    )(vol, x2, x1, r2, r1, w, bias)


def outer_kernel(far_row, near_row, r2, r1, out):
    pd = lax.rem(lax.axis_index("depth"), 2)
    out[0] = r2[1 - pd]
    out[1] = r1[1 - pd]


def outer_rows(far_row, near_row, r2, r1):
    vmem = pl.BlockSpec(memory_space=pltpu.VMEM)
    return pl.pallas_call(
        outer_kernel,
        out_shape=jax.ShapeDtypeStruct((2, 128, 128), BF16),
        in_specs=[pl.BlockSpec(memory_space=pl.ANY)] * 2 + [vmem] * 2,
        out_specs=vmem,
        compiler_params=pltpu.CompilerParams(vmem_limit_bytes=2 * 1024 * 1024),
    )(far_row, near_row, r2, r1)


def finish_kernel(ends, best, corner_w, c2, c1, e, other, out, peak):
    pr = lax.rem(lax.axis_index("rows"), 2)
    inner_d = inner("depth")
    inner_r = inner("rows")
    zero = jnp.zeros((128, 128), BF16)
    col = lax.broadcasted_iota(jnp.int32, (128, 128), 0)
    for q in range(2):
        value = best[q]
        for s in range(2):
            piece = e[q] if s == 1 else (c2, c1)[q][...]
            if q == 0:
                piece = jnp.where(inner_r, piece, zero)
            if s == 0:
                piece = jnp.where(inner_d, piece, zero)
            corner = jnp.dot(piece, corner_w[s, q], preferred_element_type=F32)
            value = jnp.maximum(value, ends[s, q] + spread(corner, col))
        peak[...] = value
        pooled = jnp.maximum(peak[pl.ds(0, 64, stride=2), :], peak[pl.ds(1, 64, stride=2), :])
        pooled = jnp.maximum(pooled, 0.0).astype(BF16)
        for k in range(8):
            out[k, q + pr * (1 - 2 * q)] = pooled


def finish(main, c2, c1, e, other):
    vmem = pl.BlockSpec(memory_space=pltpu.VMEM)
    return pl.pallas_call(
        finish_kernel,
        out_shape=jax.ShapeDtypeStruct((8, 2, 64, 128), BF16),
        in_specs=[vmem] * 6 + [pl.BlockSpec(memory_space=pl.ANY)],
        out_specs=vmem,
        scratch_shapes=[pltpu.VMEM((128, 128), F32)],
        compiler_params=pltpu.CompilerParams(vmem_limit_bytes=6 * 1024 * 1024),
    )(*main, c2, c1, e, other)


def coarse_sums(cells, taps, pair, other, add):
    lhs = jnp.concatenate(
        [
            jnp.concatenate([w[m, 9 * a + 3 * b + c] for a in taps for b in range(3)], axis=1)
            for c in range(3)
            for w, m in ((pair, 0), (other, 0), (other, 1), (pair, 1))
        ],
        axis=0,
    )
    count = len(taps)
    for start, size in ((0, 256), (256, 256), (512, 128)):
        if start < 512:
            first = start // 64 + 1
            blocks = [
                cells[i, first + b : first + b + 4].reshape(256, 128) for i in range(count) for b in range(3)
            ]
        else:
            blocks = [
                jnp.concatenate([cells[i, 9 + b], cells[i, b]], axis=0) for i in range(count) for b in range(3)
            ]
        rhs = jnp.concatenate(blocks, axis=1)
        term = lax.dot_general(lhs, rhs, (((1,), (1,)), ((), ())), preferred_element_type=F32)
        lane = lax.rem(lax.broadcasted_iota(jnp.int32, (64, size), 1), 64)
        left = jnp.where(lane == 0, 0.0, pltpu.roll(term[:64], 1, 1))
        right = jnp.where(lane == 63, 0.0, pltpu.roll(term[128:], size - 1, 1))
        add(start, size, term[64:128] + left + right)


def coarse_kernel(both, pair, other, out, cells):
    pd = lax.rem(lax.axis_index("depth"), 2)
    inner_d = inner("depth")
    for a in range(2):
        for i in (0, 1, 10, 11):
            cells[a, i] = jnp.zeros((64, 128), BF16)
    for k in range(4):
        far = both[pd, k]
        cells[0, 2 + 2 * k : 4 + 2 * k] = jnp.where(inner_d, far, jnp.zeros_like(far))
        cells[1, 2 + 2 * k : 4 + 2 * k] = both[1 - pd, k]

    def put(start, size, value):
        out[:, start : start + size] = value

    coarse_sums(cells, (2 * pd, 1), pair, other, put)


def coarse_level(both, pair, other):
    vmem = pl.BlockSpec(memory_space=pltpu.VMEM)
    return pl.pallas_call(
        coarse_kernel,
        out_shape=jax.ShapeDtypeStruct((64, 640), F32),
        in_specs=[vmem] * 3,
        out_specs=vmem,
        scratch_shapes=[pltpu.VMEM((2, 12, 64, 128), BF16)],
        compiler_params=pltpu.CompilerParams(vmem_limit_bytes=6 * 1024 * 1024),
        cost_estimate=pl.CostEstimate(flops=150_000_000, bytes_accessed=0, transcendentals=0),
    )(both, pair, other)


def near_kernel(near, sums, pair, other, o0, o1, o2, o3, cells):
    pd = lax.rem(lax.axis_index("depth"), 2)
    for i in (0, 1, 10, 11):
        cells[0, i] = jnp.zeros((64, 128), BF16)
    for k in range(4):
        cells[0, 2 + 2 * k : 4 + 2 * k] = near[k]

    def put(start, size, value):
        value = value + sums[:, start : start + size]
        for k, out in enumerate((o0, o1, o2, o3)):
            out[:, start : start + size] = value[16 * k : 16 * k + 16]

    coarse_sums(cells, (2 - 2 * pd,), pair, other, put)


def near_level(near, sums, pair, other):
    vmem = pl.BlockSpec(memory_space=pltpu.VMEM)
    return pl.pallas_call(
        near_kernel,
        out_shape=[jax.ShapeDtypeStruct((16, 640), F32)] * 4,
        in_specs=[vmem] * 4,
        out_specs=[vmem] * 4,
        scratch_shapes=[pltpu.VMEM((1, 12, 64, 128), BF16)],
        compiler_params=pltpu.CompilerParams(vmem_limit_bytes=6 * 1024 * 1024),
    )(near, sums, pair, other)


def join_kernel(s0, s2, s3, s1, bias, out, held, ready, done):
    y = lax.div(lax.axis_index("rows"), 4)
    for k, part in enumerate((s0, s1, s2, s3)):
        held[y ^ k] = part[...]
    low = lax.broadcasted_iota(jnp.int32, (16, 128), 1) < 64
    copies = []
    for m in range(4):
        tiles = [held[m, :, 128 * i : 128 * i + 128] for i in range(4)]
        if m > 0:
            tiles[0] = tiles[0] + jnp.where(low, held[m - 1, :, 512:], 0.0)
        if m < 3:
            tiles[3] = tiles[3] + jnp.where(low, 0.0, held[m + 1, :, 512:])
        for i in range(4):
            value = jnp.maximum(tiles[i] + bias[...], 0.0).astype(BF16)
            ready[:, 512 * m + 128 * i : 512 * m + 128 * i + 128] = value
        columns = pl.ds(512 * m, 512)
        copies.append(pltpu.make_async_copy(ready.at[:, columns], out.at[:, columns], done.at[m]))
        copies[m].start()
    for copy in copies:
        copy.wait()


def join(parts, bias):
    vmem = pl.BlockSpec(memory_space=pltpu.VMEM)
    return pl.pallas_call(
        join_kernel,
        out_shape=jax.ShapeDtypeStruct((16, 2048), BF16),
        in_specs=[vmem] * 5,
        out_specs=pl.BlockSpec(memory_space=pl.ANY),
        scratch_shapes=[
            pltpu.VMEM((4, 16, 640), F32),
            pltpu.VMEM((16, 2048), BF16),
            pltpu.SemaphoreType.DMA((4,)),
        ],
        compiler_params=pltpu.CompilerParams(vmem_limit_bytes=4 * 1024 * 1024),
    )(*parts, bias)


def body(volume, fine_filters, fine_bias, coarse_filters, coarse_bias):
    d = lax.axis_index("depth")
    r = lax.axis_index("rows")
    pd = lax.rem(d, 2)
    pr = lax.rem(r, 2)
    depth_near, depth_far = near_pairs(16), far_pairs(16)
    rows_near, rows_far = near_pairs(16), far_pairs(16)

    x2 = lax.ppermute(lax.dynamic_index_in_dim(volume, pd, 0, False), "depth", depth_far)
    x1 = lax.ppermute(lax.dynamic_index_in_dim(volume, 1 - pd, 0, False), "depth", depth_near)
    r2 = lax.ppermute(lax.dynamic_index_in_dim(volume, 3 * pr, 1, False), "rows", rows_far)
    r1 = lax.ppermute(lax.dynamic_index_in_dim(volume, 3 - 3 * pr, 1, False), "rows", rows_near)
    sides = jnp.stack([x2, x1])
    far_row = lax.dynamic_index_in_dim(sides, 3 * pr, 1, False)[0]
    near_row = lax.dynamic_index_in_dim(sides, 3 - 3 * pr, 1, False)[0]
    c2 = lax.ppermute(far_row, "rows", rows_far)
    c1 = lax.ppermute(near_row, "rows", rows_near)
    e = lax.ppermute(outer_rows(far_row, near_row, r2, r1), "depth", depth_near)

    def along_y(k):
        return [(i, i ^ (4 * k)) for i in range(16)]

    w = jnp.transpose(coarse_filters, (0, 1, 2, 4, 3)).reshape(27, 16, 128)
    pair = jnp.stack([w, lax.ppermute(w, "rows", along_y(3))])
    other = lax.ppermute(pair, "rows", along_y(1))
    main = fine_level(volume, x2, x1, r2, r1, fine_filters, jnp.broadcast_to(fine_bias, (8, 128)))
    pooled = finish(main, c2, c1, e, other)

    both = lax.all_to_all(
        pooled, ("depth", "rows"), 0, 0, axis_index_groups=far_and_z(), tiled=True
    ).reshape(2, 4, 2, 64, 128)
    near = lax.ppermute(lax.dynamic_index_in_dim(both, 1 - pd, 0, False), "depth", depth_near)
    sums = near_level(near, coarse_level(both, pair, other), pair, other)
    parts = [sums[0]] + [lax.ppermute(sums[k], "rows", along_y(k)) for k in (2, 3, 1)]
    result = join(parts, jnp.broadcast_to(coarse_bias[:, None], (16, 128)))
    return result.reshape(16, 1, 2048)


def solution(mesh):
    placed = (
        P("depth", "rows", None, None),
        P(),
        P(),
        P(None, None, None, None, "rows"),
        P("rows"),
    )
    return jax.shard_map(
        body, mesh=mesh, in_specs=placed, out_specs=P("rows", "depth", None), check_vma=False
    )
```

```python
import jax
import jax.numpy as jnp
from jax import lax
from jax.experimental import pallas as pl
from jax.experimental.pallas import tpu as pltpu
from jax.sharding import PartitionSpec as P

BF16 = jnp.bfloat16
F32 = jnp.float32


def near_pairs(count):
    return [(i, i ^ 1) for i in range(count)]


def far_pairs(count):
    return [(i, min(max(((i - 1) ^ 1) + 1, 0), count - 1)) for i in range(count)]


def far_and_z():
    pairs = [(d, d + 1) for d in range(1, 15, 2)] + [(15, 0)]
    return [[d * 16 + 4 * y + z for d in pair for z in range(4)] for pair in pairs for y in range(4)]


def inner(axis):
    i = lax.axis_index(axis)
    return (i > 0) & (i < 15)


def spread(line, col):
    left = jnp.where(col == 0, 0.0, pltpu.roll(line[:, :128], 1, 0))
    right = jnp.where(col == 127, 0.0, pltpu.roll(line[:, 256:], 127, 0))
    return line[:, 128:256] + left + right


def fine_kernel(vol, x2, x1, r2, r1, w, bias, ends, best, corner_w, cells):
    pd = lax.rem(lax.axis_index("depth"), 2)
    pr = lax.rem(lax.axis_index("rows"), 2)
    inner_d = inner("depth")
    inner_r = inner("rows")
    zero = jnp.zeros((128, 128), BF16)
    for j in range(4):
        for i in range(6):
            row = (i - 1) + pr * (5 - 2 * i)
            if j in (1, 2):
                plane = (j - 1) + pd * (3 - 2 * j)
                piece = r2[plane] if i == 0 else r1[plane] if i == 5 else vol[plane, row]
            elif i in (0, 5):
                piece = zero
            else:
                piece = (x2 if j == 0 else x1)[row]
            if i == 0:
                piece = jnp.where(inner_r, piece, zero)
            if j == 0:
                piece = jnp.where(inner_d, piece, zero)
            cells[j, i] = piece
    taps = [(a, b) for a in range(3) for b in range(3)]
    groups = [taps[i : i + 2] for i in range(0, 9, 2)]
    col = lax.broadcasted_iota(jnp.int32, (128, 128), 0)
    for s in range(2):
        total = None
        for group in groups:
            lhs = jnp.concatenate(
                [cells[s + a, b : b + 4].reshape(512, 128) for a, b in group], axis=1
            )
            rhs = jnp.concatenate(
                [
                    jnp.concatenate(
                        [w[a + pd * (2 - 2 * a), b + pr * (2 - 2 * b), c] for c in range(3)], axis=1
                    )
                    for a, b in group
                ],
                axis=0,
            )
            term = jnp.dot(lhs, rhs, preferred_element_type=F32)
            total = term if total is None else total + term
        for q in range(2):
            ends[s, q] = spread(total[3 * q * 128 : (3 * q + 1) * 128], col) + bias[:1]
            middle = spread(total[(q + 1) * 128 : (q + 2) * 128], col) + bias[:1]
            best[q] = middle if s == 0 else jnp.maximum(best[q], middle)
            a, b = 2 * s, 2 * q
            for c in range(3):
                corner_w[s, q, :, 128 * c : 128 * c + 128] = w[a + pd * (2 - 2 * a), b + pr * (2 - 2 * b), c]


def fine_level(vol, x2, x1, r2, r1, w, bias):
    vmem = pl.BlockSpec(memory_space=pltpu.VMEM)
    return pl.pallas_call(
        fine_kernel,
        out_shape=[
            jax.ShapeDtypeStruct((2, 2, 128, 128), F32),
            jax.ShapeDtypeStruct((2, 128, 128), F32),
            jax.ShapeDtypeStruct((2, 2, 128, 384), BF16),
        ],
        in_specs=[vmem] * 7,
        out_specs=[vmem] * 3,
        scratch_shapes=[pltpu.VMEM((4, 6, 128, 128), BF16)],
        compiler_params=pltpu.CompilerParams(vmem_limit_bytes=12 * 1024 * 1024),
        cost_estimate=pl.CostEstimate(flops=20_000_000_000, bytes_accessed=0, transcendentals=0),
    )(vol, x2, x1, r2, r1, w, bias)


def outer_kernel(far_row, near_row, r2, r1, out):
    pd = lax.rem(lax.axis_index("depth"), 2)
    out[0] = r2[1 - pd]
    out[1] = r1[1 - pd]


def outer_rows(far_row, near_row, r2, r1):
    vmem = pl.BlockSpec(memory_space=pltpu.VMEM)
    return pl.pallas_call(
        outer_kernel,
        out_shape=jax.ShapeDtypeStruct((2, 128, 128), BF16),
        in_specs=[pl.BlockSpec(memory_space=pl.ANY)] * 2 + [vmem] * 2,
        out_specs=vmem,
        compiler_params=pltpu.CompilerParams(vmem_limit_bytes=2 * 1024 * 1024),
    )(far_row, near_row, r2, r1)


def finish_kernel(ends, best, corner_w, c2, c1, e, other, out, peak):
    pr = lax.rem(lax.axis_index("rows"), 2)
    inner_d = inner("depth")
    inner_r = inner("rows")
    zero = jnp.zeros((128, 128), BF16)
    col = lax.broadcasted_iota(jnp.int32, (128, 128), 0)
    for q in range(2):
        value = best[q]
        for s in range(2):
            piece = e[q] if s == 1 else (c2, c1)[q][...]
            if q == 0:
                piece = jnp.where(inner_r, piece, zero)
            if s == 0:
                piece = jnp.where(inner_d, piece, zero)
            corner = jnp.dot(piece, corner_w[s, q], preferred_element_type=F32)
            value = jnp.maximum(value, ends[s, q] + spread(corner, col))
        peak[...] = value
        pooled = jnp.maximum(peak[pl.ds(0, 64, stride=2), :], peak[pl.ds(1, 64, stride=2), :])
        pooled = jnp.maximum(pooled, 0.0).astype(BF16)
        for k in range(8):
            out[k, q + pr * (1 - 2 * q)] = pooled


def finish(main, c2, c1, e, other):
    vmem = pl.BlockSpec(memory_space=pltpu.VMEM)
    return pl.pallas_call(
        finish_kernel,
        out_shape=jax.ShapeDtypeStruct((8, 2, 64, 128), BF16),
        in_specs=[vmem] * 6 + [pl.BlockSpec(memory_space=pl.ANY)],
        out_specs=vmem,
        scratch_shapes=[pltpu.VMEM((128, 128), F32)],
        compiler_params=pltpu.CompilerParams(vmem_limit_bytes=6 * 1024 * 1024),
    )(*main, c2, c1, e, other)


def coarse_sums(cells, taps, pair, other, add):
    lhs = jnp.concatenate(
        [
            jnp.concatenate([w[m, 9 * a + 3 * b + c] for a in taps for b in range(3)], axis=1)
            for c in range(3)
            for w, m in ((pair, 0), (other, 0), (other, 1), (pair, 1))
        ],
        axis=0,
    )
    count = len(taps)
    for start, size in ((0, 256), (256, 256), (512, 128)):
        if start < 512:
            first = start // 64 + 1
            blocks = [
                cells[i, first + b : first + b + 4].reshape(256, 128) for i in range(count) for b in range(3)
            ]
        else:
            blocks = [
                jnp.concatenate([cells[i, 9 + b], cells[i, b]], axis=0) for i in range(count) for b in range(3)
            ]
        rhs = jnp.concatenate(blocks, axis=1)
        term = lax.dot_general(lhs, rhs, (((1,), (1,)), ((), ())), preferred_element_type=F32)
        lane = lax.rem(lax.broadcasted_iota(jnp.int32, (64, size), 1), 64)
        left = jnp.where(lane == 0, 0.0, pltpu.roll(term[:64], 1, 1))
        right = jnp.where(lane == 63, 0.0, pltpu.roll(term[128:], size - 1, 1))
        add(start, size, term[64:128] + left + right)


def coarse_kernel(both, pair, other, out, cells):
    pd = lax.rem(lax.axis_index("depth"), 2)
    inner_d = inner("depth")
    for a in range(2):
        for i in (0, 1, 10, 11):
            cells[a, i] = jnp.zeros((64, 128), BF16)
    for k in range(4):
        far = both[pd, k]
        cells[0, 2 + 2 * k : 4 + 2 * k] = jnp.where(inner_d, far, jnp.zeros_like(far))
        cells[1, 2 + 2 * k : 4 + 2 * k] = both[1 - pd, k]

    def put(start, size, value):
        out[:, start : start + size] = value

    coarse_sums(cells, (2 * pd, 1), pair, other, put)


def coarse_level(both, pair, other):
    vmem = pl.BlockSpec(memory_space=pltpu.VMEM)
    return pl.pallas_call(
        coarse_kernel,
        out_shape=jax.ShapeDtypeStruct((64, 640), F32),
        in_specs=[vmem] * 3,
        out_specs=vmem,
        scratch_shapes=[pltpu.VMEM((2, 12, 64, 128), BF16)],
        compiler_params=pltpu.CompilerParams(vmem_limit_bytes=6 * 1024 * 1024),
        cost_estimate=pl.CostEstimate(flops=150_000_000, bytes_accessed=0, transcendentals=0),
    )(both, pair, other)


def near_kernel(near, sums, pair, other, o0, o1, o2, o3, cells):
    pd = lax.rem(lax.axis_index("depth"), 2)
    for i in (0, 1, 10, 11):
        cells[0, i] = jnp.zeros((64, 128), BF16)
    for k in range(4):
        cells[0, 2 + 2 * k : 4 + 2 * k] = near[k]

    def put(start, size, value):
        value = value + sums[:, start : start + size]
        for k, out in enumerate((o0, o1, o2, o3)):
            out[:, start : start + size] = value[16 * k : 16 * k + 16]

    coarse_sums(cells, (2 - 2 * pd,), pair, other, put)


def near_level(near, sums, pair, other):
    vmem = pl.BlockSpec(memory_space=pltpu.VMEM)
    return pl.pallas_call(
        near_kernel,
        out_shape=[jax.ShapeDtypeStruct((16, 640), F32)] * 4,
        in_specs=[vmem] * 4,
        out_specs=[vmem] * 4,
        scratch_shapes=[pltpu.VMEM((1, 12, 64, 128), BF16)],
        compiler_params=pltpu.CompilerParams(vmem_limit_bytes=6 * 1024 * 1024),
    )(near, sums, pair, other)


def join_kernel(s0, s3, s2, s1, bias, out, held):
    y = lax.div(lax.axis_index("rows"), 4)
    for k, part in enumerate((s0, s1, s2, s3)):
        held[y ^ k] = part[...]
    low = lax.broadcasted_iota(jnp.int32, (16, 128), 1) < 64
    for m in range(4):
        tiles = [held[m, :, 128 * i : 128 * i + 128] for i in range(4)]
        if m > 0:
            tiles[0] = tiles[0] + jnp.where(low, held[m - 1, :, 512:], 0.0)
        if m < 3:
            tiles[3] = tiles[3] + jnp.where(low, 0.0, held[m + 1, :, 512:])
        for i in range(4):
            value = jnp.maximum(tiles[i] + bias[...], 0.0).astype(BF16)
            out[:, 512 * m + 128 * i : 512 * m + 128 * i + 128] = value


def join(parts, bias):
    vmem = pl.BlockSpec(memory_space=pltpu.VMEM)
    return pl.pallas_call(
        join_kernel,
        out_shape=jax.ShapeDtypeStruct((16, 2048), BF16),
        in_specs=[vmem] * 5,
        out_specs=vmem,
        scratch_shapes=[pltpu.VMEM((4, 16, 640), F32)],
        compiler_params=pltpu.CompilerParams(vmem_limit_bytes=4 * 1024 * 1024),
    )(*parts, bias)


def body(volume, fine_filters, fine_bias, coarse_filters, coarse_bias):
    d = lax.axis_index("depth")
    r = lax.axis_index("rows")
    pd = lax.rem(d, 2)
    pr = lax.rem(r, 2)
    depth_near, depth_far = near_pairs(16), far_pairs(16)
    rows_near, rows_far = near_pairs(16), far_pairs(16)

    x2 = lax.ppermute(lax.dynamic_index_in_dim(volume, pd, 0, False), "depth", depth_far)
    x1 = lax.ppermute(lax.dynamic_index_in_dim(volume, 1 - pd, 0, False), "depth", depth_near)
    r2 = lax.ppermute(lax.dynamic_index_in_dim(volume, 3 * pr, 1, False), "rows", rows_far)
    r1 = lax.ppermute(lax.dynamic_index_in_dim(volume, 3 - 3 * pr, 1, False), "rows", rows_near)
    sides = jnp.stack([x2, x1])
    far_row = lax.dynamic_index_in_dim(sides, 3 * pr, 1, False)[0]
    near_row = lax.dynamic_index_in_dim(sides, 3 - 3 * pr, 1, False)[0]
    c2 = lax.ppermute(far_row, "rows", rows_far)
    c1 = lax.ppermute(near_row, "rows", rows_near)
    e = lax.ppermute(outer_rows(far_row, near_row, r2, r1), "depth", depth_near)

    def along_y(k):
        return [(i, i ^ (4 * k)) for i in range(16)]

    w = jnp.transpose(coarse_filters, (0, 1, 2, 4, 3)).reshape(27, 16, 128)
    pair = jnp.stack([w, lax.ppermute(w, "rows", along_y(3))])
    other = lax.ppermute(pair, "rows", along_y(1))
    main = fine_level(volume, x2, x1, r2, r1, fine_filters, jnp.broadcast_to(fine_bias, (8, 128)))
    pooled = finish(main, c2, c1, e, other)

    both = lax.all_to_all(
        pooled, ("depth", "rows"), 0, 0, axis_index_groups=far_and_z(), tiled=True
    ).reshape(2, 4, 2, 64, 128)
    near = lax.ppermute(lax.dynamic_index_in_dim(both, 1 - pd, 0, False), "depth", depth_near)
    sums = near_level(near, coarse_level(both, pair, other), pair, other)
    parts = [sums[0]] + [lax.ppermute(sums[k], "rows", along_y(k)) for k in (3, 2, 1)]
    result = join(parts, jnp.broadcast_to(coarse_bias[:, None], (16, 128)))
    return result.reshape(16, 1, 2048)


def solution(mesh):
    placed = (
        P("depth", "rows", None, None),
        P(),
        P(),
        P(None, None, None, None, "rows"),
        P("rows"),
    )
    return jax.shard_map(
        body, mesh=mesh, in_specs=placed, out_specs=P("rows", "depth", None), check_vma=False
    )
```

```python
import jax
import jax.numpy as jnp
from jax import lax
from jax.experimental import pallas as pl
from jax.experimental.pallas import tpu as pltpu
from jax.sharding import PartitionSpec as P

BF16 = jnp.bfloat16
F32 = jnp.float32


def near_pairs(count):
    return [(i, i ^ 1) for i in range(count)]


def far_pairs(count):
    return [(i, min(max(((i - 1) ^ 1) + 1, 0), count - 1)) for i in range(count)]


def far_and_z():
    pairs = [(d, d + 1) for d in range(1, 15, 2)] + [(15, 0)]
    return [[d * 16 + 4 * y + z for d in pair for z in range(4)] for pair in pairs for y in range(4)]


def inner(axis):
    i = lax.axis_index(axis)
    return (i > 0) & (i < 15)


def spread(line, col):
    left = jnp.where(col == 0, 0.0, pltpu.roll(line[:, :128], 1, 0))
    right = jnp.where(col == 127, 0.0, pltpu.roll(line[:, 256:], 127, 0))
    return line[:, 128:256] + left + right


def fine_kernel(vol, x2, x1, r2, r1, w, bias, ends, best, corner_w, cells):
    pd = lax.rem(lax.axis_index("depth"), 2)
    pr = lax.rem(lax.axis_index("rows"), 2)
    inner_d = inner("depth")
    inner_r = inner("rows")
    zero = jnp.zeros((128, 128), BF16)
    for j in range(4):
        for i in range(6):
            row = (i - 1) + pr * (5 - 2 * i)
            if j in (1, 2):
                plane = (j - 1) + pd * (3 - 2 * j)
                piece = r2[plane] if i == 0 else r1[plane] if i == 5 else vol[plane, row]
            elif i in (0, 5):
                piece = zero
            else:
                piece = (x2 if j == 0 else x1)[row]
            if i == 0:
                piece = jnp.where(inner_r, piece, zero)
            if j == 0:
                piece = jnp.where(inner_d, piece, zero)
            cells[j, i] = piece
    def tap(a, b):
        return [w[a + pd * (2 - 2 * a), b + pr * (2 - 2 * b), c] for c in range(3)]

    def line_sums(pieces, outs):
        total = None
        for i in range(0, len(pieces), 2):
            group = pieces[i : i + 2]
            lhs = jnp.concatenate([cells[j, b : b + 4].reshape(512, 128) for j, b in group], axis=1)
            rhs = jnp.concatenate(
                [jnp.concatenate(sum([tap(j - s, b) for s in outs], []), axis=1) for j, b in group], axis=0
            )
            term = jnp.dot(lhs, rhs, preferred_element_type=F32)
            total = term if total is None else total + term
        return total

    col = lax.broadcasted_iota(jnp.int32, (128, 128), 0)
    shared = line_sums([(j, b) for j in (1, 2) for b in range(3)], (0, 1))
    for s in range(2):
        total = shared[:, 384 * s : 384 * s + 384] + line_sums([(3 * s, b) for b in range(3)], (s,))
        for q in range(2):
            ends[s, q] = spread(total[3 * q * 128 : (3 * q + 1) * 128], col) + bias[:1]
            middle = spread(total[(q + 1) * 128 : (q + 2) * 128], col) + bias[:1]
            best[q] = middle if s == 0 else jnp.maximum(best[q], middle)
            a, b = 2 * s, 2 * q
            for c in range(3):
                corner_w[s, q, :, 128 * c : 128 * c + 128] = w[a + pd * (2 - 2 * a), b + pr * (2 - 2 * b), c]


def fine_level(vol, x2, x1, r2, r1, w, bias):
    vmem = pl.BlockSpec(memory_space=pltpu.VMEM)
    return pl.pallas_call(
        fine_kernel,
        out_shape=[
            jax.ShapeDtypeStruct((2, 2, 128, 128), F32),
            jax.ShapeDtypeStruct((2, 128, 128), F32),
            jax.ShapeDtypeStruct((2, 2, 128, 384), BF16),
        ],
        in_specs=[vmem] * 7,
        out_specs=[vmem] * 3,
        scratch_shapes=[pltpu.VMEM((4, 6, 128, 128), BF16)],
        compiler_params=pltpu.CompilerParams(vmem_limit_bytes=12 * 1024 * 1024),
        cost_estimate=pl.CostEstimate(flops=20_000_000_000, bytes_accessed=0, transcendentals=0),
    )(vol, x2, x1, r2, r1, w, bias)


def outer_kernel(far_row, near_row, r2, r1, out):
    pd = lax.rem(lax.axis_index("depth"), 2)
    out[0] = r2[1 - pd]
    out[1] = r1[1 - pd]


def outer_rows(far_row, near_row, r2, r1):
    vmem = pl.BlockSpec(memory_space=pltpu.VMEM)
    return pl.pallas_call(
        outer_kernel,
        out_shape=jax.ShapeDtypeStruct((2, 128, 128), BF16),
        in_specs=[pl.BlockSpec(memory_space=pl.ANY)] * 2 + [vmem] * 2,
        out_specs=vmem,
        compiler_params=pltpu.CompilerParams(vmem_limit_bytes=2 * 1024 * 1024),
    )(far_row, near_row, r2, r1)


def finish_kernel(ends, best, corner_w, c2, c1, e, other, out, peak):
    pr = lax.rem(lax.axis_index("rows"), 2)
    inner_d = inner("depth")
    inner_r = inner("rows")
    zero = jnp.zeros((128, 128), BF16)
    col = lax.broadcasted_iota(jnp.int32, (128, 128), 0)
    for q in range(2):
        value = best[q]
        for s in range(2):
            piece = e[q] if s == 1 else (c2, c1)[q][...]
            if q == 0:
                piece = jnp.where(inner_r, piece, zero)
            if s == 0:
                piece = jnp.where(inner_d, piece, zero)
            corner = jnp.dot(piece, corner_w[s, q], preferred_element_type=F32)
            value = jnp.maximum(value, ends[s, q] + spread(corner, col))
        peak[...] = value
        pooled = jnp.maximum(peak[pl.ds(0, 64, stride=2), :], peak[pl.ds(1, 64, stride=2), :])
        pooled = jnp.maximum(pooled, 0.0).astype(BF16)
        for k in range(8):
            out[k, q + pr * (1 - 2 * q)] = pooled


def finish(main, c2, c1, e, other):
    vmem = pl.BlockSpec(memory_space=pltpu.VMEM)
    return pl.pallas_call(
        finish_kernel,
        out_shape=jax.ShapeDtypeStruct((8, 2, 64, 128), BF16),
        in_specs=[vmem] * 6 + [pl.BlockSpec(memory_space=pl.ANY)],
        out_specs=vmem,
        scratch_shapes=[pltpu.VMEM((128, 128), F32)],
        compiler_params=pltpu.CompilerParams(vmem_limit_bytes=6 * 1024 * 1024),
    )(*main, c2, c1, e, other)


def coarse_sums(cells, taps, pair, other, add):
    lhs = jnp.concatenate(
        [
            jnp.concatenate([w[m, 9 * a + 3 * b + c] for a in taps for b in range(3)], axis=1)
            for c in range(3)
            for w, m in ((pair, 0), (other, 0), (other, 1), (pair, 1))
        ],
        axis=0,
    )
    count = len(taps)
    for start, size in ((0, 256), (256, 256), (512, 128)):
        if start < 512:
            first = start // 64 + 1
            blocks = [
                cells[i, first + b : first + b + 4].reshape(256, 128) for i in range(count) for b in range(3)
            ]
        else:
            blocks = [
                jnp.concatenate([cells[i, 9 + b], cells[i, b]], axis=0) for i in range(count) for b in range(3)
            ]
        rhs = jnp.concatenate(blocks, axis=1)
        term = lax.dot_general(lhs, rhs, (((1,), (1,)), ((), ())), preferred_element_type=F32)
        lane = lax.rem(lax.broadcasted_iota(jnp.int32, (64, size), 1), 64)
        left = jnp.where(lane == 0, 0.0, pltpu.roll(term[:64], 1, 1))
        right = jnp.where(lane == 63, 0.0, pltpu.roll(term[128:], size - 1, 1))
        add(start, size, term[64:128] + left + right)


def coarse_kernel(both, pair, other, out, cells):
    pd = lax.rem(lax.axis_index("depth"), 2)
    inner_d = inner("depth")
    for a in range(2):
        for i in (0, 1, 10, 11):
            cells[a, i] = jnp.zeros((64, 128), BF16)
    for k in range(4):
        far = both[pd, k]
        cells[0, 2 + 2 * k : 4 + 2 * k] = jnp.where(inner_d, far, jnp.zeros_like(far))
        cells[1, 2 + 2 * k : 4 + 2 * k] = both[1 - pd, k]

    def put(start, size, value):
        out[:, start : start + size] = value

    coarse_sums(cells, (2 * pd, 1), pair, other, put)


def coarse_level(both, pair, other):
    vmem = pl.BlockSpec(memory_space=pltpu.VMEM)
    return pl.pallas_call(
        coarse_kernel,
        out_shape=jax.ShapeDtypeStruct((64, 640), F32),
        in_specs=[vmem] * 3,
        out_specs=vmem,
        scratch_shapes=[pltpu.VMEM((2, 12, 64, 128), BF16)],
        compiler_params=pltpu.CompilerParams(vmem_limit_bytes=6 * 1024 * 1024),
        cost_estimate=pl.CostEstimate(flops=150_000_000, bytes_accessed=0, transcendentals=0),
    )(both, pair, other)


def near_kernel(near, sums, pair, other, o0, o1, o2, o3, cells):
    pd = lax.rem(lax.axis_index("depth"), 2)
    for i in (0, 1, 10, 11):
        cells[0, i] = jnp.zeros((64, 128), BF16)
    for k in range(4):
        cells[0, 2 + 2 * k : 4 + 2 * k] = near[k]

    def put(start, size, value):
        value = value + sums[:, start : start + size]
        for k, out in enumerate((o0, o1, o2, o3)):
            out[:, start : start + size] = value[16 * k : 16 * k + 16]

    coarse_sums(cells, (2 - 2 * pd,), pair, other, put)


def near_level(near, sums, pair, other):
    vmem = pl.BlockSpec(memory_space=pltpu.VMEM)
    return pl.pallas_call(
        near_kernel,
        out_shape=[jax.ShapeDtypeStruct((16, 640), F32)] * 4,
        in_specs=[vmem] * 4,
        out_specs=[vmem] * 4,
        scratch_shapes=[pltpu.VMEM((1, 12, 64, 128), BF16)],
        compiler_params=pltpu.CompilerParams(vmem_limit_bytes=6 * 1024 * 1024),
    )(near, sums, pair, other)


def join_kernel(s0, s2, s3, s1, bias, out, held):
    y = lax.div(lax.axis_index("rows"), 4)
    for k, part in enumerate((s0, s1, s2, s3)):
        held[y ^ k] = part[...]
    low = lax.broadcasted_iota(jnp.int32, (16, 128), 1) < 64
    for m in range(4):
        tiles = [held[m, :, 128 * i : 128 * i + 128] for i in range(4)]
        if m > 0:
            tiles[0] = tiles[0] + jnp.where(low, held[m - 1, :, 512:], 0.0)
        if m < 3:
            tiles[3] = tiles[3] + jnp.where(low, 0.0, held[m + 1, :, 512:])
        for i in range(4):
            value = jnp.maximum(tiles[i] + bias[...], 0.0).astype(BF16)
            out[:, 512 * m + 128 * i : 512 * m + 128 * i + 128] = value


def join(parts, bias):
    vmem = pl.BlockSpec(memory_space=pltpu.VMEM)
    return pl.pallas_call(
        join_kernel,
        out_shape=jax.ShapeDtypeStruct((16, 2048), BF16),
        in_specs=[vmem] * 5,
        out_specs=vmem,
        scratch_shapes=[pltpu.VMEM((4, 16, 640), F32)],
        compiler_params=pltpu.CompilerParams(vmem_limit_bytes=4 * 1024 * 1024),
    )(*parts, bias)


def body(volume, fine_filters, fine_bias, coarse_filters, coarse_bias):
    d = lax.axis_index("depth")
    r = lax.axis_index("rows")
    pd = lax.rem(d, 2)
    pr = lax.rem(r, 2)
    depth_near, depth_far = near_pairs(16), far_pairs(16)
    rows_near, rows_far = near_pairs(16), far_pairs(16)

    x2 = lax.ppermute(lax.dynamic_index_in_dim(volume, pd, 0, False), "depth", depth_far)
    x1 = lax.ppermute(lax.dynamic_index_in_dim(volume, 1 - pd, 0, False), "depth", depth_near)
    r2 = lax.ppermute(lax.dynamic_index_in_dim(volume, 3 * pr, 1, False), "rows", rows_far)
    r1 = lax.ppermute(lax.dynamic_index_in_dim(volume, 3 - 3 * pr, 1, False), "rows", rows_near)
    sides = jnp.stack([x2, x1])
    far_row = lax.dynamic_index_in_dim(sides, 3 * pr, 1, False)[0]
    near_row = lax.dynamic_index_in_dim(sides, 3 - 3 * pr, 1, False)[0]
    c2 = lax.ppermute(far_row, "rows", rows_far)
    c1 = lax.ppermute(near_row, "rows", rows_near)
    e = lax.ppermute(outer_rows(far_row, near_row, r2, r1), "depth", depth_near)

    def along_y(k):
        return [(i, i ^ (4 * k)) for i in range(16)]

    w = jnp.transpose(coarse_filters, (0, 1, 2, 4, 3)).reshape(27, 16, 128)
    pair = jnp.stack([w, lax.ppermute(w, "rows", along_y(3))])
    other = lax.ppermute(pair, "rows", along_y(1))
    main = fine_level(volume, x2, x1, r2, r1, fine_filters, jnp.broadcast_to(fine_bias, (8, 128)))
    pooled = finish(main, c2, c1, e, other)

    both = lax.all_to_all(
        pooled, ("depth", "rows"), 0, 0, axis_index_groups=far_and_z(), tiled=True
    ).reshape(2, 4, 2, 64, 128)
    near = lax.ppermute(lax.dynamic_index_in_dim(both, 1 - pd, 0, False), "depth", depth_near)
    sums = near_level(near, coarse_level(both, pair, other), pair, other)
    parts = [sums[0]] + [lax.ppermute(sums[k], "rows", along_y(k)) for k in (2, 3, 1)]
    result = join(parts, jnp.broadcast_to(coarse_bias[:, None], (16, 128)))
    return result.reshape(16, 1, 2048)


def solution(mesh):
    placed = (
        P("depth", "rows", None, None),
        P(),
        P(),
        P(None, None, None, None, "rows"),
        P("rows"),
    )
    return jax.shard_map(
        body, mesh=mesh, in_specs=placed, out_specs=P("rows", "depth", None), check_vma=False
    )
```

```python
import jax
import jax.numpy as jnp
from jax import lax
from jax.experimental import pallas as pl
from jax.experimental.pallas import tpu as pltpu
from jax.sharding import PartitionSpec as P

BF16 = jnp.bfloat16
F32 = jnp.float32


def near_pairs(count):
    return [(i, i ^ 1) for i in range(count)]


def far_pairs(count):
    return [(i, min(max(((i - 1) ^ 1) + 1, 0), count - 1)) for i in range(count)]


def far_and_z():
    pairs = [(d, d + 1) for d in range(1, 15, 2)] + [(15, 0)]
    return [[d * 16 + 4 * y + z for d in pair for z in range(4)] for pair in pairs for y in range(4)]


def inner(axis):
    i = lax.axis_index(axis)
    return (i > 0) & (i < 15)


def spread(line, col):
    left = jnp.where(col == 0, 0.0, pltpu.roll(line[:, :128], 1, 0))
    right = jnp.where(col == 127, 0.0, pltpu.roll(line[:, 256:], 127, 0))
    return line[:, 128:256] + left + right


def fine_kernel(vol, x2, x1, r2, r1, w, bias, ends, best, corner_w, cells):
    pd = lax.rem(lax.axis_index("depth"), 2)
    pr = lax.rem(lax.axis_index("rows"), 2)
    inner_d = inner("depth")
    inner_r = inner("rows")
    zero = jnp.zeros((128, 128), BF16)
    for j in range(4):
        for i in range(6):
            row = (i - 1) + pr * (5 - 2 * i)
            if j in (1, 2):
                plane = (j - 1) + pd * (3 - 2 * j)
                piece = r2[plane] if i == 0 else r1[plane] if i == 5 else vol[plane, row]
            elif i in (0, 5):
                piece = zero
            else:
                piece = (x2 if j == 0 else x1)[row]
            if i == 0:
                piece = jnp.where(inner_r, piece, zero)
            if j == 0:
                piece = jnp.where(inner_d, piece, zero)
            cells[j, i] = piece
    def tap(a, b):
        return [w[a + pd * (2 - 2 * a), b + pr * (2 - 2 * b), c] for c in range(3)]

    def line_sums(pieces, outs):
        total = None
        for i in range(0, len(pieces), 2):
            group = pieces[i : i + 2]
            lhs = jnp.concatenate([cells[j, b : b + 4].reshape(512, 128) for j, b in group], axis=1)
            rhs = jnp.concatenate(
                [jnp.concatenate(sum([tap(j - s, b) for s in outs], []), axis=1) for j, b in group], axis=0
            )
            term = jnp.dot(lhs, rhs, preferred_element_type=F32)
            total = term if total is None else total + term
        return total

    col = lax.broadcasted_iota(jnp.int32, (128, 128), 0)
    shared = line_sums([(j, b) for j in (1, 2) for b in range(3)], (0, 1))
    for s in range(2):
        total = shared[:, 384 * s : 384 * s + 384] + line_sums([(3 * s, b) for b in range(3)], (s,))
        for q in range(2):
            ends[s, q] = spread(total[3 * q * 128 : (3 * q + 1) * 128], col) + bias[:1]
            middle = spread(total[(q + 1) * 128 : (q + 2) * 128], col) + bias[:1]
            best[q] = middle if s == 0 else jnp.maximum(best[q], middle)
            a, b = 2 * s, 2 * q
            for c in range(3):
                corner_w[s, q, :, 128 * c : 128 * c + 128] = w[a + pd * (2 - 2 * a), b + pr * (2 - 2 * b), c]


def fine_level(vol, x2, x1, r2, r1, w, bias):
    vmem = pl.BlockSpec(memory_space=pltpu.VMEM)
    return pl.pallas_call(
        fine_kernel,
        out_shape=[
            jax.ShapeDtypeStruct((2, 2, 128, 128), F32),
            jax.ShapeDtypeStruct((2, 128, 128), F32),
            jax.ShapeDtypeStruct((2, 2, 128, 384), BF16),
        ],
        in_specs=[vmem] * 7,
        out_specs=[vmem] * 3,
        scratch_shapes=[pltpu.VMEM((4, 6, 128, 128), BF16)],
        compiler_params=pltpu.CompilerParams(vmem_limit_bytes=12 * 1024 * 1024),
        cost_estimate=pl.CostEstimate(flops=20_000_000_000, bytes_accessed=0, transcendentals=0),
    )(vol, x2, x1, r2, r1, w, bias)


def outer_kernel(far_row, near_row, r2, r1, out):
    pd = lax.rem(lax.axis_index("depth"), 2)
    out[0] = r2[1 - pd]
    out[1] = r1[1 - pd]


def outer_rows(far_row, near_row, r2, r1):
    vmem = pl.BlockSpec(memory_space=pltpu.VMEM)
    return pl.pallas_call(
        outer_kernel,
        out_shape=jax.ShapeDtypeStruct((2, 128, 128), BF16),
        in_specs=[pl.BlockSpec(memory_space=pl.ANY)] * 2 + [vmem] * 2,
        out_specs=vmem,
        compiler_params=pltpu.CompilerParams(vmem_limit_bytes=2 * 1024 * 1024),
    )(far_row, near_row, r2, r1)


def finish_kernel(ends, best, corner_w, c2, c1, e, other, out, peak):
    pr = lax.rem(lax.axis_index("rows"), 2)
    inner_d = inner("depth")
    inner_r = inner("rows")
    zero = jnp.zeros((128, 128), BF16)
    col = lax.broadcasted_iota(jnp.int32, (128, 128), 0)
    for q in range(2):
        value = best[q]
        for s in range(2):
            piece = e[q] if s == 1 else (c2, c1)[q][...]
            if q == 0:
                piece = jnp.where(inner_r, piece, zero)
            if s == 0:
                piece = jnp.where(inner_d, piece, zero)
            corner = jnp.dot(piece, corner_w[s, q], preferred_element_type=F32)
            value = jnp.maximum(value, ends[s, q] + spread(corner, col))
        peak[...] = value
        pooled = jnp.maximum(peak[pl.ds(0, 64, stride=2), :], peak[pl.ds(1, 64, stride=2), :])
        pooled = jnp.maximum(pooled, 0.0).astype(BF16)
        for k in range(8):
            out[k, q + pr * (1 - 2 * q)] = pooled


def finish(main, c2, c1, e, other):
    vmem = pl.BlockSpec(memory_space=pltpu.VMEM)
    return pl.pallas_call(
        finish_kernel,
        out_shape=jax.ShapeDtypeStruct((8, 2, 64, 128), BF16),
        in_specs=[vmem] * 6 + [pl.BlockSpec(memory_space=pl.ANY)],
        out_specs=vmem,
        scratch_shapes=[pltpu.VMEM((128, 128), F32)],
        compiler_params=pltpu.CompilerParams(vmem_limit_bytes=6 * 1024 * 1024),
    )(*main, c2, c1, e, other)


def coarse_sums(cells, taps, pair, other, add):
    lhs = jnp.concatenate(
        [
            jnp.concatenate([w[m, 9 * a + 3 * b + c] for a in taps for b in range(3)], axis=1)
            for c in range(3)
            for w, m in ((pair, 0), (other, 0), (other, 1), (pair, 1))
        ],
        axis=0,
    )
    count = len(taps)
    for start, size in ((0, 256), (256, 256), (512, 128)):
        if start < 512:
            first = start // 64 + 1
            blocks = [
                cells[i, first + b : first + b + 4].reshape(256, 128) for i in range(count) for b in range(3)
            ]
        else:
            blocks = [
                jnp.concatenate([cells[i, 9 + b], cells[i, b]], axis=0) for i in range(count) for b in range(3)
            ]
        rhs = jnp.concatenate(blocks, axis=1)
        term = lax.dot_general(lhs, rhs, (((1,), (1,)), ((), ())), preferred_element_type=F32)
        lane = lax.rem(lax.broadcasted_iota(jnp.int32, (64, size), 1), 64)
        left = jnp.where(lane == 0, 0.0, pltpu.roll(term[:64], 1, 1))
        right = jnp.where(lane == 63, 0.0, pltpu.roll(term[128:], size - 1, 1))
        add(start, size, term[64:128] + left + right)


def coarse_kernel(both, pair, other, bias, out, kept, cells):
    kept[...] = bias[...]
    pd = lax.rem(lax.axis_index("depth"), 2)
    inner_d = inner("depth")
    for a in range(2):
        for i in (0, 1, 10, 11):
            cells[a, i] = jnp.zeros((64, 128), BF16)
    for k in range(4):
        far = both[pd, k]
        cells[0, 2 + 2 * k : 4 + 2 * k] = jnp.where(inner_d, far, jnp.zeros_like(far))
        cells[1, 2 + 2 * k : 4 + 2 * k] = both[1 - pd, k]

    def put(start, size, value):
        out[:, start : start + size] = value

    coarse_sums(cells, (2 * pd, 1), pair, other, put)


def coarse_level(both, pair, other, bias):
    vmem = pl.BlockSpec(memory_space=pltpu.VMEM)
    return pl.pallas_call(
        coarse_kernel,
        out_shape=[jax.ShapeDtypeStruct((64, 640), F32), jax.ShapeDtypeStruct((16, 128), F32)],
        in_specs=[vmem] * 4,
        out_specs=[vmem] * 2,
        scratch_shapes=[pltpu.VMEM((2, 12, 64, 128), BF16)],
        compiler_params=pltpu.CompilerParams(vmem_limit_bytes=6 * 1024 * 1024),
        cost_estimate=pl.CostEstimate(flops=150_000_000, bytes_accessed=0, transcendentals=0),
    )(both, pair, other, bias)


def near_kernel(near, sums, pair, other, o0, o1, o2, o3, cells):
    pd = lax.rem(lax.axis_index("depth"), 2)
    for i in (0, 1, 10, 11):
        cells[0, i] = jnp.zeros((64, 128), BF16)
    for k in range(4):
        cells[0, 2 + 2 * k : 4 + 2 * k] = near[k]

    def put(start, size, value):
        value = value + sums[:, start : start + size]
        for k, out in enumerate((o0, o1, o2, o3)):
            out[:, start : start + size] = value[16 * k : 16 * k + 16]

    coarse_sums(cells, (2 - 2 * pd,), pair, other, put)


def near_level(near, sums, pair, other):
    vmem = pl.BlockSpec(memory_space=pltpu.VMEM)
    return pl.pallas_call(
        near_kernel,
        out_shape=[jax.ShapeDtypeStruct((16, 640), F32)] * 4,
        in_specs=[vmem] * 4,
        out_specs=[vmem] * 4,
        scratch_shapes=[pltpu.VMEM((1, 12, 64, 128), BF16)],
        compiler_params=pltpu.CompilerParams(vmem_limit_bytes=6 * 1024 * 1024),
    )(near, sums, pair, other)


def join_kernel(s0, s2, s3, s1, bias, out, held):
    y = lax.div(lax.axis_index("rows"), 4)
    for k, part in enumerate((s0, s1, s2, s3)):
        held[y ^ k] = part[...]
    low = lax.broadcasted_iota(jnp.int32, (16, 128), 1) < 64
    for m in range(4):
        tiles = [held[m, :, 128 * i : 128 * i + 128] for i in range(4)]
        if m > 0:
            tiles[0] = tiles[0] + jnp.where(low, held[m - 1, :, 512:], 0.0)
        if m < 3:
            tiles[3] = tiles[3] + jnp.where(low, 0.0, held[m + 1, :, 512:])
        for i in range(4):
            value = jnp.maximum(tiles[i] + bias[...], 0.0).astype(BF16)
            out[:, 512 * m + 128 * i : 512 * m + 128 * i + 128] = value


def join(parts, bias):
    vmem = pl.BlockSpec(memory_space=pltpu.VMEM)
    return pl.pallas_call(
        join_kernel,
        out_shape=jax.ShapeDtypeStruct((16, 2048), BF16),
        in_specs=[vmem] * 5,
        out_specs=vmem,
        scratch_shapes=[pltpu.VMEM((4, 16, 640), F32)],
        compiler_params=pltpu.CompilerParams(vmem_limit_bytes=4 * 1024 * 1024),
    )(*parts, bias)


def body(volume, fine_filters, fine_bias, coarse_filters, coarse_bias):
    d = lax.axis_index("depth")
    r = lax.axis_index("rows")
    pd = lax.rem(d, 2)
    pr = lax.rem(r, 2)
    depth_near, depth_far = near_pairs(16), far_pairs(16)
    rows_near, rows_far = near_pairs(16), far_pairs(16)

    x2 = lax.ppermute(lax.dynamic_index_in_dim(volume, pd, 0, False), "depth", depth_far)
    x1 = lax.ppermute(lax.dynamic_index_in_dim(volume, 1 - pd, 0, False), "depth", depth_near)
    r2 = lax.ppermute(lax.dynamic_index_in_dim(volume, 3 * pr, 1, False), "rows", rows_far)
    r1 = lax.ppermute(lax.dynamic_index_in_dim(volume, 3 - 3 * pr, 1, False), "rows", rows_near)
    sides = jnp.stack([x2, x1])
    far_row = lax.dynamic_index_in_dim(sides, 3 * pr, 1, False)[0]
    near_row = lax.dynamic_index_in_dim(sides, 3 - 3 * pr, 1, False)[0]
    c2 = lax.ppermute(far_row, "rows", rows_far)
    c1 = lax.ppermute(near_row, "rows", rows_near)
    e = lax.ppermute(outer_rows(far_row, near_row, r2, r1), "depth", depth_near)

    def along_y(k):
        return [(i, i ^ (4 * k)) for i in range(16)]

    w = jnp.transpose(coarse_filters, (0, 1, 2, 4, 3)).reshape(27, 16, 128)
    pair = jnp.stack([w, lax.ppermute(w, "rows", along_y(3))])
    other = lax.ppermute(pair, "rows", along_y(1))
    main = fine_level(volume, x2, x1, r2, r1, fine_filters, jnp.broadcast_to(fine_bias, (8, 128)))
    pooled = finish(main, c2, c1, e, other)

    both = lax.all_to_all(
        pooled, ("depth", "rows"), 0, 0, axis_index_groups=far_and_z(), tiled=True
    ).reshape(2, 4, 2, 64, 128)
    near = lax.ppermute(lax.dynamic_index_in_dim(both, 1 - pd, 0, False), "depth", depth_near)
    inner_sums, bias = coarse_level(
        both, pair, other, jnp.broadcast_to(coarse_bias[:, None], (16, 128))
    )
    sums = near_level(near, inner_sums, pair, other)
    parts = [sums[0]] + [lax.ppermute(sums[k], "rows", along_y(k)) for k in (2, 3, 1)]
    result = join(parts, bias)
    return result.reshape(16, 1, 2048)


def solution(mesh):
    placed = (
        P("depth", "rows", None, None),
        P(),
        P(),
        P(None, None, None, None, "rows"),
        P("rows"),
    )
    return jax.shard_map(
        body, mesh=mesh, in_specs=placed, out_specs=P("rows", "depth", None), check_vma=False
    )
```
